32 devices in a mesh: tile: 16 (over z, y, core), sub: 2 (over x).
Axes of the slice: x: 2, y: 2, z: 4, core: 2. Of those that a mesh axis runs over, the one named last changes fastest.
Arguments:
- up_check: bfloat16 [888, 2048], P('sub', 'tile'), may hold values from -6 to 6
- up_inverse: bfloat16 [888, 888], P('sub'), may hold values from -0.1875 to 0.1875
- translate: bfloat16 [8, 888, 888], P(None, 'sub'), may hold values from -0.1875 to 0.1875
- down_inverse: bfloat16 [888, 888], P('sub'), may hold values from -0.09375 to 0.09375
- list_slot: int32 [2048, 8], P('tile'), may hold values from 0 to 639
- list_class: int32 [2048, 8], P('tile'), may hold values from 0 to 7
- list_count: int32 [2048], P('tile'), may hold values from 2 to 8, as said below
Outputs:
- local_density: bfloat16 [888, 2048], P('sub', 'tile')
The draws below stay inside these ranges and needn't reach their ends.
Inputs may be any that keep to these rules, and one draw needn't show every extreme that they name: Entries at and after list_count of a cell are padding and are not used.
All inputs are finite; a program needn't handle non-finite values.
Results may differ from the reference program's by a relative error of at most 0.0061.
Values may be sent and summed in bfloat16 or wider, within the bound.
No kernel may reach another device: no remote copies, remote signals or barrier semaphores. Data moves between devices by JAX's collectives and lax.ppermute only.
A program may use at most 64 MiB of HBM per device.

```python
import jax
import jax.numpy as jnp
from jax import lax

EQ = 888
KCLS = 8
NV = 8
REACH = 2
TC = 128
CELLS = 2048
WIN = 640
N_TILE = 16


def draw_list_count(key, part):
    key = jax.random.fold_in(key, 11)
    counts = jax.random.randint(key, (CELLS,), NV // 4, NV + 1)
    counts = counts.at[0].set(NV).at[1].set(NV // 4)
    return counts.astype(jnp.int32)


def touch_ends(entries, key, least, top_value):
    longest = entries.shape.index(max(entries.shape))
    spots = []
    for shift in (0, 1):
        where = [jax.random.randint(jax.random.fold_in(key, axis), (), 0, length) for axis, length in enumerate(entries.shape)]
        where[longest] = (where[longest] + shift) % entries.shape[longest]
        spots.append(tuple(where))
    return entries.at[spots[0]].set(least).at[spots[1]].set(top_value)


def levels(stream_key, shape, shards, smallest, largest):
    loudness, own = 1.0, jax.random.fold_in(stream_key, 6)
    for position, parts in shards:
        steps = jnp.exp(jax.random.uniform(jax.random.fold_in(own, position), (parts,), jnp.float32, smallest / len(shards), largest / len(shards)))
        loudness = loudness * jnp.repeat(steps, shape[position] // parts).reshape([-1 if axis == position else 1 for axis in range(len(shape))])
    return loudness


def centred(rng, extent, spread, limit, pieces=(), dtype=jnp.bfloat16):
    values = jax.random.normal(rng, extent, jnp.float32) * spread
    if len(pieces) > 0:
        values = levels(rng, extent, pieces, -0.22, 0.18) * values
    return jnp.clip(values, min=-limit, max=limit).astype(dtype)


def setup_inputs(seed: int = 0) -> dict:
    splits = jax.random.split(jax.random.key(seed), 8)
    return {
        "up_check": centred(splits[0], (EQ, CELLS), 1.0, 6.0, ((0, 2), (1, 16))),
        "up_inverse": centred(splits[1], (EQ, EQ), EQ ** -0.5, 0.1875, ((0, 2),)),
        "translate": centred(splits[2], (KCLS, EQ, EQ), EQ ** -0.5, 0.1875, ((1, 2),)),
        "down_inverse": centred(splits[3], (EQ, EQ), (EQ * NV // 2) ** -0.5, 0.09375, ((0, 2),)),
        "list_slot": touch_ends(jax.random.randint(splits[4], (CELLS, NV), 0, WIN), jax.random.fold_in(splits[4], 1), 0, WIN - 1).astype(jnp.int32),
        "list_class": touch_ends(jax.random.randint(splits[5], (CELLS, NV), 0, KCLS), jax.random.fold_in(splits[5], 1), 0, KCLS - 1).astype(jnp.int32),
        "list_count": draw_list_count(jax.random.fold_in(splits[7], 71), 0),
    }


def reference(up_check, up_inverse, translate, down_inverse, list_slot, list_class, list_count):
    equivalent = jnp.dot(up_inverse, up_check, preferred_element_type=jnp.float32).astype(jnp.bfloat16)
    padded = jnp.pad(equivalent, ((0, 0), (REACH * TC, REACH * TC))).astype(jnp.float32)
    operators = translate.astype(jnp.float32)
    classes_all = jnp.arange(KCLS).astype(jnp.int32)
    active = jnp.arange(NV).astype(jnp.int32)[None, :] < list_count[:, None]
    slot_tiles = list_slot.reshape(N_TILE, TC, NV)
    class_tiles = list_class.reshape(N_TILE, TC, NV)
    active_tiles = active.reshape(N_TILE, TC, NV)
    tile_ids = jnp.arange(N_TILE).astype(jnp.int32)

    def tile_sum(operands):
        tile_id, slots, classes, usable = operands
        window = lax.dynamic_slice_in_dim(padded, (tile_id * TC).astype(jnp.int32), WIN, 1)
        picked = jnp.take(window, slots, axis=1)
        weights = jnp.where((classes[:, :, None] == classes_all[None, None, :]) & usable[:, :, None], 1.0, 0.0).astype(jnp.float32)
        grouped = jnp.einsum("ecj,cjk->kec", picked, weights, precision=lax.Precision.HIGHEST)
        grouped_half = lax.optimization_barrier(grouped.astype(jnp.bfloat16)).astype(jnp.float32)
        return jnp.einsum("kre,kec->rc", operators, grouped_half, precision=lax.Precision.HIGHEST)

    sums = lax.map(tile_sum, (tile_ids, slot_tiles, class_tiles, active_tiles))
    down_check = jnp.transpose(sums, (1, 0, 2)).reshape(EQ, CELLS).astype(jnp.bfloat16)
    return jnp.dot(down_inverse, down_check, preferred_element_type=jnp.float32).astype(jnp.bfloat16)
```

```python
import functools

import jax
import jax.numpy as jnp
from jax import lax
from jax.experimental import pallas as pl
from jax.experimental.pallas import tpu as pltpu
from jax.sharding import PartitionSpec as P

REACH = 2
CLASS_STRIDE = 1024
CHUNK = 112


def gathered_rows(shard):
    if lax.axis_size("sub") != 2:
        return lax.all_gather(shard, "sub", axis=0, tiled=True)
    other = lax.ppermute(shard, "sub", [(0, 1), (1, 0)])
    first = lax.axis_index("sub") == 0
    return jnp.where(
        first, jnp.concatenate([shard, other], 0), jnp.concatenate([other, shard], 0)
    )


def moved(value, step):
    count = lax.axis_size("tile")
    pairs = []
    for tile in range(count):
        target = tile + (step if tile % 2 else -step)
        if 0 <= target < count:
            pairs.append((tile, target))
    return lax.ppermute(value, "tile", pairs)


def select_kernel(codes_ref, base_ref, out_ref):
    blocks, entries, cells = codes_ref.shape
    classes = out_ref.shape[1] // cells
    for block in range(blocks):
        codes = codes_ref[block] - base_ref[block]
        source = lax.broadcasted_iota(jnp.int32, (cells, cells), 0)
        for k in range(classes):
            row = source + k * CLASS_STRIDE
            total = jnp.zeros((cells, cells), jnp.float32)
            for entry in range(entries):
                total += jnp.where(codes[entry : entry + 1, :] == row, 1.0, 0.0)
            out_ref[block, k * cells : (k + 1) * cells, :] = total.astype(jnp.bfloat16)


def push_kernel(
    translate_ref, equivalent_ref, select_ref, own_ref, near_ref, far_ref, mate_ref,
    held, product, sems,
):
    rows, classes, _ = translate_ref.shape
    cells = equivalent_ref.shape[1]
    starts = list(range(0, rows, CHUNK))
    copies = []
    for i, start in enumerate(starts):
        part = pl.ds(start, min(CHUNK, rows - start))
        copy = pltpu.make_async_copy(translate_ref.at[part], held.at[part], sems.at[i])
        copy.start()
        copies.append(copy)
    equivalent = equivalent_ref[...]
    for copy, start in zip(copies, starts):
        size = min(CHUNK, rows - start)
        copy.wait()
        left = held[start : start + size].reshape(size * classes, held.shape[2])
        product[: size * classes, :] = jnp.dot(
            left, equivalent, preferred_element_type=jnp.float32
        )
        terms = [
            product[pl.ds(k, size, stride=classes), :].astype(jnp.bfloat16)
            for k in range(classes)
        ]
        terms = jnp.concatenate(terms, axis=1)
        part = pl.ds(start, size)
        for block, ref in enumerate((own_ref, near_ref, far_ref, mate_ref, mate_ref)):
            value = jnp.dot(terms, select_ref[block], preferred_element_type=jnp.float32)
            if block < 3:
                ref[part, :] = value.astype(ref.dtype)
            else:
                column = (block - 3) * cells
                ref[part, column : column + cells] = value.astype(ref.dtype)


def shards(up_check, up_inverse, translate, down_inverse, list_slot, list_class, list_count):
    classes, rows, depth = translate.shape
    cells, entries = list_slot.shape

    slots = list_slot.T
    active = lax.broadcasted_iota(jnp.int32, slots.shape, 0) < list_count[None, :]
    code = jnp.where(active, list_class.T * CLASS_STRIDE + slots, -CLASS_STRIDE)
    codes = jnp.stack([code, moved(code, 1), moved(code, -2), moved(code, -1), moved(code, 2)])
    away = 2 * (lax.axis_index("tile") % 2) - 1
    offsets = jnp.array([0, 1, 2, -1, -2], jnp.int32) * away
    base = (REACH - offsets) * cells

    select = pl.pallas_call(
        select_kernel,
        out_shape=jax.ShapeDtypeStruct((5, classes * cells, cells), jnp.bfloat16),
        in_specs=[
            pl.BlockSpec(memory_space=pltpu.VMEM),
            pl.BlockSpec(memory_space=pltpu.SMEM),
        ],
        out_specs=pl.BlockSpec(memory_space=pltpu.VMEM),
        cost_estimate=pl.CostEstimate(
            flops=5 * 2 * entries * classes * cells * cells, bytes_accessed=2 << 20,
            transcendentals=0,
        ),
        compiler_params=pltpu.CompilerParams(vmem_limit_bytes=8 << 20),
        name="select",
    )(codes, base)

    whole_check = gathered_rows(up_check)
    equivalent = jnp.dot(up_inverse, whole_check, preferred_element_type=jnp.float32)
    whole = gathered_rows(equivalent.astype(jnp.bfloat16))

    operators = jnp.transpose(translate, (1, 0, 2))
    own, near, far, mate = pl.pallas_call(
        push_kernel,
        out_shape=[
            jax.ShapeDtypeStruct((rows, cells), jnp.float32),
            jax.ShapeDtypeStruct((rows, cells), jnp.float32),
            jax.ShapeDtypeStruct((rows, cells), jnp.bfloat16),
            jax.ShapeDtypeStruct((rows, 2 * cells), jnp.bfloat16),
        ],
        in_specs=[
            pl.BlockSpec(memory_space=pl.ANY),
            pl.BlockSpec(memory_space=pltpu.VMEM),
            pl.BlockSpec(memory_space=pltpu.VMEM),
        ],
        out_specs=[pl.BlockSpec(memory_space=pltpu.VMEM)] * 4,
        scratch_shapes=[
            pltpu.VMEM((rows, classes, depth), jnp.bfloat16),
            pltpu.VMEM((CHUNK * classes, cells), jnp.float32),
            pltpu.SemaphoreType.DMA((pl.cdiv(rows, CHUNK),)),
        ],
        cost_estimate=pl.CostEstimate(
            flops=2 * rows * classes * cells * (depth + 5 * cells),
            bytes_accessed=2 * rows * classes * depth,
            transcendentals=0,
        ),
        compiler_params=pltpu.CompilerParams(vmem_limit_bytes=24 << 20),
        name="push",
    )(operators, whole, select)

    from_far = moved(far, 2)
    from_mate = moved(mate, -1).astype(jnp.float32)
    from_near = moved((near + from_mate[:, cells:]).astype(jnp.bfloat16), 1)
    down_check = (
        (own + from_mate[:, :cells])
        + (from_far.astype(jnp.float32) + from_near.astype(jnp.float32))
    ).astype(jnp.bfloat16)
    local = jnp.dot(
        down_inverse, gathered_rows(down_check), preferred_element_type=jnp.float32
    )
    return local.astype(jnp.bfloat16)


def solution(mesh):
    in_specs = (
        P("sub", "tile"),
        P("sub", None),
        P(None, "sub", None),
        P("sub", None),
        P("tile", None),
        P("tile", None),
        P("tile"),
    )
    out_specs = P("sub", "tile")
    return jax.shard_map(shards, mesh=mesh, in_specs=in_specs, out_specs=out_specs, check_vma=False)
```

```python
import functools

import jax
import jax.numpy as jnp
from jax import lax
from jax.experimental import pallas as pl
from jax.experimental.pallas import tpu as pltpu
from jax.sharding import PartitionSpec as P

REACH = 2
CLASS_SHIFT = 10
CHUNK = 112
LANES = 128
WHOLE = pl.BlockSpec(memory_space=pltpu.VMEM)


def across_sub(shard):
    return lax.ppermute(shard, "sub", [(0, 1), (1, 0)])


def to_mate(value):
    count = lax.axis_size("tile")
    pairs = [(t, t ^ 1) for t in range(count) if t ^ 1 < count]
    return lax.ppermute(value, "tile", pairs)


def to_near(value):
    count = lax.axis_size("tile")
    pairs = [(t, t + 2 * (t % 2) - 1) for t in range(count)]
    return lax.ppermute(value, "tile", [(a, b) for a, b in pairs if 0 <= b < count])


def away():
    return 2 * lax.rem(lax.axis_index("tile"), 2) - 1


def half_windows(shard_rows, depth, count):
    windows = []
    for index in range(count):
        low, high = index * shard_rows, (index + 1) * shard_rows
        start = low // LANES * LANES
        stop = min(pl.cdiv(high, LANES) * LANES, depth)
        windows.append((start, stop, low - start))
    return windows


def chunks(rows):
    return [(start, min(CHUNK, rows - start)) for start in range(0, rows, CHUNK)]


def pad_into(padded, offset, *refs):
    padded[...] = jnp.zeros(padded.shape, padded.dtype)
    for i, ref in enumerate(refs):
        rows, cells = ref.shape
        padded[offset : offset + rows, i * cells : (i + 1) * cells] = ref[...].astype(padded.dtype)


def first_kernel(windows, matrix_ref, own_ref, out_ref, padded):
    for index, (low, high, offset) in enumerate(windows):
        def run(low=low, high=high, offset=offset):
            pad_into(padded, offset, own_ref)
            out_ref[...] = jnp.dot(
                matrix_ref[:, low:high], padded[: high - low, :].astype(jnp.bfloat16),
                preferred_element_type=jnp.float32,
            )
        pl.when(lax.axis_index("sub") == index)(run)


def first(matrix, own, windows):
    rows, depth = matrix.shape
    cells = own.shape[1]
    span = max(high - low for low, high, _ in windows)
    return pl.pallas_call(
        functools.partial(first_kernel, windows),
        out_shape=jax.ShapeDtypeStruct((rows, cells), jnp.float32),
        in_specs=[WHOLE] * 2,
        out_specs=WHOLE,
        scratch_shapes=[pltpu.VMEM((span, cells), jnp.float32)],
        cost_estimate=pl.CostEstimate(
            flops=2 * rows * depth * cells, bytes_accessed=4 * rows * depth, transcendentals=0
        ),
        compiler_params=pltpu.CompilerParams(vmem_limit_bytes=16 << 20),
        name="first",
    )(matrix, own)


def rest_kernel(windows, matrix_ref, part_ref, other_ref, out_ref, padded):
    for index, (low, high, offset) in enumerate(windows):
        def run(low=low, high=high, offset=offset):
            pad_into(padded, offset, other_ref)
            out_ref[...] = (
                part_ref[...]
                + jnp.dot(
                    matrix_ref[:, low:high], padded[: high - low, :].astype(jnp.bfloat16),
                    preferred_element_type=jnp.float32,
                )
            ).astype(jnp.bfloat16)
        pl.when(lax.axis_index("sub") != index)(run)


def rest(matrix, part, other, windows):
    rows, depth = matrix.shape
    cells = other.shape[1]
    span = max(high - low for low, high, _ in windows)
    return pl.pallas_call(
        functools.partial(rest_kernel, windows),
        out_shape=jax.ShapeDtypeStruct((rows, cells), jnp.bfloat16),
        in_specs=[WHOLE] * 3,
        out_specs=WHOLE,
        scratch_shapes=[pltpu.VMEM((span, cells), jnp.float32)],
        cost_estimate=pl.CostEstimate(
            flops=2 * rows * span * cells, bytes_accessed=2 * rows * span, transcendentals=0
        ),
        compiler_params=pltpu.CompilerParams(vmem_limit_bytes=16 << 20),
        name="rest",
    )(matrix, part, other)


def build_select(code, base, out_ref, column, classes):
    entries, cells = code.shape
    slots = (code & ((1 << CLASS_SHIFT) - 1)) - base
    kinds = code >> CLASS_SHIFT
    band = 32
    for low in range(0, cells, band):
        source = lax.broadcasted_iota(jnp.int32, (band, cells), 0) + low
        totals = [jnp.zeros((band, cells), jnp.bfloat16)] * classes
        for entry in range(entries):
            hit = jnp.where(slots[entry : entry + 1, :] == source, 1.0, 0.0).astype(jnp.bfloat16)
            for k in range(classes):
                used = jnp.where(kinds[entry : entry + 1, :] == k, 1.0, 0.0).astype(jnp.bfloat16)
                totals[k] = totals[k] + hit * used
        for k in range(classes):
            out_ref[k * cells + low : k * cells + low + band, column : column + cells] = totals[k]


def prepare_kernel(
    windows, translate_ref, own_ref, mate_ref, code_ref, near_ref,
    held_ref, product_ref, select_own_ref, select_mate_ref, padded, sems,
):
    rows, classes, _ = translate_ref.shape
    entries, cells = code_ref.shape
    copies = []
    for i, (start, size) in enumerate(chunks(rows)):
        part = pl.ds(start, size)
        copy = pltpu.make_async_copy(translate_ref.at[part], held_ref.at[part], sems.at[i])
        copy.start()
        copies.append(copy)

    step = away()
    codes = [code_ref[...], near_ref[:entries, :], near_ref[entries:, :]]
    for block, code in enumerate(codes):
        base = (REACH - block * step) * cells
        build_select(code, base, select_own_ref, block * cells, classes)
        if block < 2:
            base = (REACH - (1 + block) * step) * cells
            build_select(code, base, select_mate_ref, block * cells, classes)

    for copy in copies:
        copy.wait()

    for index, (low, high, offset) in enumerate(windows):
        def run(low=low, high=high, offset=offset):
            pad_into(padded, offset, own_ref, mate_ref)
            right = padded[: high - low, :].astype(jnp.bfloat16)
            for start, size in chunks(rows):
                left = held_ref[start : start + size, :, low:high]
                product_ref[start * classes : (start + size) * classes, :] = jnp.dot(
                    left.reshape(size * classes, high - low), right,
                    preferred_element_type=jnp.float32,
                )
        if len(windows) == 1:
            run()
        else:
            pl.when(lax.axis_index("sub") == index)(run)


def push_kernel(
    windows, held_ref, product_ref, own_ref, mate_ref, select_own_ref, select_mate_ref,
    out_ref, sent_ref, padded, own_terms_ref, mate_terms_ref,
):
    rows, classes, _ = held_ref.shape
    cells = own_ref.shape[1]

    def keep(size, value):
        own_terms_ref[: size * classes, :] = value[:, :cells]
        mate_terms_ref[: size * classes, :] = value[:, cells:]

    def finish(start, size):
        def by_class(ref):
            parts = [ref[pl.ds(k, size, stride=classes), :] for k in range(classes)]
            return jnp.concatenate([part.astype(jnp.bfloat16) for part in parts], axis=1)

        total = jnp.dot(
            by_class(own_terms_ref), select_own_ref[...], preferred_element_type=jnp.float32
        )
        extra = jnp.dot(
            by_class(mate_terms_ref), select_mate_ref[...], preferred_element_type=jnp.float32
        )
        part = slice(start, start + size)
        out_ref[part, :] = total[:, :cells] + extra[:, :cells]
        sent_ref[part, :cells] = (total[:, cells : 2 * cells] + extra[:, cells:]).astype(
            jnp.bfloat16
        )
        sent_ref[part, cells:] = total[:, 2 * cells :].astype(jnp.bfloat16)

    for index, (low, high, offset) in enumerate(windows):
        def run(low=low, high=high, offset=offset):
            pad_into(padded, offset, own_ref, mate_ref)
            right = padded[: high - low, :].astype(jnp.bfloat16)
            for start, size in chunks(rows):
                left = held_ref[start : start + size, :, low:high]
                part = pl.ds(start * classes, size * classes)
                keep(size, product_ref[part, :] + jnp.dot(
                    left.reshape(size * classes, high - low), right,
                    preferred_element_type=jnp.float32,
                ))
                finish(start, size)
        pl.when(lax.axis_index("sub") != index)(run)

    if not windows:
        for start, size in chunks(rows):
            keep(size, product_ref[pl.ds(start * classes, size * classes), :])
            finish(start, size)


def prepare(operators, own, mate, code, near_codes, windows):
    rows, classes, depth = operators.shape
    cells = code.shape[1]
    span = max(high - low for low, high, _ in windows)
    return pl.pallas_call(
        functools.partial(prepare_kernel, windows),
        out_shape=[
            jax.ShapeDtypeStruct((rows, classes, depth), jnp.bfloat16),
            jax.ShapeDtypeStruct((rows * classes, 2 * cells), jnp.float32),
            jax.ShapeDtypeStruct((classes * cells, 3 * cells), jnp.bfloat16),
            jax.ShapeDtypeStruct((classes * cells, 2 * cells), jnp.bfloat16),
        ],
        in_specs=[pl.BlockSpec(memory_space=pl.ANY)] + [WHOLE] * 4,
        out_specs=[WHOLE] * 4,
        scratch_shapes=[
            pltpu.VMEM((span, 2 * cells), jnp.float32),
            pltpu.SemaphoreType.DMA((len(chunks(rows)),)),
        ],
        cost_estimate=pl.CostEstimate(
            flops=4 * rows * classes * cells * span,
            bytes_accessed=2 * rows * classes * depth,
            transcendentals=0,
        ),
        compiler_params=pltpu.CompilerParams(vmem_limit_bytes=40 << 20),
        name="prepare",
    )(operators, own, mate, code, near_codes)


def push(held, product, own, mate, select_own, select_mate, windows):
    rows, classes, depth = held.shape
    cells = own.shape[1]
    span = max([high - low for low, high, _ in windows], default=LANES)
    return pl.pallas_call(
        functools.partial(push_kernel, windows),
        out_shape=[
            jax.ShapeDtypeStruct((rows, cells), jnp.float32),
            jax.ShapeDtypeStruct((rows, 2 * cells), jnp.bfloat16),
        ],
        in_specs=[WHOLE] * 6,
        out_specs=[WHOLE] * 2,
        scratch_shapes=[
            pltpu.VMEM((span, 2 * cells), jnp.float32),
            pltpu.VMEM((CHUNK * classes, cells), jnp.float32),
            pltpu.VMEM((CHUNK * classes, cells), jnp.float32),
        ],
        cost_estimate=pl.CostEstimate(
            flops=2 * rows * classes * cells * (2 * span + 5 * cells),
            bytes_accessed=2 * rows * classes * depth,
            transcendentals=0,
        ),
        compiler_params=pltpu.CompilerParams(vmem_limit_bytes=40 << 20),
        name="push",
    )(held, product, own, mate, select_own, select_mate)


def shards(up_check, up_inverse, translate, down_inverse, list_slot, list_class, list_count):
    classes, rows, depth = translate.shape
    cells, entries = list_slot.shape
    halves = lax.axis_size("sub") == 2

    active = lax.broadcasted_iota(jnp.int32, (entries, cells), 0) < list_count[None, :]
    code = jnp.where(active, (list_class.T << CLASS_SHIFT) + list_slot.T, -1)
    chip_codes = jnp.concatenate([code, to_mate(code)], axis=0)
    near_codes = to_near(chip_codes)

    operators = jnp.transpose(translate, (1, 0, 2))
    if halves:
        windows = half_windows(rows, depth, 2)
        other_check = across_sub(up_check)
        part = first(up_inverse, up_check, windows)
        part, near_codes = lax.optimization_barrier((part, near_codes))
        equivalent = rest(up_inverse, part, other_check, windows)
        other = across_sub(equivalent)
    else:
        equivalent = lax.all_gather(
            jnp.dot(
                up_inverse, lax.all_gather(up_check, "sub", axis=0, tiled=True),
                preferred_element_type=jnp.float32,
            ).astype(jnp.bfloat16),
            "sub", axis=0, tiled=True,
        )
        windows = [(0, depth, 0)]
        other = equivalent
    held, product, select_own, select_mate = prepare(
        operators, equivalent, to_mate(equivalent), code, near_codes, windows
    )
    if halves:
        other, product = lax.optimization_barrier((other, product))
    other_mate = to_mate(other) if halves else other
    own_sum, sent = push(
        held, product, other, other_mate, select_own, select_mate, windows if halves else []
    )

    came = to_near(sent)
    came_far = to_mate(came[:, cells:])
    down_check = (
        own_sum + (came[:, :cells].astype(jnp.float32) + came_far.astype(jnp.float32))
    ).astype(jnp.bfloat16)
    if halves:
        other_down = across_sub(down_check)
        return rest(down_inverse, first(down_inverse, down_check, windows), other_down, windows)
    return jnp.dot(
        down_inverse, lax.all_gather(down_check, "sub", axis=0, tiled=True),
        preferred_element_type=jnp.float32,
    ).astype(jnp.bfloat16)


def solution(mesh):
    in_specs = (
        P("sub", "tile"),
        P("sub", None),
        P(None, "sub", None),
        P("sub", None),
        P("tile", None),
        P("tile", None),
        P("tile"),
    )
    out_specs = P("sub", "tile")
    return jax.shard_map(shards, mesh=mesh, in_specs=in_specs, out_specs=out_specs, check_vma=False)
```

```python
import functools

import jax
import jax.numpy as jnp
from jax import lax
from jax.experimental import pallas as pl
from jax.experimental.pallas import tpu as pltpu
from jax.sharding import PartitionSpec as P

REACH = 2
CLASS_SHIFT = 10
CHUNK = 112
LANES = 128
WHOLE = pl.BlockSpec(memory_space=pltpu.VMEM)


def across_sub(shard):
    return lax.ppermute(shard, "sub", [(0, 1), (1, 0)])


def to_mate(value):
    count = lax.axis_size("tile")
    pairs = [(t, t ^ 1) for t in range(count) if t ^ 1 < count]
    return lax.ppermute(value, "tile", pairs)


def to_near(value):
    count = lax.axis_size("tile")
    pairs = [(t, t + 2 * (t % 2) - 1) for t in range(count)]
    return lax.ppermute(value, "tile", [(a, b) for a, b in pairs if 0 <= b < count])


def away():
    return 2 * lax.rem(lax.axis_index("tile"), 2) - 1


def half_windows(shard_rows, depth, count):
    windows = []
    for index in range(count):
        low, high = index * shard_rows, (index + 1) * shard_rows
        start = low // LANES * LANES
        stop = min(pl.cdiv(high, LANES) * LANES, depth)
        windows.append((start, stop, low - start))
    return windows


def chunks(rows):
    return [(start, min(CHUNK, rows - start)) for start in range(0, rows, CHUNK)]


def pad_into(padded, offset, *refs):
    padded[...] = jnp.zeros(padded.shape, padded.dtype)
    for i, ref in enumerate(refs):
        rows, cells = ref.shape
        padded[offset : offset + rows, i * cells : (i + 1) * cells] = ref[...].astype(padded.dtype)


def stage_kernel(
    windows, matrix_ref, own_ref, translate_ref, matrix_held, translate_held, part_ref,
    own_held, padded, sems,
):
    copies = [
        pltpu.make_async_copy(own_ref, own_held, sems.at[0]),
        pltpu.make_async_copy(matrix_ref, matrix_held, sems.at[1]),
        pltpu.make_async_copy(translate_ref, translate_held, sems.at[2]),
    ]
    for copy in copies:
        copy.start()
    copies[0].wait()
    copies[1].wait()
    first_kernel(windows, matrix_held, own_held, part_ref, padded)
    copies[2].wait()


def stage(matrix, own, operators, windows):
    rows, depth = matrix.shape
    cells = own.shape[1]
    span = max(high - low for low, high, _ in windows)
    return pl.pallas_call(
        functools.partial(stage_kernel, windows),
        out_shape=[
            jax.ShapeDtypeStruct(matrix.shape, matrix.dtype),
            jax.ShapeDtypeStruct(operators.shape, operators.dtype),
            jax.ShapeDtypeStruct((rows, cells), jnp.float32),
        ],
        in_specs=[pl.BlockSpec(memory_space=pltpu.HBM)] * 3,
        out_specs=[WHOLE] * 3,
        scratch_shapes=[
            pltpu.VMEM(own.shape, own.dtype),
            pltpu.VMEM((span, cells), jnp.float32),
            pltpu.SemaphoreType.DMA((3,)),
        ],
        cost_estimate=pl.CostEstimate(
            flops=2 * rows * depth * cells, bytes_accessed=2 * operators.size,
            transcendentals=0,
        ),
        compiler_params=pltpu.CompilerParams(vmem_limit_bytes=24 << 20),
        name="stage",
    )(*[pltpu.with_memory_space_constraint(x, pltpu.HBM) for x in (matrix, own, operators)])


def first_kernel(windows, matrix_ref, own_ref, out_ref, padded):
    for index, (low, high, offset) in enumerate(windows):
        def run(low=low, high=high, offset=offset):
            pad_into(padded, offset, own_ref)
            out_ref[...] = jnp.dot(
                matrix_ref[:, low:high], padded[: high - low, :].astype(jnp.bfloat16),
                preferred_element_type=jnp.float32,
            )
        pl.when(lax.axis_index("sub") == index)(run)


def first(matrix, own, windows):
    rows, depth = matrix.shape
    cells = own.shape[1]
    span = max(high - low for low, high, _ in windows)
    return pl.pallas_call(
        functools.partial(first_kernel, windows),
        out_shape=jax.ShapeDtypeStruct((rows, cells), jnp.float32),
        in_specs=[WHOLE] * 2,
        out_specs=WHOLE,
        scratch_shapes=[pltpu.VMEM((span, cells), jnp.float32)],
        cost_estimate=pl.CostEstimate(
            flops=2 * rows * depth * cells, bytes_accessed=4 * rows * depth, transcendentals=0
        ),
        compiler_params=pltpu.CompilerParams(vmem_limit_bytes=16 << 20),
        name="first",
    )(matrix, own)


def rest_kernel(windows, matrix_ref, part_ref, other_ref, out_ref, padded):
    for index, (low, high, offset) in enumerate(windows):
        def run(low=low, high=high, offset=offset):
            pad_into(padded, offset, other_ref)
            out_ref[...] = (
                part_ref[...]
                + jnp.dot(
                    matrix_ref[:, low:high], padded[: high - low, :].astype(jnp.bfloat16),
                    preferred_element_type=jnp.float32,
                )
            ).astype(jnp.bfloat16)
        pl.when(lax.axis_index("sub") != index)(run)


def rest(matrix, part, other, windows):
    rows, depth = matrix.shape
    cells = other.shape[1]
    span = max(high - low for low, high, _ in windows)
    return pl.pallas_call(
        functools.partial(rest_kernel, windows),
        out_shape=jax.ShapeDtypeStruct((rows, cells), jnp.bfloat16),
        in_specs=[WHOLE] * 3,
        out_specs=WHOLE,
        scratch_shapes=[pltpu.VMEM((span, cells), jnp.float32)],
        cost_estimate=pl.CostEstimate(
            flops=2 * rows * span * cells, bytes_accessed=2 * rows * span, transcendentals=0
        ),
        compiler_params=pltpu.CompilerParams(vmem_limit_bytes=16 << 20),
        name="rest",
    )(matrix, part, other)


def build_select(code, base, out_ref, column, classes):
    entries, cells = code.shape
    slots = (code & ((1 << CLASS_SHIFT) - 1)) - base
    kinds = code >> CLASS_SHIFT
    band = 32
    for low in range(0, cells, band):
        source = lax.broadcasted_iota(jnp.int32, (band, cells), 0) + low
        totals = [jnp.zeros((band, cells), jnp.bfloat16)] * classes
        for entry in range(entries):
            hit = jnp.where(slots[entry : entry + 1, :] == source, 1.0, 0.0).astype(jnp.bfloat16)
            for k in range(classes):
                used = jnp.where(kinds[entry : entry + 1, :] == k, 1.0, 0.0).astype(jnp.bfloat16)
                totals[k] = totals[k] + hit * used
        for k in range(classes):
            out_ref[k * cells + low : k * cells + low + band, column : column + cells] = totals[k]


def prepare_kernel(
    windows, held_ref, own_ref, mate_ref, codes_ref,
    product_ref, select_own_ref, select_mate_ref, padded,
):
    rows, classes, _ = held_ref.shape
    tiles, _, cells = codes_ref.shape
    step = away()
    tile = lax.axis_index("tile")
    for block in range(3):
        code = codes_ref[jnp.clip(tile + block * step, 0, tiles - 1)]
        base = (REACH - block * step) * cells
        build_select(code, base, select_own_ref, block * cells, classes)
        if block < 2:
            base = (REACH - (1 + block) * step) * cells
            build_select(code, base, select_mate_ref, block * cells, classes)

    for index, (low, high, offset) in enumerate(windows):
        def run(low=low, high=high, offset=offset):
            pad_into(padded, offset, own_ref, mate_ref)
            right = padded[: high - low, :].astype(jnp.bfloat16)
            for start, size in chunks(rows):
                left = held_ref[start : start + size, :, low:high]
                product_ref[start * classes : (start + size) * classes, :] = jnp.dot(
                    left.reshape(size * classes, high - low), right,
                    preferred_element_type=jnp.float32,
                )
        if len(windows) == 1:
            run()
        else:
            pl.when(lax.axis_index("sub") == index)(run)


def push_kernel(
    windows, held_ref, product_ref, own_ref, mate_ref, select_own_ref, select_mate_ref,
    out_ref, sent_ref, padded, own_terms, mate_terms,
):
    rows, classes, _ = held_ref.shape
    cells = own_ref.shape[1]
    band = 256 // classes
    line = lax.broadcasted_iota(jnp.int32, (256, 256), 0)
    column = lax.broadcasted_iota(jnp.int32, (256, 256), 1)
    apart = (column == (line % band) * classes + line // band).astype(jnp.bfloat16)

    def keep(start, size, value):
        value = value.astype(jnp.bfloat16)
        if size < band:
            value = jnp.concatenate(
                [value, jnp.zeros(((band - size) * classes, 2 * cells), jnp.bfloat16)], axis=0
            )
        value = jnp.dot(apart, value, preferred_element_type=jnp.float32).astype(jnp.bfloat16)
        for k in range(classes):
            part = value[k * band : (k + 1) * band, :]
            own_terms[start : start + band, k * cells : (k + 1) * cells] = part[:, :cells]
            mate_terms[start : start + band, k * cells : (k + 1) * cells] = part[:, cells:]

    bands = [(start, min(band, rows - start)) for start in range(0, rows, band)]
    for index, (low, high, offset) in enumerate(windows):
        def run(low=low, high=high, offset=offset):
            pad_into(padded, offset, own_ref, mate_ref)
            right = padded[: high - low, :].astype(jnp.bfloat16)
            for start, size in bands:
                left = held_ref[start : start + size, :, low:high]
                part = pl.ds(start * classes, size * classes)
                keep(start, size, product_ref[part, :] + jnp.dot(
                    left.reshape(size * classes, high - low), right,
                    preferred_element_type=jnp.float32,
                ))
        pl.when(lax.axis_index("sub") != index)(run)

    if not windows:
        for start, size in bands:
            keep(start, size, product_ref[pl.ds(start * classes, size * classes), :])

    total = jnp.dot(own_terms[...], select_own_ref[...], preferred_element_type=jnp.float32)
    extra = jnp.dot(mate_terms[...], select_mate_ref[...], preferred_element_type=jnp.float32)
    total, extra = total[:rows], extra[:rows]
    out_ref[...] = total[:, :cells] + extra[:, :cells]
    sent_ref[:, :cells] = (total[:, cells : 2 * cells] + extra[:, cells:]).astype(jnp.bfloat16)
    sent_ref[:, cells:] = total[:, 2 * cells :].astype(jnp.bfloat16)


def prepare(held, own, mate, codes, windows):
    rows, classes, depth = held.shape
    cells = codes.shape[2]
    span = max(high - low for low, high, _ in windows)
    return pl.pallas_call(
        functools.partial(prepare_kernel, windows),
        out_shape=[
            jax.ShapeDtypeStruct((rows * classes, 2 * cells), jnp.float32),
            jax.ShapeDtypeStruct((classes * cells, 3 * cells), jnp.bfloat16),
            jax.ShapeDtypeStruct((classes * cells, 2 * cells), jnp.bfloat16),
        ],
        in_specs=[WHOLE] * 4,
        out_specs=[WHOLE] * 3,
        scratch_shapes=[pltpu.VMEM((span, 2 * cells), jnp.float32)],
        cost_estimate=pl.CostEstimate(
            flops=4 * rows * classes * cells * span,
            bytes_accessed=2 * rows * classes * depth,
            transcendentals=0,
        ),
        compiler_params=pltpu.CompilerParams(vmem_limit_bytes=32 << 20),
        name="prepare",
    )(held, own, mate, codes)


def push(held, product, own, mate, select_own, select_mate, windows):
    rows, classes, depth = held.shape
    cells = own.shape[1]
    span = max([high - low for low, high, _ in windows], default=LANES)
    padded_rows = pl.cdiv(rows * classes, 256) * 256 // classes
    return pl.pallas_call(
        functools.partial(push_kernel, windows),
        out_shape=[
            jax.ShapeDtypeStruct((rows, cells), jnp.float32),
            jax.ShapeDtypeStruct((rows, 2 * cells), jnp.bfloat16),
        ],
        in_specs=[WHOLE] * 6,
        out_specs=[WHOLE] * 2,
        scratch_shapes=[
            pltpu.VMEM((span, 2 * cells), jnp.float32),
            pltpu.VMEM((padded_rows, classes * cells), jnp.bfloat16),
            pltpu.VMEM((padded_rows, classes * cells), jnp.bfloat16),
        ],
        cost_estimate=pl.CostEstimate(
            flops=2 * rows * classes * cells * (2 * span + 5 * cells),
            bytes_accessed=2 * rows * classes * depth,
            transcendentals=0,
        ),
        compiler_params=pltpu.CompilerParams(vmem_limit_bytes=40 << 20),
        name="push",
    )(held, product, own, mate, select_own, select_mate)


def shards(up_check, up_inverse, translate, down_inverse, list_slot, list_class, list_count):
    classes, rows, depth = translate.shape
    cells, entries = list_slot.shape
    halves = lax.axis_size("sub") == 2

    active = lax.broadcasted_iota(jnp.int32, (entries, cells), 0) < list_count[None, :]
    code = jnp.where(active, (list_class.T << CLASS_SHIFT) + list_slot.T, -1)
    operators = jnp.transpose(translate, (1, 0, 2))
    codes = lax.all_gather(code, "tile")
    if halves:
        windows = half_windows(rows, depth, 2)
        other_check = across_sub(up_check)
        operators, code = lax.optimization_barrier((operators, code))
        up_held, held, part = stage(up_inverse, up_check, operators, windows)
        part, codes = lax.optimization_barrier((part, codes))
        equivalent = rest(up_held, part, other_check, windows)
        other = across_sub(equivalent)
    else:
        equivalent = lax.all_gather(
            jnp.dot(
                up_inverse, lax.all_gather(up_check, "sub", axis=0, tiled=True),
                preferred_element_type=jnp.float32,
            ).astype(jnp.bfloat16),
            "sub", axis=0, tiled=True,
        )
        windows = [(0, depth, 0)]
        other = equivalent
        held = operators
    product, select_own, select_mate = prepare(
        held, equivalent, to_mate(equivalent), codes, windows
    )
    if halves:
        other, product = lax.optimization_barrier((other, product))
    other_mate = to_mate(other) if halves else other
    own_sum, sent = push(
        held, product, other, other_mate, select_own, select_mate, windows if halves else []
    )

    came = to_near(sent)
    came_far = to_mate(came[:, cells:])
    down_check = (
        own_sum + (came[:, :cells].astype(jnp.float32) + came_far.astype(jnp.float32))
    ).astype(jnp.bfloat16)
    if halves:
        other_down = across_sub(down_check)
        return rest(down_inverse, first(down_inverse, down_check, windows), other_down, windows)
    return jnp.dot(
        down_inverse, lax.all_gather(down_check, "sub", axis=0, tiled=True),
        preferred_element_type=jnp.float32,
    ).astype(jnp.bfloat16)


def solution(mesh):
    in_specs = (
        P("sub", "tile"),
        P("sub", None),
        P(None, "sub", None),
        P("sub", None),
        P("tile", None),
        P("tile", None),
        P("tile"),
    )
    out_specs = P("sub", "tile")
    return jax.shard_map(shards, mesh=mesh, in_specs=in_specs, out_specs=out_specs, check_vma=False)
```

```python
import functools

import jax
import jax.numpy as jnp
from jax import lax
from jax.experimental import pallas as pl
from jax.experimental.pallas import tpu as pltpu
from jax.sharding import PartitionSpec as P

REACH = 2
CLASS_SHIFT = 10
CHUNK = 112
LANES = 128
WHOLE = pl.BlockSpec(memory_space=pltpu.VMEM)


def across_sub(shard):
    return lax.ppermute(shard, "sub", [(0, 1), (1, 0)])


def to_mate(value):
    count = lax.axis_size("tile")
    pairs = [(t, t ^ 1) for t in range(count) if t ^ 1 < count]
    return lax.ppermute(value, "tile", pairs)


def to_near(value):
    count = lax.axis_size("tile")
    pairs = [(t, t + 2 * (t % 2) - 1) for t in range(count)]
    return lax.ppermute(value, "tile", [(a, b) for a, b in pairs if 0 <= b < count])


def to_far(value):
    count = lax.axis_size("tile")
    pairs = [(t, t + 4 * (t % 2) - 2) for t in range(count)]
    return lax.ppermute(value, "tile", [(a, b) for a, b in pairs if 0 <= b < count])


def away():
    return 2 * lax.rem(lax.axis_index("tile"), 2) - 1


def half_windows(shard_rows, depth, count):
    windows = []
    for index in range(count):
        low, high = index * shard_rows, (index + 1) * shard_rows
        start = low // LANES * LANES
        stop = min(pl.cdiv(high, LANES) * LANES, depth)
        windows.append((start, stop, low - start))
    return windows


def chunks(rows):
    return [(start, min(CHUNK, rows - start)) for start in range(0, rows, CHUNK)]


def pad_into(padded, offset, *refs):
    padded[...] = jnp.zeros(padded.shape, padded.dtype)
    for i, ref in enumerate(refs):
        rows, cells = ref.shape
        padded[offset : offset + rows, i * cells : (i + 1) * cells] = ref[...].astype(padded.dtype)


def stage_kernel(windows, matrix_ref, own_ref, held_ref, part_ref, own_held, padded, sems):
    copies = [
        pltpu.make_async_copy(own_ref, own_held, sems.at[0]),
        pltpu.make_async_copy(matrix_ref, held_ref, sems.at[1]),
    ]
    for copy in copies:
        copy.start()
    for copy in copies:
        copy.wait()
    first_kernel(windows, held_ref, own_held, part_ref, padded)


def stage(matrix, own, windows):
    rows, depth = matrix.shape
    cells = own.shape[1]
    span = max(high - low for low, high, _ in windows)
    return pl.pallas_call(
        functools.partial(stage_kernel, windows),
        out_shape=[
            jax.ShapeDtypeStruct(matrix.shape, matrix.dtype),
            jax.ShapeDtypeStruct((rows, cells), jnp.float32),
        ],
        in_specs=[pl.BlockSpec(memory_space=pltpu.HBM)] * 2,
        out_specs=[WHOLE] * 2,
        scratch_shapes=[
            pltpu.VMEM(own.shape, own.dtype),
            pltpu.VMEM((span, cells), jnp.float32),
            pltpu.SemaphoreType.DMA((2,)),
        ],
        cost_estimate=pl.CostEstimate(
            flops=2 * rows * depth * cells, bytes_accessed=4 * matrix.size, transcendentals=0
        ),
        compiler_params=pltpu.CompilerParams(vmem_limit_bytes=24 << 20),
        name="stage",
    )(*[pltpu.with_memory_space_constraint(x, pltpu.HBM) for x in (matrix, own)])


def first_kernel(windows, matrix_ref, own_ref, out_ref, padded):
    for index, (low, high, offset) in enumerate(windows):
        def run(low=low, high=high, offset=offset):
            pad_into(padded, offset, own_ref)
            out_ref[...] = jnp.dot(
                matrix_ref[:, low:high], padded[: high - low, :].astype(jnp.bfloat16),
                preferred_element_type=jnp.float32,
            )
        pl.when(lax.axis_index("sub") == index)(run)


def first(matrix, own, windows):
    rows, depth = matrix.shape
    cells = own.shape[1]
    span = max(high - low for low, high, _ in windows)
    return pl.pallas_call(
        functools.partial(first_kernel, windows),
        out_shape=jax.ShapeDtypeStruct((rows, cells), jnp.float32),
        in_specs=[WHOLE] * 2,
        out_specs=WHOLE,
        scratch_shapes=[pltpu.VMEM((span, cells), jnp.float32)],
        cost_estimate=pl.CostEstimate(
            flops=2 * rows * depth * cells, bytes_accessed=4 * rows * depth, transcendentals=0
        ),
        compiler_params=pltpu.CompilerParams(vmem_limit_bytes=16 << 20),
        name="first",
    )(matrix, own)


def rest_kernel(windows, matrix_ref, part_ref, other_ref, out_ref, padded):
    for index, (low, high, offset) in enumerate(windows):
        def run(low=low, high=high, offset=offset):
            pad_into(padded, offset, other_ref)
            out_ref[...] = (
                part_ref[...]
                + jnp.dot(
                    matrix_ref[:, low:high], padded[: high - low, :].astype(jnp.bfloat16),
                    preferred_element_type=jnp.float32,
                )
            ).astype(jnp.bfloat16)
        pl.when(lax.axis_index("sub") != index)(run)


def rest(matrix, part, other, windows):
    rows, depth = matrix.shape
    cells = other.shape[1]
    span = max(high - low for low, high, _ in windows)
    return pl.pallas_call(
        functools.partial(rest_kernel, windows),
        out_shape=jax.ShapeDtypeStruct((rows, cells), jnp.bfloat16),
        in_specs=[WHOLE] * 3,
        out_specs=WHOLE,
        scratch_shapes=[pltpu.VMEM((span, cells), jnp.float32)],
        cost_estimate=pl.CostEstimate(
            flops=2 * rows * span * cells, bytes_accessed=2 * rows * span, transcendentals=0
        ),
        compiler_params=pltpu.CompilerParams(vmem_limit_bytes=16 << 20),
        name="rest",
    )(matrix, part, other)


def build_select(code, base, out_ref, column, classes):
    entries, cells = code.shape
    slots = (code & ((1 << CLASS_SHIFT) - 1)) - base
    kinds = code >> CLASS_SHIFT
    band = 32
    for low in range(0, cells, band):
        source = lax.broadcasted_iota(jnp.int32, (band, cells), 0) + low
        totals = [jnp.zeros((band, cells), jnp.bfloat16)] * classes
        for entry in range(entries):
            hit = jnp.where(slots[entry : entry + 1, :] == source, 1.0, 0.0).astype(jnp.bfloat16)
            for k in range(classes):
                used = jnp.where(kinds[entry : entry + 1, :] == k, 1.0, 0.0).astype(jnp.bfloat16)
                totals[k] = totals[k] + hit * used
        for k in range(classes):
            out_ref[k * cells + low : k * cells + low + band, column : column + cells] = totals[k]


def prepare_kernel(
    windows, translate_ref, own_ref, code_ref, near_ref, mate_ref, mate_near_ref,
    held_ref, product_ref, away_select_ref, home_select_ref, padded, sems,
):
    rows, classes, _ = translate_ref.shape
    entries, cells = code_ref.shape
    copies = []
    for i, (start, size) in enumerate(chunks(rows)):
        part = pl.ds(start, size)
        copy = pltpu.make_async_copy(translate_ref.at[part], held_ref.at[part], sems.at[i])
        copy.start()
        copies.append(copy)

    step = away()
    for block, (code, offset) in enumerate(
        [(mate_ref[...], -step), (mate_near_ref[...], -2 * step), (near_ref[entries:], 2 * step)]
    ):
        base = (REACH - offset) * cells
        build_select(code, base, away_select_ref, block * cells, classes)
    for block, (code, offset) in enumerate([(code_ref[...], 0), (near_ref[:entries], step)]):
        base = (REACH - offset) * cells
        build_select(code, base, home_select_ref, block * cells, classes)

    for index, (low, high, offset) in enumerate(windows):
        def run(low=low, high=high, offset=offset):
            pad_into(padded, offset, own_ref)
            right = padded[: high - low, :].astype(jnp.bfloat16)
            for copy, (start, size) in zip(copies, chunks(rows)):
                copy.wait()
                left = held_ref[start : start + size, :, low:high]
                product_ref[start * classes : (start + size) * classes, :] = jnp.dot(
                    left.reshape(size * classes, high - low), right,
                    preferred_element_type=jnp.float32,
                )
        if len(windows) == 1:
            run()
        else:
            pl.when(lax.axis_index("sub") == index)(run)


def prepare(operators, own, code, near_codes, mate_code, mate_near_code, windows):
    rows, classes, depth = operators.shape
    cells = code.shape[1]
    span = max(high - low for low, high, _ in windows)
    return pl.pallas_call(
        functools.partial(prepare_kernel, windows),
        out_shape=[
            jax.ShapeDtypeStruct((rows, classes, depth), jnp.bfloat16),
            jax.ShapeDtypeStruct((rows * classes, cells), jnp.float32),
            jax.ShapeDtypeStruct((classes * cells, 3 * cells), jnp.bfloat16),
            jax.ShapeDtypeStruct((classes * cells, 2 * cells), jnp.bfloat16),
        ],
        in_specs=[pl.BlockSpec(memory_space=pltpu.HBM)] + [WHOLE] * 5,
        out_specs=[WHOLE] * 4,
        scratch_shapes=[
            pltpu.VMEM((span, cells), jnp.float32),
            pltpu.SemaphoreType.DMA((len(chunks(rows)),)),
        ],
        cost_estimate=pl.CostEstimate(
            flops=4 * rows * classes * cells * span,
            bytes_accessed=2 * rows * classes * depth,
            transcendentals=0,
        ),
        compiler_params=pltpu.CompilerParams(vmem_limit_bytes=32 << 20),
        name="prepare",
    )(
        pltpu.with_memory_space_constraint(operators, pltpu.HBM),
        own, code, near_codes, mate_code, mate_near_code,
    )


def push_away_kernel(
    windows, held_ref, product_ref, other_ref, select_ref,
    terms_ref, mate_ref, far_ref, padded, product,
):
    rows, classes, _ = held_ref.shape
    cells = far_ref.shape[1]

    def part_classes(source, start, size):
        for k in range(classes):
            term = source[pl.ds(start * classes + k, size, stride=classes), :]
            terms_ref[start : start + size, k * cells : (k + 1) * cells] = term.astype(jnp.bfloat16)

    for index, (low, high, offset) in enumerate(windows):
        def run(low=low, high=high, offset=offset):
            pad_into(padded, offset, other_ref)
            right = padded[: high - low, :].astype(jnp.bfloat16)
            for start, size in chunks(rows):
                left = held_ref[start : start + size, :, low:high]
                part = slice(start * classes, (start + size) * classes)
                product[part, :] = product_ref[part, :] + jnp.dot(
                    left.reshape(size * classes, high - low), right,
                    preferred_element_type=jnp.float32,
                )
                part_classes(product, start, size)
        pl.when(lax.axis_index("sub") != index)(run)

    if not windows:
        for start, size in chunks(rows):
            part_classes(product_ref, start, size)

    total = jnp.dot(terms_ref[...], select_ref[...], preferred_element_type=jnp.float32)
    mate_ref[...] = total[:, : 2 * cells].astype(jnp.bfloat16)
    far_ref[...] = total[:, 2 * cells :].astype(jnp.bfloat16)


def push_away(held, product, other, select, windows):
    rows, classes, depth = held.shape
    cells = other.shape[1]
    span = max([high - low for low, high, _ in windows], default=LANES)
    return pl.pallas_call(
        functools.partial(push_away_kernel, windows),
        out_shape=[
            jax.ShapeDtypeStruct((rows, classes * cells), jnp.bfloat16),
            jax.ShapeDtypeStruct((rows, 2 * cells), jnp.bfloat16),
            jax.ShapeDtypeStruct((rows, cells), jnp.bfloat16),
        ],
        in_specs=[WHOLE] * 4,
        out_specs=[WHOLE] * 3,
        scratch_shapes=[
            pltpu.VMEM((span, cells), jnp.float32),
            pltpu.VMEM((rows * classes, cells), jnp.float32),
        ],
        cost_estimate=pl.CostEstimate(
            flops=2 * rows * classes * cells * (span + 3 * cells),
            bytes_accessed=2 * rows * classes * depth,
            transcendentals=0,
        ),
        compiler_params=pltpu.CompilerParams(vmem_limit_bytes=32 << 20),
        name="push_away",
    )(held, product, other, select)


def push_home_kernel(terms_ref, select_ref, came_ref, own_ref, near_ref):
    cells = near_ref.shape[1]
    total = jnp.dot(terms_ref[...], select_ref[...], preferred_element_type=jnp.float32)
    total = total + came_ref[...].astype(jnp.float32)
    own_ref[...] = total[:, :cells]
    near_ref[...] = total[:, cells:].astype(jnp.bfloat16)


def push_home(terms, select, came):
    rows = terms.shape[0]
    cells = select.shape[1] // 2
    return pl.pallas_call(
        push_home_kernel,
        out_shape=[
            jax.ShapeDtypeStruct((rows, cells), jnp.float32),
            jax.ShapeDtypeStruct((rows, cells), jnp.bfloat16),
        ],
        in_specs=[WHOLE] * 3,
        out_specs=[WHOLE] * 2,
        cost_estimate=pl.CostEstimate(
            flops=2 * terms.size * 2 * cells, bytes_accessed=4 * terms.size, transcendentals=0
        ),
        compiler_params=pltpu.CompilerParams(vmem_limit_bytes=16 << 20),
        name="push_home",
    )(terms, select, came)


def shards(up_check, up_inverse, translate, down_inverse, list_slot, list_class, list_count):
    classes, rows, depth = translate.shape
    cells, entries = list_slot.shape
    halves = lax.axis_size("sub") == 2

    active = lax.broadcasted_iota(jnp.int32, (entries, cells), 0) < list_count[None, :]
    code = jnp.where(active, (list_class.T << CLASS_SHIFT) + list_slot.T, -1)
    operators = jnp.transpose(translate, (1, 0, 2))
    mate_code = to_mate(code)
    near_codes = to_near(jnp.concatenate([code, mate_code], axis=0))
    mate_near_code = to_mate(near_codes[:entries])

    operators = jnp.transpose(translate, (1, 0, 2))
    if halves:
        windows = half_windows(rows, depth, 2)
        other_check = across_sub(up_check)
        staged, code = lax.optimization_barrier((up_inverse, code))
        up_held, part = stage(staged, up_check, windows)
        part, near_codes = lax.optimization_barrier((part, near_codes))
        equivalent = rest(up_held, part, other_check, windows)
        other = across_sub(equivalent)
    else:
        equivalent = lax.all_gather(
            jnp.dot(
                up_inverse, lax.all_gather(up_check, "sub", axis=0, tiled=True),
                preferred_element_type=jnp.float32,
            ).astype(jnp.bfloat16),
            "sub", axis=0, tiled=True,
        )
        windows = [(0, depth, 0)]
        other = equivalent
    held, product, away_select, home_select = prepare(
        operators, equivalent, code, near_codes, mate_code, mate_near_code, windows
    )
    terms, mate_sum, far_sum = push_away(
        held, product, other, away_select, windows if halves else []
    )
    mate_came = to_mate(mate_sum)
    far_came = to_far(far_sum)
    own_sum, near_sum = push_home(terms, home_select, mate_came)
    near_came = to_near(near_sum)
    down_check = (
        own_sum + (far_came.astype(jnp.float32) + near_came.astype(jnp.float32))
    ).astype(jnp.bfloat16)
    if halves:
        other_down = across_sub(down_check)
        return rest(down_inverse, first(down_inverse, down_check, windows), other_down, windows)
    return jnp.dot(
        down_inverse, lax.all_gather(down_check, "sub", axis=0, tiled=True),
        preferred_element_type=jnp.float32,
    ).astype(jnp.bfloat16)


def solution(mesh):
    in_specs = (
        P("sub", "tile"),
        P("sub", None),
        P(None, "sub", None),
        P("sub", None),
        P("tile", None),
        P("tile", None),
        P("tile"),
    )
    out_specs = P("sub", "tile")
    return jax.shard_map(shards, mesh=mesh, in_specs=in_specs, out_specs=out_specs, check_vma=False)
```

```python
import functools

import jax
import jax.numpy as jnp
from jax import lax
from jax.experimental import pallas as pl
from jax.experimental.pallas import tpu as pltpu
from jax.sharding import PartitionSpec as P

REACH = 2
CLASS_SHIFT = 10
CHUNK = 112
LANES = 128
PREPARE = 1 << 32
WHOLE = pl.BlockSpec(memory_space=pltpu.VMEM)


def across_sub(shard):
    return lax.ppermute(shard, "sub", [(0, 1), (1, 0)])


def to_mate(value):
    count = lax.axis_size("tile")
    pairs = [(t, t ^ 1) for t in range(count) if t ^ 1 < count]
    return lax.ppermute(value, "tile", pairs)


def to_near(value):
    count = lax.axis_size("tile")
    pairs = [(t, t + 2 * (t % 2) - 1) for t in range(count)]
    return lax.ppermute(value, "tile", [(a, b) for a, b in pairs if 0 <= b < count])


def to_far(value):
    count = lax.axis_size("tile")
    pairs = [(t, t + 4 * (t % 2) - 2) for t in range(count)]
    return lax.ppermute(value, "tile", [(a, b) for a, b in pairs if 0 <= b < count])


def away():
    return 2 * lax.rem(lax.axis_index("tile"), 2) - 1


def half_windows(shard_rows, depth, count):
    windows = []
    for index in range(count):
        low, high = index * shard_rows, (index + 1) * shard_rows
        start = low // LANES * LANES
        stop = min(pl.cdiv(high, LANES) * LANES, depth)
        windows.append((start, stop, low - start))
    return windows


def chunks(rows):
    return [(start, min(CHUNK, rows - start)) for start in range(0, rows, CHUNK)]


def pad_into(padded, offset, *refs):
    padded[...] = jnp.zeros(padded.shape, padded.dtype)
    for i, ref in enumerate(refs):
        rows, cells = ref.shape
        padded[offset : offset + rows, i * cells : (i + 1) * cells] = ref[...].astype(padded.dtype)


def first_kernel(windows, matrix_ref, own_ref, out_ref, padded):
    for index, (low, high, offset) in enumerate(windows):
        def run(low=low, high=high, offset=offset):
            pad_into(padded, offset, own_ref)
            out_ref[...] = jnp.dot(
                matrix_ref[:, low:high], padded[: high - low, :].astype(jnp.bfloat16),
                preferred_element_type=jnp.float32,
            )
        pl.when(lax.axis_index("sub") == index)(run)


def first(matrix, own, windows):
    rows, depth = matrix.shape
    cells = own.shape[1]
    span = max(high - low for low, high, _ in windows)
    return pl.pallas_call(
        functools.partial(first_kernel, windows),
        out_shape=jax.ShapeDtypeStruct((rows, cells), jnp.float32),
        in_specs=[WHOLE] * 2,
        out_specs=WHOLE,
        scratch_shapes=[pltpu.VMEM((span, cells), jnp.float32)],
        cost_estimate=pl.CostEstimate(
            flops=2 * rows * depth * cells, bytes_accessed=4 * rows * depth, transcendentals=0
        ),
        compiler_params=pltpu.CompilerParams(vmem_limit_bytes=16 << 20),
        name="first",
    )(matrix, own)


def rest_kernel(windows, matrix_ref, part_ref, other_ref, out_ref, padded):
    for index, (low, high, offset) in enumerate(windows):
        def run(low=low, high=high, offset=offset):
            pad_into(padded, offset, other_ref)
            out_ref[...] = (
                part_ref[...]
                + jnp.dot(
                    matrix_ref[:, low:high], padded[: high - low, :].astype(jnp.bfloat16),
                    preferred_element_type=jnp.float32,
                )
            ).astype(jnp.bfloat16)
        pl.when(lax.axis_index("sub") != index)(run)


def rest(matrix, part, other, windows):
    rows, depth = matrix.shape
    cells = other.shape[1]
    span = max(high - low for low, high, _ in windows)
    return pl.pallas_call(
        functools.partial(rest_kernel, windows),
        out_shape=jax.ShapeDtypeStruct((rows, cells), jnp.bfloat16),
        in_specs=[WHOLE] * 3,
        out_specs=WHOLE,
        scratch_shapes=[pltpu.VMEM((span, cells), jnp.float32)],
        cost_estimate=pl.CostEstimate(
            flops=2 * rows * span * cells, bytes_accessed=2 * rows * span, transcendentals=0
        ),
        compiler_params=pltpu.CompilerParams(vmem_limit_bytes=16 << 20),
        name="rest",
    )(matrix, part, other)


def build_select(code, base, out_ref, classes):
    entries, cells = code.shape
    slots = (code & ((1 << CLASS_SHIFT) - 1)) - base
    kinds = code >> CLASS_SHIFT
    band = 32
    for low in range(0, cells, band):
        source = lax.broadcasted_iota(jnp.int32, (band, cells), 0) + low
        totals = [jnp.zeros((band, cells), jnp.bfloat16)] * classes
        for entry in range(entries):
            hit = jnp.where(slots[entry : entry + 1, :] == source, 1.0, 0.0).astype(jnp.bfloat16)
            for k in range(classes):
                used = jnp.where(kinds[entry : entry + 1, :] == k, 1.0, 0.0).astype(jnp.bfloat16)
                totals[k] = totals[k] + hit * used
        for k in range(classes):
            out_ref[k * cells + low : k * cells + low + band, :] = totals[k]


def prepare_kernel(
    windows, translate_ref, own_ref, code_ref, mate_ref,
    held_ref, product_ref, home_ref, mate_select_ref, padded, sems,
):
    rows, classes, _ = translate_ref.shape
    cells = code_ref.shape[1]
    copies = []
    for i, (start, size) in enumerate(chunks(rows)):
        part = pl.ds(start, size)
        copy = pltpu.make_async_copy(translate_ref.at[part], held_ref.at[part], sems.at[i])
        copy.start()
        copies.append(copy)

    build_select(code_ref[...], REACH * cells, home_ref, classes)
    build_select(mate_ref[...], (REACH + away()) * cells, mate_select_ref, classes)

    for index, (low, high, offset) in enumerate(windows):
        def run(low=low, high=high, offset=offset):
            pad_into(padded, offset, own_ref)
            right = padded[: high - low, :].astype(jnp.bfloat16)
            for copy, (start, size) in zip(copies, chunks(rows)):
                copy.wait()
                left = held_ref[start : start + size, :, low:high]
                product_ref[start * classes : (start + size) * classes, :] = jnp.dot(
                    left.reshape(size * classes, high - low), right,
                    preferred_element_type=jnp.float32,
                )
        if len(windows) == 1:
            run()
        else:
            pl.when(lax.axis_index("sub") == index)(run)


def prepare(operators, own, code, mate_code, windows):
    rows, classes, depth = operators.shape
    cells = code.shape[1]
    span = max(high - low for low, high, _ in windows)
    select = jax.ShapeDtypeStruct((classes * cells, cells), jnp.bfloat16)
    return pl.pallas_call(
        functools.partial(prepare_kernel, windows),
        out_shape=[
            jax.ShapeDtypeStruct((rows, classes, depth), jnp.bfloat16),
            jax.ShapeDtypeStruct((rows * classes, cells), jnp.float32),
            select,
            select,
        ],
        in_specs=[pl.BlockSpec(memory_space=pltpu.HBM)] + [WHOLE] * 3,
        out_specs=[WHOLE] * 4,
        scratch_shapes=[
            pltpu.VMEM((span, cells), jnp.float32),
            pltpu.SemaphoreType.DMA((len(chunks(rows)),)),
        ],
        cost_estimate=pl.CostEstimate(flops=PREPARE, bytes_accessed=0, transcendentals=0),
        compiler_params=pltpu.CompilerParams(vmem_limit_bytes=32 << 20),
        name="prepare",
    )(pltpu.with_memory_space_constraint(operators, pltpu.HBM), own, code, mate_code)


def select_kernel(near_ref, near_select_ref, far_select_ref):
    entries, cells = near_ref.shape[0] // 2, near_ref.shape[1]
    classes = near_select_ref.shape[0] // cells
    step = away()
    build_select(near_ref[:entries, :], (REACH - step) * cells, near_select_ref, classes)
    build_select(near_ref[entries:, :], (REACH - 2 * step) * cells, far_select_ref, classes)


def selections(near_codes, classes):
    cells = near_codes.shape[1]
    select = jax.ShapeDtypeStruct((classes * cells, cells), jnp.bfloat16)
    return pl.pallas_call(
        select_kernel,
        out_shape=[select, select],
        in_specs=[WHOLE],
        out_specs=[WHOLE] * 2,
        cost_estimate=pl.CostEstimate(flops=PREPARE, bytes_accessed=0, transcendentals=0),
        compiler_params=pltpu.CompilerParams(vmem_limit_bytes=8 << 20),
        name="selections",
    )(near_codes)


def push_away_kernel(
    windows, held_ref, product_ref, other_ref, mate_select_ref, far_select_ref, code_ref,
    terms_ref, mate_ref, far_ref, padded, product, select,
):
    rows, classes, _ = held_ref.shape
    cells = far_ref.shape[1]
    build_select(code_ref[...], (REACH + 2 * away()) * cells, select, classes)

    def part_classes(source, start, size):
        for k in range(classes):
            term = source[pl.ds(start * classes + k, size, stride=classes), :]
            terms_ref[start : start + size, k * cells : (k + 1) * cells] = term.astype(jnp.bfloat16)

    for index, (low, high, offset) in enumerate(windows):
        def run(low=low, high=high, offset=offset):
            pad_into(padded, offset, other_ref)
            right = padded[: high - low, :].astype(jnp.bfloat16)
            for start, size in chunks(rows):
                left = held_ref[start : start + size, :, low:high]
                part = slice(start * classes, (start + size) * classes)
                product[part, :] = product_ref[part, :] + jnp.dot(
                    left.reshape(size * classes, high - low), right,
                    preferred_element_type=jnp.float32,
                )
                part_classes(product, start, size)
        pl.when(lax.axis_index("sub") != index)(run)

    if not windows:
        for start, size in chunks(rows):
            part_classes(product_ref, start, size)

    for ref, column, chosen in (
        (mate_ref, 0, mate_select_ref), (far_ref, 0, far_select_ref), (mate_ref, cells, select)
    ):
        ref[:, column : column + cells] = jnp.dot(
            terms_ref[...], chosen[...], preferred_element_type=jnp.float32
        ).astype(jnp.bfloat16)


def push_away(held, product, other, mate_select, far_select, code, windows):
    rows, classes, depth = held.shape
    cells = other.shape[1]
    span = max([high - low for low, high, _ in windows], default=LANES)
    return pl.pallas_call(
        functools.partial(push_away_kernel, windows),
        out_shape=[
            jax.ShapeDtypeStruct((rows, classes * cells), jnp.bfloat16),
            jax.ShapeDtypeStruct((rows, 2 * cells), jnp.bfloat16),
            jax.ShapeDtypeStruct((rows, cells), jnp.bfloat16),
        ],
        in_specs=[WHOLE] * 6,
        out_specs=[WHOLE] * 3,
        scratch_shapes=[
            pltpu.VMEM((span, cells), jnp.float32),
            pltpu.VMEM((rows * classes, cells), jnp.float32),
            pltpu.VMEM((classes * cells, cells), jnp.bfloat16),
        ],
        cost_estimate=pl.CostEstimate(
            flops=2 * rows * classes * cells * (span + 3 * cells),
            bytes_accessed=2 * rows * classes * depth,
            transcendentals=0,
        ),
        compiler_params=pltpu.CompilerParams(vmem_limit_bytes=32 << 20),
        name="push_away",
    )(held, product, other, mate_select, far_select, code)


def push_home_kernel(terms_ref, home_ref, near_select_ref, came_ref, own_ref, near_ref):
    cells = near_ref.shape[1]
    terms = terms_ref[...]
    near_ref[...] = (
        jnp.dot(terms, near_select_ref[...], preferred_element_type=jnp.float32)
        + came_ref[:, cells:].astype(jnp.float32)
    ).astype(jnp.bfloat16)
    own_ref[...] = jnp.dot(
        terms, home_ref[...], preferred_element_type=jnp.float32
    ) + came_ref[:, :cells].astype(jnp.float32)


def push_home(terms, home, near_select, came):
    rows = terms.shape[0]
    cells = home.shape[1]
    return pl.pallas_call(
        push_home_kernel,
        out_shape=[
            jax.ShapeDtypeStruct((rows, cells), jnp.float32),
            jax.ShapeDtypeStruct((rows, cells), jnp.bfloat16),
        ],
        in_specs=[WHOLE] * 4,
        out_specs=[WHOLE] * 2,
        cost_estimate=pl.CostEstimate(
            flops=2 * terms.size * 2 * cells, bytes_accessed=4 * terms.size, transcendentals=0
        ),
        compiler_params=pltpu.CompilerParams(vmem_limit_bytes=16 << 20),
        name="push_home",
    )(terms, home, near_select, came)


def shards(up_check, up_inverse, translate, down_inverse, list_slot, list_class, list_count):
    classes, rows, depth = translate.shape
    cells, entries = list_slot.shape
    halves = lax.axis_size("sub") == 2

    active = lax.broadcasted_iota(jnp.int32, (entries, cells), 0) < list_count[None, :]
    code = jnp.where(active, (list_class.T << CLASS_SHIFT) + list_slot.T, -1)
    operators = jnp.transpose(translate, (1, 0, 2))
    mate_code = to_mate(code)
    near_codes = to_near(jnp.concatenate([code, mate_code], axis=0))

    operators = jnp.transpose(translate, (1, 0, 2))
    if halves:
        windows = half_windows(rows, depth, 2)
        mine = lax.axis_index("sub") * rows
        check = lax.dynamic_update_slice(
            jnp.zeros((depth, cells), up_check.dtype), up_check, (mine, 0)
        )
        check, mate_code = lax.optimization_barrier((check, mate_code))
        check = lax.dynamic_update_slice(check, across_sub(up_check), (rows - mine, 0))
    else:
        windows = [(0, depth, 0)]
        check = lax.all_gather(up_check, "sub", axis=0, tiled=True)
    equivalent = jnp.dot(up_inverse, check, preferred_element_type=jnp.float32)
    equivalent = equivalent.astype(jnp.bfloat16)
    if halves:
        other = across_sub(equivalent)
    else:
        equivalent = lax.all_gather(equivalent, "sub", axis=0, tiled=True)
        other = equivalent
    held, product, home, mate_select = prepare(operators, equivalent, code, mate_code, windows)
    near_codes, product = lax.optimization_barrier((near_codes, product))
    near_select, far_select = selections(near_codes, classes)
    mate_near_code = to_mate(near_codes[:entries])
    terms, mate_sum, far_sum = push_away(
        held, product, other, mate_select, far_select, mate_near_code, windows if halves else []
    )
    mate_came = to_mate(mate_sum)
    far_came = to_far(far_sum)
    own_sum, near_sum = push_home(terms, home, near_select, mate_came)
    near_came = to_near(near_sum)
    down_check = (
        own_sum + (far_came.astype(jnp.float32) + near_came.astype(jnp.float32))
    ).astype(jnp.bfloat16)
    if halves:
        other_down = across_sub(down_check)
        return rest(down_inverse, first(down_inverse, down_check, windows), other_down, windows)
    return jnp.dot(
        down_inverse, lax.all_gather(down_check, "sub", axis=0, tiled=True),
        preferred_element_type=jnp.float32,
    ).astype(jnp.bfloat16)


def solution(mesh):
    in_specs = (
        P("sub", "tile"),
        P("sub", None),
        P(None, "sub", None),
        P("sub", None),
        P("tile", None),
        P("tile", None),
        P("tile"),
    )
    out_specs = P("sub", "tile")
    return jax.shard_map(shards, mesh=mesh, in_specs=in_specs, out_specs=out_specs, check_vma=False)
```

```python
import functools

import jax
import jax.numpy as jnp
from jax import lax
from jax.experimental import pallas as pl
from jax.experimental.pallas import tpu as pltpu
from jax.sharding import PartitionSpec as P

REACH = 2
CLASS_SHIFT = 10
CHUNK = 112
LANES = 128
LOAD = 56
IN_FLIGHT = 3
WHOLE = pl.BlockSpec(memory_space=pltpu.VMEM)


def across_sub(shard):
    return lax.ppermute(shard, "sub", [(0, 1), (1, 0)])


def to_mate(value):
    count = lax.axis_size("tile")
    pairs = [(t, t ^ 1) for t in range(count) if t ^ 1 < count]
    return lax.ppermute(value, "tile", pairs)


def to_near(value):
    count = lax.axis_size("tile")
    pairs = [(t, t + 2 * (t % 2) - 1) for t in range(count)]
    return lax.ppermute(value, "tile", [(a, b) for a, b in pairs if 0 <= b < count])


def to_far(value):
    count = lax.axis_size("tile")
    pairs = [(t, t + 4 * (t % 2) - 2) for t in range(count)]
    return lax.ppermute(value, "tile", [(a, b) for a, b in pairs if 0 <= b < count])


def away():
    return 2 * lax.rem(lax.axis_index("tile"), 2) - 1


def half_windows(shard_rows, depth, count):
    windows = []
    for index in range(count):
        low, high = index * shard_rows, (index + 1) * shard_rows
        start = low // LANES * LANES
        stop = min(pl.cdiv(high, LANES) * LANES, depth)
        windows.append((start, stop, low - start))
    return windows


def chunks(rows, size):
    return [(start, min(size, rows - start)) for start in range(0, rows, size)]


def pad_into(padded, offset, *refs):
    padded[...] = jnp.zeros(padded.shape, padded.dtype)
    for i, ref in enumerate(refs):
        rows, cells = ref.shape
        padded[offset : offset + rows, i * cells : (i + 1) * cells] = ref[...].astype(padded.dtype)


def stage_kernel(windows, matrix_ref, own_ref, held_ref, part_ref, own_held, padded, sems):
    copies = [
        pltpu.make_async_copy(own_ref, own_held, sems.at[0]),
        pltpu.make_async_copy(matrix_ref, held_ref, sems.at[1]),
    ]
    for copy in copies:
        copy.start()
    for copy in copies:
        copy.wait()
    first_kernel(windows, held_ref, own_held, part_ref, padded)


def stage(matrix, own, windows):
    rows, depth = matrix.shape
    cells = own.shape[1]
    span = max(high - low for low, high, _ in windows)
    return pl.pallas_call(
        functools.partial(stage_kernel, windows),
        out_shape=[
            jax.ShapeDtypeStruct(matrix.shape, matrix.dtype),
            jax.ShapeDtypeStruct((rows, cells), jnp.float32),
        ],
        in_specs=[pl.BlockSpec(memory_space=pltpu.HBM)] * 2,
        out_specs=[WHOLE] * 2,
        scratch_shapes=[
            pltpu.VMEM(own.shape, own.dtype),
            pltpu.VMEM((span, cells), jnp.float32),
            pltpu.SemaphoreType.DMA((2,)),
        ],
        cost_estimate=pl.CostEstimate(
            flops=2 * rows * depth * cells, bytes_accessed=4 * matrix.size, transcendentals=0
        ),
        compiler_params=pltpu.CompilerParams(vmem_limit_bytes=24 << 20),
        name="stage",
    )(*[pltpu.with_memory_space_constraint(x, pltpu.HBM) for x in (matrix, own)])


def first_kernel(windows, matrix_ref, own_ref, out_ref, padded):
    for index, (low, high, offset) in enumerate(windows):
        def run(low=low, high=high, offset=offset):
            pad_into(padded, offset, own_ref)
            out_ref[...] = jnp.dot(
                matrix_ref[:, low:high], padded[: high - low, :].astype(jnp.bfloat16),
                preferred_element_type=jnp.float32,
            )
        pl.when(lax.axis_index("sub") == index)(run)


def first(matrix, own, windows):
    rows, depth = matrix.shape
    cells = own.shape[1]
    span = max(high - low for low, high, _ in windows)
    return pl.pallas_call(
        functools.partial(first_kernel, windows),
        out_shape=jax.ShapeDtypeStruct((rows, cells), jnp.float32),
        in_specs=[WHOLE] * 2,
        out_specs=WHOLE,
        scratch_shapes=[pltpu.VMEM((span, cells), jnp.float32)],
        cost_estimate=pl.CostEstimate(
            flops=2 * rows * depth * cells, bytes_accessed=4 * rows * depth, transcendentals=0
        ),
        compiler_params=pltpu.CompilerParams(vmem_limit_bytes=16 << 20),
        name="first",
    )(matrix, own)


def rest_kernel(windows, matrix_ref, part_ref, other_ref, out_ref, padded):
    for index, (low, high, offset) in enumerate(windows):
        def run(low=low, high=high, offset=offset):
            pad_into(padded, offset, other_ref)
            out_ref[...] = (
                part_ref[...]
                + jnp.dot(
                    matrix_ref[:, low:high], padded[: high - low, :].astype(jnp.bfloat16),
                    preferred_element_type=jnp.float32,
                )
            ).astype(jnp.bfloat16)
        pl.when(lax.axis_index("sub") != index)(run)


def rest(matrix, part, other, windows):
    rows, depth = matrix.shape
    cells = other.shape[1]
    span = max(high - low for low, high, _ in windows)
    return pl.pallas_call(
        functools.partial(rest_kernel, windows),
        out_shape=jax.ShapeDtypeStruct((rows, cells), jnp.bfloat16),
        in_specs=[WHOLE] * 3,
        out_specs=WHOLE,
        scratch_shapes=[pltpu.VMEM((span, cells), jnp.float32)],
        cost_estimate=pl.CostEstimate(
            flops=2 * rows * span * cells, bytes_accessed=2 * rows * span, transcendentals=0
        ),
        compiler_params=pltpu.CompilerParams(vmem_limit_bytes=16 << 20),
        name="rest",
    )(matrix, part, other)


def build_select(code, base, out_ref, column, classes):
    entries, cells = code.shape
    slots = (code & ((1 << CLASS_SHIFT) - 1)) - base
    kinds = code >> CLASS_SHIFT
    band = 32
    for low in range(0, cells, band):
        source = lax.broadcasted_iota(jnp.int32, (band, cells), 0) + low
        totals = [jnp.zeros((band, cells), jnp.bfloat16)] * classes
        for entry in range(entries):
            hit = jnp.where(slots[entry : entry + 1, :] == source, 1.0, 0.0).astype(jnp.bfloat16)
            for k in range(classes):
                used = jnp.where(kinds[entry : entry + 1, :] == k, 1.0, 0.0).astype(jnp.bfloat16)
                totals[k] = totals[k] + hit * used
        for k in range(classes):
            row = k * cells + low
            out_ref[row : row + band, column : column + cells] = totals[k]


def prepare_kernel(
    windows, translate_ref, own_ref, code_ref, mate_ref, near_ref,
    held_ref, product_ref, home_ref, away_ref, padded, sems,
):
    rows, classes, _ = translate_ref.shape
    entries, cells = code_ref.shape
    parts = chunks(rows, LOAD)
    copies = []
    for i, (start, size) in enumerate(parts):
        part = pl.ds(start, size)
        copies.append(
            pltpu.make_async_copy(translate_ref.at[part], held_ref.at[part], sems.at[i])
        )
    for copy in copies[:IN_FLIGHT]:
        copy.start()

    step = away()
    build_select(code_ref[...], REACH * cells, home_ref, 0, classes)
    build_select(near_ref[:entries, :], (REACH - step) * cells, home_ref, cells, classes)
    build_select(mate_ref[...], (REACH + step) * cells, away_ref, 0, classes)
    build_select(near_ref[entries:, :], (REACH - 2 * step) * cells, away_ref, cells, classes)

    for index, (low, high, offset) in enumerate(windows):
        def run(low=low, high=high, offset=offset):
            pad_into(padded, offset, own_ref)
            right = padded[: high - low, :].astype(jnp.bfloat16)
            for i, (start, size) in enumerate(parts):
                copies[i].wait()
                if i + IN_FLIGHT < len(parts):
                    copies[i + IN_FLIGHT].start()
                left = held_ref[start : start + size, :, low:high]
                product_ref[start * classes : (start + size) * classes, :] = jnp.dot(
                    left.reshape(size * classes, high - low), right,
                    preferred_element_type=jnp.float32,
                )
        if len(windows) == 1:
            run()
        else:
            pl.when(lax.axis_index("sub") == index)(run)


def prepare(operators, own, code, mate_code, near_codes, windows):
    rows, classes, depth = operators.shape
    cells = code.shape[1]
    span = max(high - low for low, high, _ in windows)
    select = jax.ShapeDtypeStruct((classes * cells, 2 * cells), jnp.bfloat16)
    return pl.pallas_call(
        functools.partial(prepare_kernel, windows),
        out_shape=[
            jax.ShapeDtypeStruct((rows, classes, depth), jnp.bfloat16),
            jax.ShapeDtypeStruct((rows * classes, cells), jnp.float32),
            select,
            select,
        ],
        in_specs=[pl.BlockSpec(memory_space=pltpu.HBM)] + [WHOLE] * 4,
        out_specs=[WHOLE] * 4,
        scratch_shapes=[
            pltpu.VMEM((span, cells), jnp.float32),
            pltpu.SemaphoreType.DMA((len(chunks(rows, LOAD)),)),
        ],
        cost_estimate=pl.CostEstimate(flops=1 << 32, bytes_accessed=0, transcendentals=0),
        compiler_params=pltpu.CompilerParams(vmem_limit_bytes=32 << 20),
        name="prepare",
    )(
        pltpu.with_memory_space_constraint(operators, pltpu.HBM),
        own, code, mate_code, near_codes,
    )


def push_away_kernel(
    windows, held_ref, product_ref, other_ref, away_ref, code_ref,
    terms_ref, mate_ref, far_ref, padded, product, select,
):
    rows, classes, _ = held_ref.shape
    cells = far_ref.shape[1]
    build_select(code_ref[...], (REACH + 2 * away()) * cells, select, 0, classes)

    def part_classes(source, start, size):
        for k in range(classes):
            term = source[pl.ds(start * classes + k, size, stride=classes), :]
            terms_ref[start : start + size, k * cells : (k + 1) * cells] = term.astype(jnp.bfloat16)

    for index, (low, high, offset) in enumerate(windows):
        def run(low=low, high=high, offset=offset):
            pad_into(padded, offset, other_ref)
            right = padded[: high - low, :].astype(jnp.bfloat16)
            for start, size in chunks(rows, CHUNK):
                left = held_ref[start : start + size, :, low:high]
                part = slice(start * classes, (start + size) * classes)
                product[part, :] = product_ref[part, :] + jnp.dot(
                    left.reshape(size * classes, high - low), right,
                    preferred_element_type=jnp.float32,
                )
                part_classes(product, start, size)
        pl.when(lax.axis_index("sub") != index)(run)

    if not windows:
        for start, size in chunks(rows, CHUNK):
            part_classes(product_ref, start, size)

    terms = terms_ref[...]
    total = jnp.dot(terms, away_ref[...], preferred_element_type=jnp.float32)
    mate_ref[:, :cells] = total[:, :cells].astype(jnp.bfloat16)
    far_ref[...] = total[:, cells:].astype(jnp.bfloat16)
    mate_ref[:, cells:] = jnp.dot(
        terms, select[...], preferred_element_type=jnp.float32
    ).astype(jnp.bfloat16)


def push_away(held, product, other, away_select, code, windows):
    rows, classes, depth = held.shape
    cells = other.shape[1]
    span = max([high - low for low, high, _ in windows], default=LANES)
    return pl.pallas_call(
        functools.partial(push_away_kernel, windows),
        out_shape=[
            jax.ShapeDtypeStruct((rows, classes * cells), jnp.bfloat16),
            jax.ShapeDtypeStruct((rows, 2 * cells), jnp.bfloat16),
            jax.ShapeDtypeStruct((rows, cells), jnp.bfloat16),
        ],
        in_specs=[WHOLE] * 5,
        out_specs=[WHOLE] * 3,
        scratch_shapes=[
            pltpu.VMEM((span, cells), jnp.float32),
            pltpu.VMEM((rows * classes, cells), jnp.float32),
            pltpu.VMEM((classes * cells, cells), jnp.bfloat16),
        ],
        cost_estimate=pl.CostEstimate(
            flops=2 * rows * classes * cells * (span + 3 * cells),
            bytes_accessed=2 * rows * classes * depth,
            transcendentals=0,
        ),
        compiler_params=pltpu.CompilerParams(vmem_limit_bytes=32 << 20),
        name="push_away",
    )(held, product, other, away_select, code)


def push_home_kernel(terms_ref, select_ref, came_ref, own_ref, near_ref):
    cells = near_ref.shape[1]
    total = jnp.dot(terms_ref[...], select_ref[...], preferred_element_type=jnp.float32)
    total = total + came_ref[...].astype(jnp.float32)
    own_ref[...] = total[:, :cells]
    near_ref[...] = total[:, cells:].astype(jnp.bfloat16)


def push_home(terms, select, came):
    rows = terms.shape[0]
    cells = select.shape[1] // 2
    return pl.pallas_call(
        push_home_kernel,
        out_shape=[
            jax.ShapeDtypeStruct((rows, cells), jnp.float32),
            jax.ShapeDtypeStruct((rows, cells), jnp.bfloat16),
        ],
        in_specs=[WHOLE] * 3,
        out_specs=[WHOLE] * 2,
        cost_estimate=pl.CostEstimate(
            flops=2 * terms.size * 2 * cells, bytes_accessed=4 * terms.size, transcendentals=0
        ),
        compiler_params=pltpu.CompilerParams(vmem_limit_bytes=16 << 20),
        name="push_home",
    )(terms, select, came)


def shards(up_check, up_inverse, translate, down_inverse, list_slot, list_class, list_count):
    classes, rows, depth = translate.shape
    cells, entries = list_slot.shape
    halves = lax.axis_size("sub") == 2

    active = lax.broadcasted_iota(jnp.int32, (entries, cells), 0) < list_count[None, :]
    code = jnp.where(active, (list_class.T << CLASS_SHIFT) + list_slot.T, -1)
    operators = jnp.transpose(translate, (1, 0, 2))
    mate_code = to_mate(code)
    near_codes = to_near(jnp.concatenate([code, mate_code], axis=0))

    operators = jnp.transpose(translate, (1, 0, 2))
    if halves:
        windows = half_windows(rows, depth, 2)
        other_check = across_sub(up_check)
        staged, mate_code = lax.optimization_barrier((up_inverse, mate_code))
        up_held, part = stage(staged, up_check, windows)
        equivalent = rest(up_held, part, other_check, windows)
        other = across_sub(equivalent)
    else:
        windows = [(0, depth, 0)]
        equivalent = lax.all_gather(
            jnp.dot(
                up_inverse, lax.all_gather(up_check, "sub", axis=0, tiled=True),
                preferred_element_type=jnp.float32,
            ).astype(jnp.bfloat16),
            "sub", axis=0, tiled=True,
        )
        other = equivalent
    near_codes, _ = lax.optimization_barrier((near_codes, equivalent))
    mate_near_code = to_mate(near_codes[:entries])
    held, product, home, away_select = prepare(
        operators, equivalent, code, mate_code, near_codes, windows
    )
    mate_near_code, product = lax.optimization_barrier((mate_near_code, product))
    terms, mate_sum, far_sum = push_away(
        held, product, other, away_select, mate_near_code, windows if halves else []
    )
    mate_came = to_mate(mate_sum)
    far_came = to_far(far_sum)
    own_sum, near_sum = push_home(terms, home, mate_came)
    near_came = to_near(near_sum)
    down_check = (
        own_sum + (far_came.astype(jnp.float32) + near_came.astype(jnp.float32))
    ).astype(jnp.bfloat16)
    if halves:
        other_down = across_sub(down_check)
        return rest(down_inverse, first(down_inverse, down_check, windows), other_down, windows)
    return jnp.dot(
        down_inverse, lax.all_gather(down_check, "sub", axis=0, tiled=True),
        preferred_element_type=jnp.float32,
    ).astype(jnp.bfloat16)


def solution(mesh):
    in_specs = (
        P("sub", "tile"),
        P("sub", None),
        P(None, "sub", None),
        P("sub", None),
        P("tile", None),
        P("tile", None),
        P("tile"),
    )
    out_specs = P("sub", "tile")
    return jax.shard_map(shards, mesh=mesh, in_specs=in_specs, out_specs=out_specs, check_vma=False)
```

```python
import functools

import jax
import jax.numpy as jnp
from jax import lax
from jax.experimental import pallas as pl
from jax.experimental.pallas import tpu as pltpu
from jax.sharding import PartitionSpec as P

REACH = 2
CLASS_SHIFT = 10
CHUNK = 112
LANES = 128
WHOLE = pl.BlockSpec(memory_space=pltpu.VMEM)


def across_sub(shard):
    return lax.ppermute(shard, "sub", [(0, 1), (1, 0)])


def to_mate(value):
    count = lax.axis_size("tile")
    pairs = [(t, t ^ 1) for t in range(count) if t ^ 1 < count]
    return lax.ppermute(value, "tile", pairs)


def to_near(value):
    count = lax.axis_size("tile")
    pairs = [(t, t + 2 * (t % 2) - 1) for t in range(count)]
    return lax.ppermute(value, "tile", [(a, b) for a, b in pairs if 0 <= b < count])


def to_far(value):
    count = lax.axis_size("tile")
    pairs = [(t, t + 4 * (t % 2) - 2) for t in range(count)]
    return lax.ppermute(value, "tile", [(a, b) for a, b in pairs if 0 <= b < count])


def away():
    return 2 * lax.rem(lax.axis_index("tile"), 2) - 1


def half_windows(shard_rows, depth, count):
    windows = []
    for index in range(count):
        low, high = index * shard_rows, (index + 1) * shard_rows
        start = low // LANES * LANES
        stop = min(pl.cdiv(high, LANES) * LANES, depth)
        windows.append((start, stop, low - start))
    return windows


def chunks(rows, size):
    return [(start, min(size, rows - start)) for start in range(0, rows, size)]


def pad_into(padded, offset, *refs):
    padded[...] = jnp.zeros(padded.shape, padded.dtype)
    for i, ref in enumerate(refs):
        rows, cells = ref.shape
        padded[offset : offset + rows, i * cells : (i + 1) * cells] = ref[...].astype(padded.dtype)


def stage_kernel(windows, matrix_ref, own_ref, held_ref, part_ref, own_held, padded, sems):
    copies = [
        pltpu.make_async_copy(own_ref, own_held, sems.at[0]),
        pltpu.make_async_copy(matrix_ref, held_ref, sems.at[1]),
    ]
    for copy in copies:
        copy.start()
    for copy in copies:
        copy.wait()
    first_kernel(windows, held_ref, own_held, part_ref, padded)


def stage(matrix, own, windows):
    rows, depth = matrix.shape
    cells = own.shape[1]
    span = max(high - low for low, high, _ in windows)
    return pl.pallas_call(
        functools.partial(stage_kernel, windows),
        out_shape=[
            jax.ShapeDtypeStruct(matrix.shape, matrix.dtype),
            jax.ShapeDtypeStruct((rows, cells), jnp.float32),
        ],
        in_specs=[pl.BlockSpec(memory_space=pltpu.HBM)] * 2,
        out_specs=[WHOLE] * 2,
        scratch_shapes=[
            pltpu.VMEM(own.shape, own.dtype),
            pltpu.VMEM((span, cells), jnp.float32),
            pltpu.SemaphoreType.DMA((2,)),
        ],
        cost_estimate=pl.CostEstimate(
            flops=2 * rows * depth * cells, bytes_accessed=4 * matrix.size, transcendentals=0
        ),
        compiler_params=pltpu.CompilerParams(vmem_limit_bytes=24 << 20),
        name="stage",
    )(*[pltpu.with_memory_space_constraint(x, pltpu.HBM) for x in (matrix, own)])


def first_kernel(windows, matrix_ref, own_ref, out_ref, padded):
    for index, (low, high, offset) in enumerate(windows):
        def run(low=low, high=high, offset=offset):
            pad_into(padded, offset, own_ref)
            out_ref[...] = jnp.dot(
                matrix_ref[:, low:high], padded[: high - low, :].astype(jnp.bfloat16),
                preferred_element_type=jnp.float32,
            )
        pl.when(lax.axis_index("sub") == index)(run)


def first(matrix, own, windows):
    rows, depth = matrix.shape
    cells = own.shape[1]
    span = max(high - low for low, high, _ in windows)
    return pl.pallas_call(
        functools.partial(first_kernel, windows),
        out_shape=jax.ShapeDtypeStruct((rows, cells), jnp.float32),
        in_specs=[WHOLE] * 2,
        out_specs=WHOLE,
        scratch_shapes=[pltpu.VMEM((span, cells), jnp.float32)],
        cost_estimate=pl.CostEstimate(
            flops=2 * rows * depth * cells, bytes_accessed=4 * rows * depth, transcendentals=0
        ),
        compiler_params=pltpu.CompilerParams(vmem_limit_bytes=16 << 20),
        name="first",
    )(matrix, own)


def rest_kernel(windows, matrix_ref, part_ref, other_ref, out_ref, padded):
    for index, (low, high, offset) in enumerate(windows):
        def run(low=low, high=high, offset=offset):
            pad_into(padded, offset, other_ref)
            out_ref[...] = (
                part_ref[...]
                + jnp.dot(
                    matrix_ref[:, low:high], padded[: high - low, :].astype(jnp.bfloat16),
                    preferred_element_type=jnp.float32,
                )
            ).astype(jnp.bfloat16)
        pl.when(lax.axis_index("sub") != index)(run)


def rest(matrix, part, other, windows):
    rows, depth = matrix.shape
    cells = other.shape[1]
    span = max(high - low for low, high, _ in windows)
    return pl.pallas_call(
        functools.partial(rest_kernel, windows),
        out_shape=jax.ShapeDtypeStruct((rows, cells), jnp.bfloat16),
        in_specs=[WHOLE] * 3,
        out_specs=WHOLE,
        scratch_shapes=[pltpu.VMEM((span, cells), jnp.float32)],
        cost_estimate=pl.CostEstimate(
            flops=2 * rows * span * cells, bytes_accessed=2 * rows * span, transcendentals=0
        ),
        compiler_params=pltpu.CompilerParams(vmem_limit_bytes=16 << 20),
        name="rest",
    )(matrix, part, other)


def build_select(code, base, out_ref, column, classes):
    entries, cells = code.shape
    slots = (code & ((1 << CLASS_SHIFT) - 1)) - base
    kinds = code >> CLASS_SHIFT
    band = 32
    for low in range(0, cells, band):
        source = lax.broadcasted_iota(jnp.int32, (band, cells), 0) + low
        totals = [jnp.zeros((band, cells), jnp.bfloat16)] * classes
        for entry in range(entries):
            hit = jnp.where(slots[entry : entry + 1, :] == source, 1.0, 0.0).astype(jnp.bfloat16)
            for k in range(classes):
                used = jnp.where(kinds[entry : entry + 1, :] == k, 1.0, 0.0).astype(jnp.bfloat16)
                totals[k] = totals[k] + hit * used
        for k in range(classes):
            row = k * cells + low
            out_ref[row : row + band, column : column + cells] = totals[k]


def prepare_kernel(
    windows, translate_ref, own_ref, code_ref, mate_ref, near_ref,
    held_ref, product_ref, home_ref, away_ref, padded, sems,
):
    rows, classes, _ = translate_ref.shape
    entries, cells = code_ref.shape
    depth = translate_ref.shape[2]
    parts = chunks(rows, CHUNK)

    def load(low, high, semaphore):
        copies = []
        for i, (start, size) in enumerate(parts):
            where = (pl.ds(start, size), slice(None), pl.ds(low, high - low))
            copies.append(
                pltpu.make_async_copy(
                    translate_ref.at[where], held_ref.at[where], sems.at[semaphore, i]
                )
            )
        return copies

    def on_window(run):
        for index, window in enumerate(windows):
            if len(windows) == 1:
                run(*window)
            else:
                pl.when(lax.axis_index("sub") == index)(functools.partial(run, *window))

    def begin(low, high, offset):
        for copy in load(low, high, 0):
            copy.start()

    on_window(begin)

    step = away()
    build_select(code_ref[...], REACH * cells, home_ref, 0, classes)
    build_select(near_ref[:entries, :], (REACH - step) * cells, home_ref, cells, classes)
    build_select(mate_ref[...], (REACH + step) * cells, away_ref, 0, classes)
    build_select(near_ref[entries:, :], (REACH - 2 * step) * cells, away_ref, cells, classes)

    def run(low, high, offset):
        first_copies = load(low, high, 0)
        other_copies = []
        for left, right in ((0, low), (high, depth)):
            if left < right:
                other_copies += load(left, right, 1)
        pad_into(padded, offset, own_ref)
        equivalent = padded[: high - low, :].astype(jnp.bfloat16)
        for copy in first_copies:
            copy.wait()
        for copy in other_copies:
            copy.start()
        for start, size in parts:
            matrix = held_ref[start : start + size, :, low:high]
            product_ref[start * classes : (start + size) * classes, :] = jnp.dot(
                matrix.reshape(size * classes, high - low), equivalent,
                preferred_element_type=jnp.float32,
            )
        for copy in other_copies:
            copy.wait()

    on_window(run)


def prepare(operators, own, code, mate_code, near_codes, windows):
    rows, classes, depth = operators.shape
    cells = code.shape[1]
    span = max(high - low for low, high, _ in windows)
    select = jax.ShapeDtypeStruct((classes * cells, 2 * cells), jnp.bfloat16)
    return pl.pallas_call(
        functools.partial(prepare_kernel, windows),
        out_shape=[
            jax.ShapeDtypeStruct((rows, classes, depth), jnp.bfloat16),
            jax.ShapeDtypeStruct((rows * classes, cells), jnp.float32),
            select,
            select,
        ],
        in_specs=[pl.BlockSpec(memory_space=pltpu.HBM)] + [WHOLE] * 4,
        out_specs=[WHOLE] * 4,
        scratch_shapes=[
            pltpu.VMEM((span, cells), jnp.float32),
            pltpu.SemaphoreType.DMA((2, len(chunks(rows, CHUNK)))),
        ],
        cost_estimate=pl.CostEstimate(flops=1 << 32, bytes_accessed=0, transcendentals=0),
        compiler_params=pltpu.CompilerParams(vmem_limit_bytes=32 << 20),
        name="prepare",
    )(
        pltpu.with_memory_space_constraint(operators, pltpu.HBM),
        own, code, mate_code, near_codes,
    )


def push_away_kernel(
    windows, held_ref, product_ref, other_ref, away_ref, code_ref,
    terms_ref, mate_ref, far_ref, padded, product, select,
):
    rows, classes, _ = held_ref.shape
    cells = far_ref.shape[1]
    build_select(code_ref[...], (REACH + 2 * away()) * cells, select, 0, classes)

    def part_classes(source, start, size):
        for k in range(classes):
            term = source[pl.ds(start * classes + k, size, stride=classes), :]
            terms_ref[start : start + size, k * cells : (k + 1) * cells] = term.astype(jnp.bfloat16)

    for index, (low, high, offset) in enumerate(windows):
        def run(low=low, high=high, offset=offset):
            pad_into(padded, offset, other_ref)
            right = padded[: high - low, :].astype(jnp.bfloat16)
            for start, size in chunks(rows, CHUNK):
                left = held_ref[start : start + size, :, low:high]
                part = slice(start * classes, (start + size) * classes)
                product[part, :] = product_ref[part, :] + jnp.dot(
                    left.reshape(size * classes, high - low), right,
                    preferred_element_type=jnp.float32,
                )
                part_classes(product, start, size)
        pl.when(lax.axis_index("sub") != index)(run)

    if not windows:
        for start, size in chunks(rows, CHUNK):
            part_classes(product_ref, start, size)

    terms = terms_ref[...]
    total = jnp.dot(terms, away_ref[...], preferred_element_type=jnp.float32)
    mate_ref[:, :cells] = total[:, :cells].astype(jnp.bfloat16)
    far_ref[...] = total[:, cells:].astype(jnp.bfloat16)
    mate_ref[:, cells:] = jnp.dot(
        terms, select[...], preferred_element_type=jnp.float32
    ).astype(jnp.bfloat16)


def push_away(held, product, other, away_select, code, windows):
    rows, classes, depth = held.shape
    cells = other.shape[1]
    span = max([high - low for low, high, _ in windows], default=LANES)
    return pl.pallas_call(
        functools.partial(push_away_kernel, windows),
        out_shape=[
            jax.ShapeDtypeStruct((rows, classes * cells), jnp.bfloat16),
            jax.ShapeDtypeStruct((rows, 2 * cells), jnp.bfloat16),
            jax.ShapeDtypeStruct((rows, cells), jnp.bfloat16),
        ],
        in_specs=[WHOLE] * 5,
        out_specs=[WHOLE] * 3,
        scratch_shapes=[
            pltpu.VMEM((span, cells), jnp.float32),
            pltpu.VMEM((rows * classes, cells), jnp.float32),
            pltpu.VMEM((classes * cells, cells), jnp.bfloat16),
        ],
        cost_estimate=pl.CostEstimate(
            flops=2 * rows * classes * cells * (span + 3 * cells),
            bytes_accessed=2 * rows * classes * depth,
            transcendentals=0,
        ),
        compiler_params=pltpu.CompilerParams(vmem_limit_bytes=32 << 20),
        name="push_away",
    )(held, product, other, away_select, code)


def push_home_kernel(terms_ref, select_ref, came_ref, own_ref, near_ref):
    cells = near_ref.shape[1]
    total = jnp.dot(terms_ref[...], select_ref[...], preferred_element_type=jnp.float32)
    total = total + came_ref[...].astype(jnp.float32)
    own_ref[...] = total[:, :cells]
    near_ref[...] = total[:, cells:].astype(jnp.bfloat16)


def push_home(terms, select, came):
    rows = terms.shape[0]
    cells = select.shape[1] // 2
    return pl.pallas_call(
        push_home_kernel,
        out_shape=[
            jax.ShapeDtypeStruct((rows, cells), jnp.float32),
            jax.ShapeDtypeStruct((rows, cells), jnp.bfloat16),
        ],
        in_specs=[WHOLE] * 3,
        out_specs=[WHOLE] * 2,
        cost_estimate=pl.CostEstimate(
            flops=2 * terms.size * 2 * cells, bytes_accessed=4 * terms.size, transcendentals=0
        ),
        compiler_params=pltpu.CompilerParams(vmem_limit_bytes=16 << 20),
        name="push_home",
    )(terms, select, came)


def shards(up_check, up_inverse, translate, down_inverse, list_slot, list_class, list_count):
    classes, rows, depth = translate.shape
    cells, entries = list_slot.shape
    halves = lax.axis_size("sub") == 2

    active = lax.broadcasted_iota(jnp.int32, (entries, cells), 0) < list_count[None, :]
    code = jnp.where(active, (list_class.T << CLASS_SHIFT) + list_slot.T, -1)
    operators = jnp.transpose(translate, (1, 0, 2))
    mate_code = to_mate(code)
    near_codes = to_near(jnp.concatenate([code, mate_code], axis=0))

    operators = jnp.transpose(translate, (1, 0, 2))
    if halves:
        windows = half_windows(rows, depth, 2)
        other_check = across_sub(up_check)
        staged, mate_code = lax.optimization_barrier((up_inverse, mate_code))
        up_held, part = stage(staged, up_check, windows)
        equivalent = rest(up_held, part, other_check, windows)
        other = across_sub(equivalent)
    else:
        windows = [(0, depth, 0)]
        equivalent = lax.all_gather(
            jnp.dot(
                up_inverse, lax.all_gather(up_check, "sub", axis=0, tiled=True),
                preferred_element_type=jnp.float32,
            ).astype(jnp.bfloat16),
            "sub", axis=0, tiled=True,
        )
        other = equivalent
    near_codes, _ = lax.optimization_barrier((near_codes, equivalent))
    mate_near_code = to_mate(near_codes[:entries])
    held, product, home, away_select = prepare(
        operators, equivalent, code, mate_code, near_codes, windows
    )
    mate_near_code, product = lax.optimization_barrier((mate_near_code, product))
    terms, mate_sum, far_sum = push_away(
        held, product, other, away_select, mate_near_code, windows if halves else []
    )
    mate_came = to_mate(mate_sum)
    far_came = to_far(far_sum)
    own_sum, near_sum = push_home(terms, home, mate_came)
    near_came = to_near(near_sum)
    down_check = (
        own_sum + (far_came.astype(jnp.float32) + near_came.astype(jnp.float32))
    ).astype(jnp.bfloat16)
    if halves:
        other_down = across_sub(down_check)
        return rest(down_inverse, first(down_inverse, down_check, windows), other_down, windows)
    return jnp.dot(
        down_inverse, lax.all_gather(down_check, "sub", axis=0, tiled=True),
        preferred_element_type=jnp.float32,
    ).astype(jnp.bfloat16)


def solution(mesh):
    in_specs = (
        P("sub", "tile"),
        P("sub", None),
        P(None, "sub", None),
        P("sub", None),
        P("tile", None),
        P("tile", None),
        P("tile"),
    )
    out_specs = P("sub", "tile")
    return jax.shard_map(shards, mesh=mesh, in_specs=in_specs, out_specs=out_specs, check_vma=False)
```

```python
import functools

import jax
import jax.numpy as jnp
from jax import lax
from jax.experimental import pallas as pl
from jax.experimental.pallas import tpu as pltpu
from jax.sharding import PartitionSpec as P

REACH = 2
CLASS_SHIFT = 10
CHUNK = 112
LANES = 128
WHOLE = pl.BlockSpec(memory_space=pltpu.VMEM)


def across_sub(shard):
    return lax.ppermute(shard, "sub", [(0, 1), (1, 0)])


def to_mate(value):
    count = lax.axis_size("tile")
    pairs = [(t, t ^ 1) for t in range(count) if t ^ 1 < count]
    return lax.ppermute(value, "tile", pairs)


def to_near(value):
    count = lax.axis_size("tile")
    pairs = [(t, t + 2 * (t % 2) - 1) for t in range(count)]
    return lax.ppermute(value, "tile", [(a, b) for a, b in pairs if 0 <= b < count])


def to_far(value):
    count = lax.axis_size("tile")
    pairs = [(t, t + 4 * (t % 2) - 2) for t in range(count)]
    return lax.ppermute(value, "tile", [(a, b) for a, b in pairs if 0 <= b < count])


def away():
    return 2 * lax.rem(lax.axis_index("tile"), 2) - 1


def half_windows(shard_rows, depth, count):
    windows = []
    for index in range(count):
        low, high = index * shard_rows, (index + 1) * shard_rows
        start = low // LANES * LANES
        stop = min(pl.cdiv(high, LANES) * LANES, depth)
        windows.append((start, stop, low - start))
    return windows


def chunks(rows, size):
    return [(start, min(size, rows - start)) for start in range(0, rows, size)]


def pad_into(padded, offset, *refs):
    padded[...] = jnp.zeros(padded.shape, padded.dtype)
    for i, ref in enumerate(refs):
        rows, cells = ref.shape
        padded[offset : offset + rows, i * cells : (i + 1) * cells] = ref[...].astype(padded.dtype)


def first_kernel(windows, matrix_ref, own_ref, out_ref, padded):
    for index, (low, high, offset) in enumerate(windows):
        def run(low=low, high=high, offset=offset):
            pad_into(padded, offset, own_ref)
            out_ref[...] = jnp.dot(
                matrix_ref[:, low:high], padded[: high - low, :].astype(jnp.bfloat16),
                preferred_element_type=jnp.float32,
            )
        pl.when(lax.axis_index("sub") == index)(run)


def first(matrix, own, windows):
    rows, depth = matrix.shape
    cells = own.shape[1]
    span = max(high - low for low, high, _ in windows)
    return pl.pallas_call(
        functools.partial(first_kernel, windows),
        out_shape=jax.ShapeDtypeStruct((rows, cells), jnp.float32),
        in_specs=[WHOLE] * 2,
        out_specs=WHOLE,
        scratch_shapes=[pltpu.VMEM((span, cells), jnp.float32)],
        cost_estimate=pl.CostEstimate(
            flops=2 * rows * depth * cells, bytes_accessed=4 * rows * depth, transcendentals=0
        ),
        compiler_params=pltpu.CompilerParams(vmem_limit_bytes=16 << 20),
        name="first",
    )(matrix, own)


def rest_kernel(windows, matrix_ref, part_ref, other_ref, out_ref, padded):
    for index, (low, high, offset) in enumerate(windows):
        def run(low=low, high=high, offset=offset):
            pad_into(padded, offset, other_ref)
            out_ref[...] = (
                part_ref[...]
                + jnp.dot(
                    matrix_ref[:, low:high], padded[: high - low, :].astype(jnp.bfloat16),
                    preferred_element_type=jnp.float32,
                )
            ).astype(jnp.bfloat16)
        pl.when(lax.axis_index("sub") != index)(run)


def rest(matrix, part, other, windows):
    rows, depth = matrix.shape
    cells = other.shape[1]
    span = max(high - low for low, high, _ in windows)
    return pl.pallas_call(
        functools.partial(rest_kernel, windows),
        out_shape=jax.ShapeDtypeStruct((rows, cells), jnp.bfloat16),
        in_specs=[WHOLE] * 3,
        out_specs=WHOLE,
        scratch_shapes=[pltpu.VMEM((span, cells), jnp.float32)],
        cost_estimate=pl.CostEstimate(
            flops=2 * rows * span * cells, bytes_accessed=2 * rows * span, transcendentals=0
        ),
        compiler_params=pltpu.CompilerParams(vmem_limit_bytes=16 << 20),
        name="rest",
    )(matrix, part, other)


def build_select(code, base, out_ref, column, classes):
    entries, cells = code.shape
    slots = (code & ((1 << CLASS_SHIFT) - 1)) - base
    kinds = code >> CLASS_SHIFT
    band = 32
    for low in range(0, cells, band):
        source = lax.broadcasted_iota(jnp.int32, (band, cells), 0) + low
        totals = [jnp.zeros((band, cells), jnp.bfloat16)] * classes
        for entry in range(entries):
            hit = jnp.where(slots[entry : entry + 1, :] == source, 1.0, 0.0).astype(jnp.bfloat16)
            for k in range(classes):
                used = jnp.where(kinds[entry : entry + 1, :] == k, 1.0, 0.0).astype(jnp.bfloat16)
                totals[k] = totals[k] + hit * used
        for k in range(classes):
            row = k * cells + low
            out_ref[row : row + band, column : column + cells] = totals[k]


def window_copies(translate_ref, held_ref, sems, low, high):
    copies = []
    for i, (start, size) in enumerate(chunks(translate_ref.shape[0], CHUNK)):
        where = (pl.ds(start, size), slice(None), pl.ds(low, high - low))
        copies.append(
            pltpu.make_async_copy(translate_ref.at[where], held_ref.at[where], sems.at[i])
        )
    return copies


def load_kernel(windows, translate_ref, held_ref, sems):
    for index, (low, high, _) in enumerate(windows):
        def run(low=low, high=high):
            copies = window_copies(translate_ref, held_ref, sems, low, high)
            for copy in copies:
                copy.start()
            for copy in copies:
                copy.wait()
        pl.when(lax.axis_index("sub") != index)(run)


def load(operators, windows):
    rows = operators.shape[0]
    return pl.pallas_call(
        functools.partial(load_kernel, windows),
        out_shape=jax.ShapeDtypeStruct(operators.shape, jnp.bfloat16),
        in_specs=[pl.BlockSpec(memory_space=pltpu.HBM)],
        out_specs=WHOLE,
        scratch_shapes=[pltpu.SemaphoreType.DMA((len(chunks(rows, CHUNK)),))],
        cost_estimate=pl.CostEstimate(flops=1 << 30, bytes_accessed=0, transcendentals=0),
        compiler_params=pltpu.CompilerParams(vmem_limit_bytes=16 << 20),
        name="load",
    )(pltpu.with_memory_space_constraint(operators, pltpu.HBM))


def prepare_kernel(
    windows, translate_ref, own_ref, code_ref, mate_ref, near_ref,
    product_ref, home_ref, away_ref, held, padded, sems,
):
    rows, classes, _ = translate_ref.shape
    entries, cells = code_ref.shape

    def on_window(run):
        for index, window in enumerate(windows):
            if len(windows) == 1:
                run(*window)
            else:
                pl.when(lax.axis_index("sub") == index)(functools.partial(run, *window))

    def begin(low, high, offset):
        for copy in window_copies(translate_ref, held, sems, low, high):
            copy.start()

    on_window(begin)

    step = away()
    build_select(code_ref[...], REACH * cells, home_ref, 0, classes)
    build_select(near_ref[:entries, :], (REACH - step) * cells, home_ref, cells, classes)
    build_select(mate_ref[...], (REACH + step) * cells, away_ref, 0, classes)
    build_select(near_ref[entries:, :], (REACH - 2 * step) * cells, away_ref, cells, classes)

    def run(low, high, offset):
        pad_into(padded, offset, own_ref)
        equivalent = padded[: high - low, :].astype(jnp.bfloat16)
        copies = window_copies(translate_ref, held, sems, low, high)
        for copy, (start, size) in zip(copies, chunks(rows, CHUNK)):
            copy.wait()
            matrix = held[start : start + size, :, low:high]
            product_ref[start * classes : (start + size) * classes, :] = jnp.dot(
                matrix.reshape(size * classes, high - low), equivalent,
                preferred_element_type=jnp.float32,
            )

    on_window(run)


def prepare(operators, own, code, mate_code, near_codes, windows):
    rows, classes, depth = operators.shape
    cells = code.shape[1]
    span = max(high - low for low, high, _ in windows)
    select = jax.ShapeDtypeStruct((classes * cells, 2 * cells), jnp.bfloat16)
    return pl.pallas_call(
        functools.partial(prepare_kernel, windows),
        out_shape=[
            jax.ShapeDtypeStruct((rows * classes, cells), jnp.float32),
            select,
            select,
        ],
        in_specs=[pl.BlockSpec(memory_space=pltpu.HBM)] + [WHOLE] * 4,
        out_specs=[WHOLE] * 3,
        scratch_shapes=[
            pltpu.VMEM(operators.shape, jnp.bfloat16),
            pltpu.VMEM((span, cells), jnp.float32),
            pltpu.SemaphoreType.DMA((len(chunks(rows, CHUNK)),)),
        ],
        cost_estimate=pl.CostEstimate(flops=1 << 32, bytes_accessed=0, transcendentals=0),
        compiler_params=pltpu.CompilerParams(vmem_limit_bytes=32 << 20),
        name="prepare",
    )(
        pltpu.with_memory_space_constraint(operators, pltpu.HBM),
        own, code, mate_code, near_codes,
    )


def push_away_kernel(
    windows, held_ref, product_ref, other_ref, away_ref, code_ref,
    terms_ref, mate_ref, far_ref, padded, product, select,
):
    rows, classes, _ = held_ref.shape
    cells = far_ref.shape[1]
    build_select(code_ref[...], (REACH + 2 * away()) * cells, select, 0, classes)

    def part_classes(source, start, size):
        for k in range(classes):
            term = source[pl.ds(start * classes + k, size, stride=classes), :]
            terms_ref[start : start + size, k * cells : (k + 1) * cells] = term.astype(jnp.bfloat16)

    for index, (low, high, offset) in enumerate(windows):
        def run(low=low, high=high, offset=offset):
            pad_into(padded, offset, other_ref)
            right = padded[: high - low, :].astype(jnp.bfloat16)
            for start, size in chunks(rows, CHUNK):
                left = held_ref[start : start + size, :, low:high]
                part = slice(start * classes, (start + size) * classes)
                product[part, :] = product_ref[part, :] + jnp.dot(
                    left.reshape(size * classes, high - low), right,
                    preferred_element_type=jnp.float32,
                )
                part_classes(product, start, size)
        pl.when(lax.axis_index("sub") != index)(run)

    if not windows:
        for start, size in chunks(rows, CHUNK):
            part_classes(product_ref, start, size)

    terms = terms_ref[...]
    total = jnp.dot(terms, away_ref[...], preferred_element_type=jnp.float32)
    mate_ref[:, :cells] = total[:, :cells].astype(jnp.bfloat16)
    far_ref[...] = total[:, cells:].astype(jnp.bfloat16)
    mate_ref[:, cells:] = jnp.dot(
        terms, select[...], preferred_element_type=jnp.float32
    ).astype(jnp.bfloat16)


def push_away(held, product, other, away_select, code, windows):
    rows, classes, depth = held.shape
    cells = other.shape[1]
    span = max([high - low for low, high, _ in windows], default=LANES)
    return pl.pallas_call(
        functools.partial(push_away_kernel, windows),
        out_shape=[
            jax.ShapeDtypeStruct((rows, classes * cells), jnp.bfloat16),
            jax.ShapeDtypeStruct((rows, 2 * cells), jnp.bfloat16),
            jax.ShapeDtypeStruct((rows, cells), jnp.bfloat16),
        ],
        in_specs=[WHOLE] * 5,
        out_specs=[WHOLE] * 3,
        scratch_shapes=[
            pltpu.VMEM((span, cells), jnp.float32),
            pltpu.VMEM((rows * classes, cells), jnp.float32),
            pltpu.VMEM((classes * cells, cells), jnp.bfloat16),
        ],
        cost_estimate=pl.CostEstimate(
            flops=2 * rows * classes * cells * (span + 3 * cells),
            bytes_accessed=2 * rows * classes * depth,
            transcendentals=0,
        ),
        compiler_params=pltpu.CompilerParams(vmem_limit_bytes=32 << 20),
        name="push_away",
    )(held, product, other, away_select, code)


def push_home_kernel(terms_ref, select_ref, came_ref, own_ref, near_ref):
    cells = near_ref.shape[1]
    total = jnp.dot(terms_ref[...], select_ref[...], preferred_element_type=jnp.float32)
    total = total + came_ref[...].astype(jnp.float32)
    own_ref[...] = total[:, :cells]
    near_ref[...] = total[:, cells:].astype(jnp.bfloat16)


def push_home(terms, select, came):
    rows = terms.shape[0]
    cells = select.shape[1] // 2
    return pl.pallas_call(
        push_home_kernel,
        out_shape=[
            jax.ShapeDtypeStruct((rows, cells), jnp.float32),
            jax.ShapeDtypeStruct((rows, cells), jnp.bfloat16),
        ],
        in_specs=[WHOLE] * 3,
        out_specs=[WHOLE] * 2,
        cost_estimate=pl.CostEstimate(
            flops=2 * terms.size * 2 * cells, bytes_accessed=4 * terms.size, transcendentals=0
        ),
        compiler_params=pltpu.CompilerParams(vmem_limit_bytes=16 << 20),
        name="push_home",
    )(terms, select, came)


def shards(up_check, up_inverse, translate, down_inverse, list_slot, list_class, list_count):
    classes, rows, depth = translate.shape
    cells, entries = list_slot.shape
    halves = lax.axis_size("sub") == 2

    active = lax.broadcasted_iota(jnp.int32, (entries, cells), 0) < list_count[None, :]
    code = jnp.where(active, (list_class.T << CLASS_SHIFT) + list_slot.T, -1)
    operators = jnp.transpose(translate, (1, 0, 2))
    mate_code = to_mate(code)
    near_codes = to_near(jnp.concatenate([code, mate_code], axis=0))

    operators = jnp.transpose(translate, (1, 0, 2))
    if halves:
        windows = half_windows(rows, depth, 2)
        other_check = across_sub(up_check)
        check = jnp.where(
            lax.axis_index("sub") == 0,
            jnp.concatenate([up_check, other_check], axis=0),
            jnp.concatenate([other_check, up_check], axis=0),
        )
        check = lax.optimization_barrier((check, mate_code))[0]
    else:
        windows = [(0, depth, 0)]
        check = lax.all_gather(up_check, "sub", axis=0, tiled=True)
    equivalent = jnp.dot(up_inverse, check, preferred_element_type=jnp.float32)
    equivalent = equivalent.astype(jnp.bfloat16)
    if halves:
        other = across_sub(equivalent)
        held = load(lax.optimization_barrier((operators, equivalent))[0], windows)
    else:
        equivalent = lax.all_gather(equivalent, "sub", axis=0, tiled=True)
        other, held = equivalent, operators
    near_codes, _, _ = lax.optimization_barrier((near_codes, equivalent, held))
    mate_near_code = to_mate(near_codes[:entries])
    product, home, away_select = prepare(
        operators, equivalent, code, mate_code, near_codes, windows
    )
    mate_near_code, product = lax.optimization_barrier((mate_near_code, product))
    terms, mate_sum, far_sum = push_away(
        held, product, other, away_select, mate_near_code, windows if halves else []
    )
    mate_came = to_mate(mate_sum)
    far_came = to_far(far_sum)
    own_sum, near_sum = push_home(terms, home, mate_came)
    near_came = to_near(near_sum)
    down_check = (
        own_sum + (far_came.astype(jnp.float32) + near_came.astype(jnp.float32))
    ).astype(jnp.bfloat16)
    if halves:
        other_down = across_sub(down_check)
        return rest(down_inverse, first(down_inverse, down_check, windows), other_down, windows)
    return jnp.dot(
        down_inverse, lax.all_gather(down_check, "sub", axis=0, tiled=True),
        preferred_element_type=jnp.float32,
    ).astype(jnp.bfloat16)


def solution(mesh):
    in_specs = (
        P("sub", "tile"),
        P("sub", None),
        P(None, "sub", None),
        P("sub", None),
        P("tile", None),
        P("tile", None),
        P("tile"),
    )
    out_specs = P("sub", "tile")
    return jax.shard_map(shards, mesh=mesh, in_specs=in_specs, out_specs=out_specs, check_vma=False)
```

```python
import functools

import jax
import jax.numpy as jnp
from jax import lax
from jax.experimental import pallas as pl
from jax.experimental.pallas import tpu as pltpu
from jax.sharding import PartitionSpec as P

REACH = 2
CLASS_SHIFT = 10
CHUNK = 112
LANES = 128
WHOLE = pl.BlockSpec(memory_space=pltpu.VMEM)


def across_sub(shard):
    return lax.ppermute(shard, "sub", [(0, 1), (1, 0)])


def to_mate(value):
    count = lax.axis_size("tile")
    pairs = [(t, t ^ 1) for t in range(count) if t ^ 1 < count]
    return lax.ppermute(value, "tile", pairs)


def to_near(value):
    count = lax.axis_size("tile")
    pairs = [(t, t + 2 * (t % 2) - 1) for t in range(count)]
    return lax.ppermute(value, "tile", [(a, b) for a, b in pairs if 0 <= b < count])


def to_far(value):
    count = lax.axis_size("tile")
    pairs = [(t, t + 4 * (t % 2) - 2) for t in range(count)]
    return lax.ppermute(value, "tile", [(a, b) for a, b in pairs if 0 <= b < count])


def away():
    return 2 * lax.rem(lax.axis_index("tile"), 2) - 1


def half_windows(shard_rows, depth, count):
    windows = []
    for index in range(count):
        low, high = index * shard_rows, (index + 1) * shard_rows
        start = low // LANES * LANES
        stop = min(pl.cdiv(high, LANES) * LANES, depth)
        windows.append((start, stop, low - start))
    return windows


def chunks(rows, size):
    return [(start, min(size, rows - start)) for start in range(0, rows, size)]


def pad_into(padded, offset, *refs):
    padded[...] = jnp.zeros(padded.shape, padded.dtype)
    for i, ref in enumerate(refs):
        rows, cells = ref.shape
        padded[offset : offset + rows, i * cells : (i + 1) * cells] = ref[...].astype(padded.dtype)


def code_kernel(slot_ref, class_ref, count_ref, code_ref, slots, classes, counts, sems):
    copies = [
        pltpu.make_async_copy(source, target, sems.at[i])
        for i, (source, target) in enumerate(
            ((slot_ref, slots), (class_ref, classes), (count_ref, counts))
        )
    ]
    for copy in copies:
        copy.start()
    for copy in copies:
        copy.wait()
    entry = lax.broadcasted_iota(jnp.int32, code_ref.shape, 0)
    code_ref[...] = jnp.where(
        entry < counts[...], (classes[...] << CLASS_SHIFT) + slots[...], -1
    )


def coded(list_slot, list_class, list_count):
    operands = (list_slot.T, list_class.T, list_count[None, :])
    return pl.pallas_call(
        code_kernel,
        out_shape=jax.ShapeDtypeStruct(operands[0].shape, jnp.int32),
        in_specs=[pl.BlockSpec(memory_space=pltpu.HBM)] * 3,
        out_specs=WHOLE,
        scratch_shapes=[pltpu.VMEM(x.shape, x.dtype) for x in operands]
        + [pltpu.SemaphoreType.DMA((3,))],
        cost_estimate=pl.CostEstimate(flops=1 << 33, bytes_accessed=0, transcendentals=0),
        compiler_params=pltpu.CompilerParams(vmem_limit_bytes=4 << 20),
        name="code",
    )(*[pltpu.with_memory_space_constraint(x, pltpu.HBM) for x in operands])


def joined_kernel(matrix_ref, own_ref, other_ref, out_ref, joined):
    rows = own_ref.shape[0]
    halves = [slice(0, rows), slice(rows, 2 * rows)]
    for index in range(2):
        def place(index=index):
            joined[halves[index], :] = own_ref[...].astype(jnp.float32)
            joined[halves[1 - index], :] = other_ref[...].astype(jnp.float32)
        pl.when(lax.axis_index("sub") == index)(place)
    out_ref[...] = jnp.dot(
        matrix_ref[...], joined[...].astype(jnp.bfloat16), preferred_element_type=jnp.float32
    ).astype(jnp.bfloat16)


def joined_product(matrix, own, other):
    rows, depth = matrix.shape
    cells = own.shape[1]
    return pl.pallas_call(
        joined_kernel,
        out_shape=jax.ShapeDtypeStruct((rows, cells), jnp.bfloat16),
        in_specs=[WHOLE] * 3,
        out_specs=WHOLE,
        scratch_shapes=[pltpu.VMEM((depth, cells), jnp.float32)],
        cost_estimate=pl.CostEstimate(
            flops=2 * rows * depth * cells, bytes_accessed=2 * rows * depth, transcendentals=0
        ),
        compiler_params=pltpu.CompilerParams(vmem_limit_bytes=8 << 20),
        name="joined",
    )(matrix, own, other)


def first_kernel(windows, matrix_ref, own_ref, out_ref, padded):
    for index, (low, high, offset) in enumerate(windows):
        def run(low=low, high=high, offset=offset):
            pad_into(padded, offset, own_ref)
            out_ref[...] = jnp.dot(
                matrix_ref[:, low:high], padded[: high - low, :].astype(jnp.bfloat16),
                preferred_element_type=jnp.float32,
            )
        pl.when(lax.axis_index("sub") == index)(run)


def first(matrix, own, windows):
    rows, depth = matrix.shape
    cells = own.shape[1]
    span = max(high - low for low, high, _ in windows)
    return pl.pallas_call(
        functools.partial(first_kernel, windows),
        out_shape=jax.ShapeDtypeStruct((rows, cells), jnp.float32),
        in_specs=[WHOLE] * 2,
        out_specs=WHOLE,
        scratch_shapes=[pltpu.VMEM((span, cells), jnp.float32)],
        cost_estimate=pl.CostEstimate(
            flops=2 * rows * depth * cells, bytes_accessed=4 * rows * depth, transcendentals=0
        ),
        compiler_params=pltpu.CompilerParams(vmem_limit_bytes=16 << 20),
        name="first",
    )(matrix, own)


def rest_kernel(windows, matrix_ref, part_ref, other_ref, out_ref, padded):
    for index, (low, high, offset) in enumerate(windows):
        def run(low=low, high=high, offset=offset):
            pad_into(padded, offset, other_ref)
            out_ref[...] = (
                part_ref[...]
                + jnp.dot(
                    matrix_ref[:, low:high], padded[: high - low, :].astype(jnp.bfloat16),
                    preferred_element_type=jnp.float32,
                )
            ).astype(jnp.bfloat16)
        pl.when(lax.axis_index("sub") != index)(run)


def rest(matrix, part, other, windows):
    rows, depth = matrix.shape
    cells = other.shape[1]
    span = max(high - low for low, high, _ in windows)
    return pl.pallas_call(
        functools.partial(rest_kernel, windows),
        out_shape=jax.ShapeDtypeStruct((rows, cells), jnp.bfloat16),
        in_specs=[WHOLE] * 3,
        out_specs=WHOLE,
        scratch_shapes=[pltpu.VMEM((span, cells), jnp.float32)],
        cost_estimate=pl.CostEstimate(
            flops=2 * rows * span * cells, bytes_accessed=2 * rows * span, transcendentals=0
        ),
        compiler_params=pltpu.CompilerParams(vmem_limit_bytes=16 << 20),
        name="rest",
    )(matrix, part, other)


def build_select(code, base, out_ref, column, classes):
    entries, cells = code.shape
    slots = (code & ((1 << CLASS_SHIFT) - 1)) - base
    kinds = code >> CLASS_SHIFT
    band = 32
    for low in range(0, cells, band):
        source = lax.broadcasted_iota(jnp.int32, (band, cells), 0) + low
        totals = [jnp.zeros((band, cells), jnp.bfloat16)] * classes
        for entry in range(entries):
            hit = jnp.where(slots[entry : entry + 1, :] == source, 1.0, 0.0).astype(jnp.bfloat16)
            for k in range(classes):
                used = jnp.where(kinds[entry : entry + 1, :] == k, 1.0, 0.0).astype(jnp.bfloat16)
                totals[k] = totals[k] + hit * used
        for k in range(classes):
            row = k * cells + low
            out_ref[row : row + band, column : column + cells] = totals[k]


def prepare_kernel(
    windows, operators_ref, own_ref, code_ref, mate_ref,
    product_ref, home_ref, mate_select_ref, padded,
):
    rows, classes, _ = operators_ref.shape
    cells = code_ref.shape[1]
    build_select(code_ref[...], REACH * cells, home_ref, 0, classes)
    build_select(mate_ref[...], (REACH + away()) * cells, mate_select_ref, 0, classes)

    for index, (low, high, offset) in enumerate(windows):
        def run(low=low, high=high, offset=offset):
            pad_into(padded, offset, own_ref)
            right = padded[: high - low, :].astype(jnp.bfloat16)
            for start, size in chunks(rows, CHUNK):
                left = operators_ref[start : start + size, :, low:high]
                product_ref[start * classes : (start + size) * classes, :] = jnp.dot(
                    left.reshape(size * classes, high - low), right,
                    preferred_element_type=jnp.float32,
                )
        if len(windows) == 1:
            run()
        else:
            pl.when(lax.axis_index("sub") == index)(run)


def prepare(operators, own, code, mate_code, windows):
    rows, classes, depth = operators.shape
    cells = code.shape[1]
    span = max(high - low for low, high, _ in windows)
    select = jax.ShapeDtypeStruct((classes * cells, cells), jnp.bfloat16)
    return pl.pallas_call(
        functools.partial(prepare_kernel, windows),
        out_shape=[
            jax.ShapeDtypeStruct((rows * classes, cells), jnp.float32), select, select,
        ],
        in_specs=[WHOLE] * 4,
        out_specs=[WHOLE] * 3,
        scratch_shapes=[pltpu.VMEM((span, cells), jnp.float32)],
        cost_estimate=pl.CostEstimate(flops=1 << 32, bytes_accessed=0, transcendentals=0),
        compiler_params=pltpu.CompilerParams(vmem_limit_bytes=24 << 20),
        name="prepare",
    )(operators, own, code, mate_code)


def select_kernel(near_ref, near_select_ref, far_select_ref):
    entries, cells = near_ref.shape[0] // 2, near_ref.shape[1]
    classes = near_select_ref.shape[0] // cells
    step = away()
    build_select(near_ref[:entries, :], (REACH - step) * cells, near_select_ref, 0, classes)
    build_select(near_ref[entries:, :], (REACH - 2 * step) * cells, far_select_ref, 0, classes)


def selections(near_codes, classes):
    cells = near_codes.shape[1]
    select = jax.ShapeDtypeStruct((classes * cells, cells), jnp.bfloat16)
    return pl.pallas_call(
        select_kernel,
        out_shape=[select, select],
        in_specs=[WHOLE],
        out_specs=[WHOLE] * 2,
        cost_estimate=pl.CostEstimate(flops=1 << 29, bytes_accessed=0, transcendentals=0),
        compiler_params=pltpu.CompilerParams(vmem_limit_bytes=8 << 20),
        name="selections",
    )(near_codes)


def push_away_kernel(
    windows, held_ref, product_ref, other_ref, mate_select_ref, far_select_ref, code_ref,
    terms_ref, mate_ref, far_ref, padded, product, select,
):
    rows, classes, _ = held_ref.shape
    cells = far_ref.shape[1]
    build_select(code_ref[...], (REACH + 2 * away()) * cells, select, 0, classes)

    def part_classes(source, start, size):
        for k in range(classes):
            term = source[pl.ds(start * classes + k, size, stride=classes), :]
            terms_ref[start : start + size, k * cells : (k + 1) * cells] = term.astype(jnp.bfloat16)

    for index, (low, high, offset) in enumerate(windows):
        def run(low=low, high=high, offset=offset):
            pad_into(padded, offset, other_ref)
            right = padded[: high - low, :].astype(jnp.bfloat16)
            for start, size in chunks(rows, CHUNK):
                left = held_ref[start : start + size, :, low:high]
                part = slice(start * classes, (start + size) * classes)
                product[part, :] = product_ref[part, :] + jnp.dot(
                    left.reshape(size * classes, high - low), right,
                    preferred_element_type=jnp.float32,
                )
                part_classes(product, start, size)
        pl.when(lax.axis_index("sub") != index)(run)

    if not windows:
        for start, size in chunks(rows, CHUNK):
            part_classes(product_ref, start, size)

    terms = terms_ref[...]
    chosen = jnp.concatenate([mate_select_ref[...], far_select_ref[...], select[...]], axis=1)
    total = jnp.dot(terms, chosen, preferred_element_type=jnp.float32).astype(jnp.bfloat16)
    mate_ref[:, :cells] = total[:, :cells]
    far_ref[...] = total[:, cells : 2 * cells]
    mate_ref[:, cells:] = total[:, 2 * cells :]


def push_away(held, product, other, mate_select, far_select, code, windows):
    rows, classes, depth = held.shape
    cells = other.shape[1]
    span = max([high - low for low, high, _ in windows], default=LANES)
    return pl.pallas_call(
        functools.partial(push_away_kernel, windows),
        out_shape=[
            jax.ShapeDtypeStruct((rows, classes * cells), jnp.bfloat16),
            jax.ShapeDtypeStruct((rows, 2 * cells), jnp.bfloat16),
            jax.ShapeDtypeStruct((rows, cells), jnp.bfloat16),
        ],
        in_specs=[WHOLE] * 6,
        out_specs=[WHOLE] * 3,
        scratch_shapes=[
            pltpu.VMEM((span, cells), jnp.float32),
            pltpu.VMEM((rows * classes, cells), jnp.float32),
            pltpu.VMEM((classes * cells, cells), jnp.bfloat16),
        ],
        cost_estimate=pl.CostEstimate(
            flops=2 * rows * classes * cells * (span + 3 * cells),
            bytes_accessed=2 * rows * classes * depth,
            transcendentals=0,
        ),
        compiler_params=pltpu.CompilerParams(vmem_limit_bytes=32 << 20),
        name="push_away",
    )(held, product, other, mate_select, far_select, code)


def push_home_kernel(terms_ref, home_ref, near_select_ref, came_ref, own_ref, near_ref):
    cells = near_ref.shape[1]
    chosen = jnp.concatenate([home_ref[...], near_select_ref[...]], axis=1)
    total = jnp.dot(terms_ref[...], chosen, preferred_element_type=jnp.float32)
    total = total + came_ref[...].astype(jnp.float32)
    own_ref[...] = total[:, :cells]
    near_ref[...] = total[:, cells:].astype(jnp.bfloat16)


def push_home(terms, home, near_select, came):
    rows = terms.shape[0]
    cells = home.shape[1]
    return pl.pallas_call(
        push_home_kernel,
        out_shape=[
            jax.ShapeDtypeStruct((rows, cells), jnp.float32),
            jax.ShapeDtypeStruct((rows, cells), jnp.bfloat16),
        ],
        in_specs=[WHOLE] * 4,
        out_specs=[WHOLE] * 2,
        cost_estimate=pl.CostEstimate(
            flops=2 * terms.size * 2 * cells, bytes_accessed=4 * terms.size, transcendentals=0
        ),
        compiler_params=pltpu.CompilerParams(vmem_limit_bytes=16 << 20),
        name="push_home",
    )(terms, home, near_select, came)


def shards(up_check, up_inverse, translate, down_inverse, list_slot, list_class, list_count):
    classes, rows, depth = translate.shape
    cells, entries = list_slot.shape
    halves = lax.axis_size("sub") == 2

    code = coded(list_slot, list_class, list_count)
    mate_code = to_mate(code)
    near_codes = to_near(jnp.concatenate([code, mate_code], axis=0))

    operators = jnp.transpose(translate, (1, 0, 2))
    if halves:
        windows = half_windows(rows, depth, 2)
        own_check = lax.optimization_barrier((up_check, mate_code))[0]
        equivalent = joined_product(up_inverse, own_check, across_sub(up_check))
        other = across_sub(equivalent)
    else:
        windows = [(0, depth, 0)]
        equivalent = lax.all_gather(
            jnp.dot(
                up_inverse, lax.all_gather(up_check, "sub", axis=0, tiled=True),
                preferred_element_type=jnp.float32,
            ).astype(jnp.bfloat16),
            "sub", axis=0, tiled=True,
        )
        other = equivalent
    product, home, mate_select = prepare(operators, equivalent, code, mate_code, windows)
    near_codes, product = lax.optimization_barrier((near_codes, product))
    near_select, far_select = selections(near_codes, classes)
    terms, mate_sum, far_sum = push_away(
        operators, product, other, mate_select, far_select, to_mate(near_codes[:entries]),
        windows if halves else [],
    )
    mate_came = to_mate(mate_sum)
    far_came = to_far(far_sum)
    own_sum, near_sum = push_home(terms, home, near_select, mate_came)
    near_came = to_near(near_sum)
    down_check = (
        own_sum + (far_came.astype(jnp.float32) + near_came.astype(jnp.float32))
    ).astype(jnp.bfloat16)
    if halves:
        other_down = across_sub(down_check)
        return rest(down_inverse, first(down_inverse, down_check, windows), other_down, windows)
    return jnp.dot(
        down_inverse, lax.all_gather(down_check, "sub", axis=0, tiled=True),
        preferred_element_type=jnp.float32,
    ).astype(jnp.bfloat16)


def solution(mesh):
    in_specs = (
        P("sub", "tile"),
        P("sub", None),
        P(None, "sub", None),
        P("sub", None),
        P("tile", None),
        P("tile", None),
        P("tile"),
    )
    out_specs = P("sub", "tile")
    return jax.shard_map(shards, mesh=mesh, in_specs=in_specs, out_specs=out_specs, check_vma=False)
```

```python
import functools

import jax
import jax.numpy as jnp
from jax import lax
from jax.experimental import pallas as pl
from jax.experimental.pallas import tpu as pltpu
from jax.sharding import PartitionSpec as P

REACH = 2
CLASS_SHIFT = 10
CHUNK = 112
LANES = 128
WHOLE = pl.BlockSpec(memory_space=pltpu.VMEM)


def across_sub(shard):
    return lax.ppermute(shard, "sub", [(0, 1), (1, 0)])


def to_mate(value):
    count = lax.axis_size("tile")
    pairs = [(t, t ^ 1) for t in range(count) if t ^ 1 < count]
    return lax.ppermute(value, "tile", pairs)


def to_near(value):
    count = lax.axis_size("tile")
    pairs = [(t, t + 2 * (t % 2) - 1) for t in range(count)]
    return lax.ppermute(value, "tile", [(a, b) for a, b in pairs if 0 <= b < count])


def to_far(value):
    count = lax.axis_size("tile")
    pairs = [(t, t + 4 * (t % 2) - 2) for t in range(count)]
    return lax.ppermute(value, "tile", [(a, b) for a, b in pairs if 0 <= b < count])


def near_or_mates_far(value):
    count = lax.axis_size("tile")
    pairs = []
    for t in range(count):
        step = 2 * (t % 2) - 1
        for index, target in ((0, t + step), (1, t - 3 * step)):
            if 0 <= target < count:
                pairs.append((2 * t + index, 2 * target + index))
    return lax.ppermute(value, ("tile", "sub"), pairs)


def crosswise(value):
    count = lax.axis_size("tile")
    pairs = [
        (2 * t + index, 2 * (t ^ 1) + 1 - index)
        for t in range(count) for index in range(2) if t ^ 1 < count
    ]
    return lax.ppermute(value, ("tile", "sub"), pairs)


def away():
    return 2 * lax.rem(lax.axis_index("tile"), 2) - 1


def half_windows(shard_rows, depth, count):
    windows = []
    for index in range(count):
        low, high = index * shard_rows, (index + 1) * shard_rows
        start = low // LANES * LANES
        stop = min(pl.cdiv(high, LANES) * LANES, depth)
        windows.append((start, stop, low - start))
    return windows


def chunks(rows, size):
    return [(start, min(size, rows - start)) for start in range(0, rows, size)]


def pad_into(padded, offset, *refs):
    padded[...] = jnp.zeros(padded.shape, padded.dtype)
    for i, ref in enumerate(refs):
        rows, cells = ref.shape
        padded[offset : offset + rows, i * cells : (i + 1) * cells] = ref[...].astype(padded.dtype)


def code_kernel(slot_ref, class_ref, count_ref, code_ref, slots, classes, counts, sems):
    copies = [
        pltpu.make_async_copy(source, target, sems.at[i])
        for i, (source, target) in enumerate(
            ((slot_ref, slots), (class_ref, classes), (count_ref, counts))
        )
    ]
    for copy in copies:
        copy.start()
    for copy in copies:
        copy.wait()
    entry = lax.broadcasted_iota(jnp.int32, code_ref.shape, 0)
    code_ref[...] = jnp.where(
        entry < counts[...], (classes[...] << CLASS_SHIFT) + slots[...], -1
    )


def coded(list_slot, list_class, list_count):
    operands = (list_slot.T, list_class.T, list_count[None, :])
    return pl.pallas_call(
        code_kernel,
        out_shape=jax.ShapeDtypeStruct(operands[0].shape, jnp.int32),
        in_specs=[pl.BlockSpec(memory_space=pltpu.HBM)] * 3,
        out_specs=WHOLE,
        scratch_shapes=[pltpu.VMEM(x.shape, x.dtype) for x in operands]
        + [pltpu.SemaphoreType.DMA((3,))],
        cost_estimate=pl.CostEstimate(flops=1 << 33, bytes_accessed=0, transcendentals=0),
        compiler_params=pltpu.CompilerParams(vmem_limit_bytes=4 << 20),
        name="code",
    )(*[pltpu.with_memory_space_constraint(x, pltpu.HBM) for x in operands])


def joined_kernel(matrix_ref, own_ref, other_ref, out_ref, joined):
    rows = own_ref.shape[0]
    halves = [slice(0, rows), slice(rows, 2 * rows)]
    for index in range(2):
        def place(index=index):
            joined[halves[index], :] = own_ref[...].astype(jnp.float32)
            joined[halves[1 - index], :] = other_ref[...].astype(jnp.float32)
        pl.when(lax.axis_index("sub") == index)(place)
    out_ref[...] = jnp.dot(
        matrix_ref[...], joined[...].astype(jnp.bfloat16), preferred_element_type=jnp.float32
    ).astype(jnp.bfloat16)


def joined_product(matrix, own, other):
    rows, depth = matrix.shape
    cells = own.shape[1]
    return pl.pallas_call(
        joined_kernel,
        out_shape=jax.ShapeDtypeStruct((rows, cells), jnp.bfloat16),
        in_specs=[WHOLE] * 3,
        out_specs=WHOLE,
        scratch_shapes=[pltpu.VMEM((depth, cells), jnp.float32)],
        cost_estimate=pl.CostEstimate(
            flops=2 * rows * depth * cells, bytes_accessed=2 * rows * depth, transcendentals=0
        ),
        compiler_params=pltpu.CompilerParams(vmem_limit_bytes=8 << 20),
        name="joined",
    )(matrix, own, other)


def first_kernel(windows, matrix_ref, own_ref, out_ref, padded):
    for index, (low, high, offset) in enumerate(windows):
        def run(low=low, high=high, offset=offset):
            pad_into(padded, offset, own_ref)
            out_ref[...] = jnp.dot(
                matrix_ref[:, low:high], padded[: high - low, :].astype(jnp.bfloat16),
                preferred_element_type=jnp.float32,
            )
        pl.when(lax.axis_index("sub") == index)(run)


def first(matrix, own, windows):
    rows, depth = matrix.shape
    cells = own.shape[1]
    span = max(high - low for low, high, _ in windows)
    return pl.pallas_call(
        functools.partial(first_kernel, windows),
        out_shape=jax.ShapeDtypeStruct((rows, cells), jnp.float32),
        in_specs=[WHOLE] * 2,
        out_specs=WHOLE,
        scratch_shapes=[pltpu.VMEM((span, cells), jnp.float32)],
        cost_estimate=pl.CostEstimate(
            flops=2 * rows * depth * cells, bytes_accessed=4 * rows * depth, transcendentals=0
        ),
        compiler_params=pltpu.CompilerParams(vmem_limit_bytes=16 << 20),
        name="first",
    )(matrix, own)


def rest_kernel(windows, matrix_ref, part_ref, other_ref, out_ref, padded):
    for index, (low, high, offset) in enumerate(windows):
        def run(low=low, high=high, offset=offset):
            pad_into(padded, offset, other_ref)
            out_ref[...] = (
                part_ref[...]
                + jnp.dot(
                    matrix_ref[:, low:high], padded[: high - low, :].astype(jnp.bfloat16),
                    preferred_element_type=jnp.float32,
                )
            ).astype(jnp.bfloat16)
        pl.when(lax.axis_index("sub") != index)(run)


def rest(matrix, part, other, windows):
    rows, depth = matrix.shape
    cells = other.shape[1]
    span = max(high - low for low, high, _ in windows)
    return pl.pallas_call(
        functools.partial(rest_kernel, windows),
        out_shape=jax.ShapeDtypeStruct((rows, cells), jnp.bfloat16),
        in_specs=[WHOLE] * 3,
        out_specs=WHOLE,
        scratch_shapes=[pltpu.VMEM((span, cells), jnp.float32)],
        cost_estimate=pl.CostEstimate(
            flops=2 * rows * span * cells, bytes_accessed=2 * rows * span, transcendentals=0
        ),
        compiler_params=pltpu.CompilerParams(vmem_limit_bytes=16 << 20),
        name="rest",
    )(matrix, part, other)


def build_select(code, base, out_ref, column, classes):
    entries, cells = code.shape
    slots = (code & ((1 << CLASS_SHIFT) - 1)) - base
    kinds = code >> CLASS_SHIFT
    band = 32
    for low in range(0, cells, band):
        source = lax.broadcasted_iota(jnp.int32, (band, cells), 0) + low
        totals = [jnp.zeros((band, cells), jnp.bfloat16)] * classes
        for entry in range(entries):
            hit = jnp.where(slots[entry : entry + 1, :] == source, 1.0, 0.0).astype(jnp.bfloat16)
            for k in range(classes):
                used = jnp.where(kinds[entry : entry + 1, :] == k, 1.0, 0.0).astype(jnp.bfloat16)
                totals[k] = totals[k] + hit * used
        for k in range(classes):
            row = k * cells + low
            out_ref[row : row + band, column : column + cells] = totals[k]


def prepare_kernel(
    windows, part, distance, operators_ref, own_ref, code_ref, product_ref, select_ref, padded
):
    classes = operators_ref.shape[1]
    cells = own_ref.shape[1]
    build_select(code_ref[...], (REACH + distance * away()) * cells, select_ref, 0, classes)

    for index, (low, high, offset) in enumerate(windows):
        def run(low=low, high=high, offset=offset):
            pad_into(padded, offset, own_ref)
            right = padded[: high - low, :].astype(jnp.bfloat16)
            for start, size in part:
                left = operators_ref[start : start + size, :, low:high]
                row = (start - part[0][0]) * classes
                product_ref[row : row + size * classes, :] = jnp.dot(
                    left.reshape(size * classes, high - low), right,
                    preferred_element_type=jnp.float32,
                )
        if len(windows) == 1:
            run()
        else:
            pl.when(lax.axis_index("sub") == index)(run)


def prepare(operators, own, code, windows, part, distance):
    classes = operators.shape[1]
    cells = own.shape[1]
    span = max(high - low for low, high, _ in windows)
    rows = sum(size for _, size in part)
    return pl.pallas_call(
        functools.partial(prepare_kernel, windows, part, distance),
        out_shape=[
            jax.ShapeDtypeStruct((rows * classes, cells), jnp.float32),
            jax.ShapeDtypeStruct((classes * cells, cells), jnp.bfloat16),
        ],
        in_specs=[WHOLE] * 3,
        out_specs=[WHOLE] * 2,
        scratch_shapes=[pltpu.VMEM((span, cells), jnp.float32)],
        cost_estimate=pl.CostEstimate(flops=1 << 32, bytes_accessed=0, transcendentals=0),
        compiler_params=pltpu.CompilerParams(vmem_limit_bytes=24 << 20),
        name="prepare",
    )(operators, own, code)


def select_kernel(
    halves, got_ref, crossed_ref, swapped_ref, near_select_ref, far_select_ref, mate_near_ref
):
    entries, cells = got_ref.shape
    classes = near_select_ref.shape[0] // cells
    step = away()
    got, crossed = got_ref[...], crossed_ref[...]
    low, high = swapped_ref[:entries, :], swapped_ref[entries:, :]
    near, far, mate_near = got, crossed, low
    if halves:
        first = lax.axis_index("sub") == 0
        near = jnp.where(first, near, high)
        far = jnp.where(first, far, low)
        mate_near = jnp.where(first, mate_near, crossed)
    build_select(near, (REACH - step) * cells, near_select_ref, 0, classes)
    build_select(far, (REACH - 2 * step) * cells, far_select_ref, 0, classes)
    build_select(mate_near, (REACH + 2 * step) * cells, mate_near_ref, 0, classes)


def selections(got, crossed, swapped, classes, halves):
    cells = got.shape[1]
    select = jax.ShapeDtypeStruct((classes * cells, cells), jnp.bfloat16)
    return pl.pallas_call(
        functools.partial(select_kernel, halves),
        out_shape=[select] * 3,
        in_specs=[WHOLE] * 3,
        out_specs=[WHOLE] * 3,
        cost_estimate=pl.CostEstimate(flops=1 << 20, bytes_accessed=0, transcendentals=0),
        compiler_params=pltpu.CompilerParams(vmem_limit_bytes=8 << 20),
        name="selections",
    )(got, crossed, swapped)


def push_away_kernel(
    windows, held_ref, low_ref, high_ref, other_ref,
    mate_select_ref, far_select_ref, mate_near_ref,
    terms_ref, mate_ref, far_ref, padded, product,
):
    rows, classes, _ = held_ref.shape
    cells = far_ref.shape[1]
    split = low_ref.shape[0]

    def own_half(start, size):
        if start * classes < split:
            return low_ref[start * classes : (start + size) * classes, :]
        row = start * classes - split
        return high_ref[row : row + size * classes, :]

    def part_classes(source, start, size):
        for k in range(classes):
            term = source[pl.ds(start * classes + k, size, stride=classes), :]
            terms_ref[start : start + size, k * cells : (k + 1) * cells] = term.astype(jnp.bfloat16)

    for index, (low, high, offset) in enumerate(windows):
        def run(low=low, high=high, offset=offset):
            pad_into(padded, offset, other_ref)
            right = padded[: high - low, :].astype(jnp.bfloat16)
            for start, size in chunks(rows, CHUNK):
                left = held_ref[start : start + size, :, low:high]
                part = slice(start * classes, (start + size) * classes)
                product[part, :] = own_half(start, size) + jnp.dot(
                    left.reshape(size * classes, high - low), right,
                    preferred_element_type=jnp.float32,
                )
                part_classes(product, start, size)
        pl.when(lax.axis_index("sub") != index)(run)

    if not windows:
        for start, size in chunks(rows, CHUNK):
            product[start * classes : (start + size) * classes, :] = own_half(start, size)
            part_classes(product, start, size)

    terms = terms_ref[...]
    chosen = jnp.concatenate([mate_select_ref[...], far_select_ref[...], mate_near_ref[...]], axis=1)
    total = jnp.dot(terms, chosen, preferred_element_type=jnp.float32).astype(jnp.bfloat16)
    mate_ref[:, :cells] = total[:, :cells]
    far_ref[...] = total[:, cells : 2 * cells]
    mate_ref[:, cells:] = total[:, 2 * cells :]


def push_away(held, low, high, other, mate_select, far_select, mate_near, windows):
    rows, classes, depth = held.shape
    cells = other.shape[1]
    span = max([high - low for low, high, _ in windows], default=LANES)
    return pl.pallas_call(
        functools.partial(push_away_kernel, windows),
        out_shape=[
            jax.ShapeDtypeStruct((rows, classes * cells), jnp.bfloat16),
            jax.ShapeDtypeStruct((rows, 2 * cells), jnp.bfloat16),
            jax.ShapeDtypeStruct((rows, cells), jnp.bfloat16),
        ],
        in_specs=[WHOLE] * 7,
        out_specs=[WHOLE] * 3,
        scratch_shapes=[
            pltpu.VMEM((span, cells), jnp.float32),
            pltpu.VMEM((rows * classes, cells), jnp.float32),
        ],
        cost_estimate=pl.CostEstimate(
            flops=2 * rows * classes * cells * (span + 3 * cells),
            bytes_accessed=2 * rows * classes * depth,
            transcendentals=0,
        ),
        compiler_params=pltpu.CompilerParams(vmem_limit_bytes=32 << 20),
        name="push_away",
    )(held, low, high, other, mate_select, far_select, mate_near)


def push_home_kernel(terms_ref, home_ref, near_select_ref, came_ref, own_ref, near_ref):
    cells = near_ref.shape[1]
    chosen = jnp.concatenate([home_ref[...], near_select_ref[...]], axis=1)
    total = jnp.dot(terms_ref[...], chosen, preferred_element_type=jnp.float32)
    total = total + came_ref[...].astype(jnp.float32)
    own_ref[...] = total[:, :cells]
    near_ref[...] = total[:, cells:].astype(jnp.bfloat16)


def push_home(terms, home, near_select, came):
    rows = terms.shape[0]
    cells = home.shape[1]
    return pl.pallas_call(
        push_home_kernel,
        out_shape=[
            jax.ShapeDtypeStruct((rows, cells), jnp.float32),
            jax.ShapeDtypeStruct((rows, cells), jnp.bfloat16),
        ],
        in_specs=[WHOLE] * 4,
        out_specs=[WHOLE] * 2,
        cost_estimate=pl.CostEstimate(
            flops=2 * terms.size * 2 * cells, bytes_accessed=4 * terms.size, transcendentals=0
        ),
        compiler_params=pltpu.CompilerParams(vmem_limit_bytes=16 << 20),
        name="push_home",
    )(terms, home, near_select, came)


def shards(up_check, up_inverse, translate, down_inverse, list_slot, list_class, list_count):
    classes, rows, depth = translate.shape
    cells, entries = list_slot.shape
    halves = lax.axis_size("sub") == 2

    code = coded(list_slot, list_class, list_count)
    mate_code = to_mate(code)

    operators = jnp.transpose(translate, (1, 0, 2))
    if halves:
        windows = half_windows(rows, depth, 2)
        got = near_or_mates_far(code)
        equivalent = joined_product(up_inverse, up_check, across_sub(up_check))
        other = across_sub(equivalent)
        got, _ = lax.optimization_barrier((got, equivalent))
        crossed = crosswise(got)
    else:
        windows = [(0, depth, 0)]
        equivalent = lax.all_gather(
            jnp.dot(
                up_inverse, lax.all_gather(up_check, "sub", axis=0, tiled=True),
                preferred_element_type=jnp.float32,
            ).astype(jnp.bfloat16),
            "sub", axis=0, tiled=True,
        )
        other = equivalent
        near_codes = to_near(jnp.concatenate([code, mate_code], axis=0))
        got, crossed = near_codes[:entries], near_codes[entries:]

    parts = chunks(rows, CHUNK)
    half = pl.cdiv(len(parts), 2)
    low, home = prepare(operators, equivalent, code, windows, parts[:half], 0)
    crossed, low = lax.optimization_barrier((crossed, low))
    swapped = to_mate(jnp.concatenate([got, crossed], axis=0))
    high, mate_select = prepare(operators, equivalent, mate_code, windows, parts[half:], 1)
    swapped, high = lax.optimization_barrier((swapped, high))
    near_select, far_select, mate_near = selections(got, crossed, swapped, classes, halves)
    terms, mate_sum, far_sum = push_away(
        operators, low, high, other, mate_select, far_select, mate_near,
        windows if halves else [],
    )
    mate_came = to_mate(mate_sum)
    far_came = to_far(far_sum)
    own_sum, near_sum = push_home(terms, home, near_select, mate_came)
    near_came = to_near(near_sum)
    down_check = (
        own_sum + (far_came.astype(jnp.float32) + near_came.astype(jnp.float32))
    ).astype(jnp.bfloat16)
    if halves:
        other_down = across_sub(down_check)
        return rest(down_inverse, first(down_inverse, down_check, windows), other_down, windows)
    return jnp.dot(
        down_inverse, lax.all_gather(down_check, "sub", axis=0, tiled=True),
        preferred_element_type=jnp.float32,
    ).astype(jnp.bfloat16)


def solution(mesh):
    in_specs = (
        P("sub", "tile"),
        P("sub", None),
        P(None, "sub", None),
        P("sub", None),
        P("tile", None),
        P("tile", None),
        P("tile"),
    )
    out_specs = P("sub", "tile")
    return jax.shard_map(shards, mesh=mesh, in_specs=in_specs, out_specs=out_specs, check_vma=False)
```

```python
import functools

import jax
import jax.numpy as jnp
from jax import lax
from jax.experimental import pallas as pl
from jax.experimental.pallas import tpu as pltpu
from jax.sharding import PartitionSpec as P

REACH = 2
CLASS_SHIFT = 10
CHUNK = 112
LANES = 128
WHOLE = pl.BlockSpec(memory_space=pltpu.VMEM)


def across_sub(shard):
    return lax.ppermute(shard, "sub", [(0, 1), (1, 0)])


def to_mate(value):
    count = lax.axis_size("tile")
    pairs = [(t, t ^ 1) for t in range(count) if t ^ 1 < count]
    return lax.ppermute(value, "tile", pairs)


def to_near(value):
    count = lax.axis_size("tile")
    pairs = [(t, t + 2 * (t % 2) - 1) for t in range(count)]
    return lax.ppermute(value, "tile", [(a, b) for a, b in pairs if 0 <= b < count])


def to_far(value):
    count = lax.axis_size("tile")
    pairs = [(t, t + 4 * (t % 2) - 2) for t in range(count)]
    return lax.ppermute(value, "tile", [(a, b) for a, b in pairs if 0 <= b < count])


def away():
    return 2 * lax.rem(lax.axis_index("tile"), 2) - 1


def half_windows(shard_rows, depth, count):
    windows = []
    for index in range(count):
        low, high = index * shard_rows, (index + 1) * shard_rows
        start = low // LANES * LANES
        stop = min(pl.cdiv(high, LANES) * LANES, depth)
        windows.append((start, stop, low - start))
    return windows


def chunks(rows, size):
    return [(start, min(size, rows - start)) for start in range(0, rows, size)]


def pad_into(padded, offset, *refs):
    padded[...] = jnp.zeros(padded.shape, padded.dtype)
    for i, ref in enumerate(refs):
        rows, cells = ref.shape
        padded[offset : offset + rows, i * cells : (i + 1) * cells] = ref[...].astype(padded.dtype)


def joined_kernel(matrix_ref, own_ref, other_ref, out_ref, joined):
    rows = own_ref.shape[0]
    halves = [slice(0, rows), slice(rows, 2 * rows)]
    for index in range(2):
        def place(index=index):
            joined[halves[index], :] = own_ref[...].astype(jnp.float32)
            joined[halves[1 - index], :] = other_ref[...].astype(jnp.float32)
        pl.when(lax.axis_index("sub") == index)(place)
    out_ref[...] = jnp.dot(
        matrix_ref[...], joined[...].astype(jnp.bfloat16), preferred_element_type=jnp.float32
    ).astype(jnp.bfloat16)


def joined_product(matrix, own, other):
    rows, depth = matrix.shape
    cells = own.shape[1]
    return pl.pallas_call(
        joined_kernel,
        out_shape=jax.ShapeDtypeStruct((rows, cells), jnp.bfloat16),
        in_specs=[WHOLE] * 3,
        out_specs=WHOLE,
        scratch_shapes=[pltpu.VMEM((depth, cells), jnp.float32)],
        cost_estimate=pl.CostEstimate(
            flops=2 * rows * depth * cells, bytes_accessed=2 * rows * depth, transcendentals=0
        ),
        compiler_params=pltpu.CompilerParams(vmem_limit_bytes=8 << 20),
        name="joined",
    )(matrix, own, other)


def first_kernel(windows, matrix_ref, own_ref, out_ref, padded):
    for index, (low, high, offset) in enumerate(windows):
        def run(low=low, high=high, offset=offset):
            pad_into(padded, offset, own_ref)
            out_ref[...] = jnp.dot(
                matrix_ref[:, low:high], padded[: high - low, :].astype(jnp.bfloat16),
                preferred_element_type=jnp.float32,
            )
        pl.when(lax.axis_index("sub") == index)(run)


def first(matrix, own, windows):
    rows, depth = matrix.shape
    cells = own.shape[1]
    span = max(high - low for low, high, _ in windows)
    return pl.pallas_call(
        functools.partial(first_kernel, windows),
        out_shape=jax.ShapeDtypeStruct((rows, cells), jnp.float32),
        in_specs=[WHOLE] * 2,
        out_specs=WHOLE,
        scratch_shapes=[pltpu.VMEM((span, cells), jnp.float32)],
        cost_estimate=pl.CostEstimate(
            flops=2 * rows * depth * cells, bytes_accessed=4 * rows * depth, transcendentals=0
        ),
        compiler_params=pltpu.CompilerParams(vmem_limit_bytes=16 << 20),
        name="first",
    )(matrix, own)


def rest_kernel(windows, matrix_ref, part_ref, other_ref, out_ref, padded):
    for index, (low, high, offset) in enumerate(windows):
        def run(low=low, high=high, offset=offset):
            pad_into(padded, offset, other_ref)
            out_ref[...] = (
                part_ref[...]
                + jnp.dot(
                    matrix_ref[:, low:high], padded[: high - low, :].astype(jnp.bfloat16),
                    preferred_element_type=jnp.float32,
                )
            ).astype(jnp.bfloat16)
        pl.when(lax.axis_index("sub") != index)(run)


def rest(matrix, part, other, windows):
    rows, depth = matrix.shape
    cells = other.shape[1]
    span = max(high - low for low, high, _ in windows)
    return pl.pallas_call(
        functools.partial(rest_kernel, windows),
        out_shape=jax.ShapeDtypeStruct((rows, cells), jnp.bfloat16),
        in_specs=[WHOLE] * 3,
        out_specs=WHOLE,
        scratch_shapes=[pltpu.VMEM((span, cells), jnp.float32)],
        cost_estimate=pl.CostEstimate(
            flops=2 * rows * span * cells, bytes_accessed=2 * rows * span, transcendentals=0
        ),
        compiler_params=pltpu.CompilerParams(vmem_limit_bytes=16 << 20),
        name="rest",
    )(matrix, part, other)


def build_select(code, base, out_ref, column, classes):
    entries, cells = code.shape
    slots = (code & ((1 << CLASS_SHIFT) - 1)) - base
    kinds = code >> CLASS_SHIFT
    band = 32
    for low in range(0, cells, band):
        source = lax.broadcasted_iota(jnp.int32, (band, cells), 0) + low
        totals = [jnp.zeros((band, cells), jnp.bfloat16)] * classes
        for entry in range(entries):
            hit = jnp.where(slots[entry : entry + 1, :] == source, 1.0, 0.0).astype(jnp.bfloat16)
            for k in range(classes):
                used = jnp.where(kinds[entry : entry + 1, :] == k, 1.0, 0.0).astype(jnp.bfloat16)
                totals[k] = totals[k] + hit * used
        for k in range(classes):
            row = k * cells + low
            out_ref[row : row + band, column : column + cells] = totals[k]


def prepare_kernel(
    windows, part, operators_ref, own_ref, product_ref, padded
):
    classes = operators_ref.shape[1]

    for index, (low, high, offset) in enumerate(windows):
        def run(low=low, high=high, offset=offset):
            pad_into(padded, offset, own_ref)
            right = padded[: high - low, :].astype(jnp.bfloat16)
            for start, size in part:
                left = operators_ref[start : start + size, :, low:high]
                row = (start - part[0][0]) * classes
                product_ref[row : row + size * classes, :] = jnp.dot(
                    left.reshape(size * classes, high - low), right,
                    preferred_element_type=jnp.float32,
                )
        if len(windows) == 1:
            run()
        else:
            pl.when(lax.axis_index("sub") == index)(run)


def prepare(operators, own, windows, part):
    classes = operators.shape[1]
    cells = own.shape[1]
    span = max(high - low for low, high, _ in windows)
    rows = sum(size for _, size in part)
    return pl.pallas_call(
        functools.partial(prepare_kernel, windows, part),
        out_shape=jax.ShapeDtypeStruct((rows * classes, cells), jnp.float32),
        in_specs=[WHOLE] * 2,
        out_specs=WHOLE,
        scratch_shapes=[pltpu.VMEM((span, cells), jnp.float32)],
        cost_estimate=pl.CostEstimate(flops=1 << 32, bytes_accessed=0, transcendentals=0),
        compiler_params=pltpu.CompilerParams(vmem_limit_bytes=24 << 20),
        name="prepare",
    )(operators, own)


def home_kernel(code_ref, out_ref):
    cells = code_ref.shape[1]
    build_select(code_ref[...], REACH * cells, out_ref, 0, out_ref.shape[0] // cells)


def home_selection(code, classes):
    cells = code.shape[1]
    return pl.pallas_call(
        home_kernel,
        out_shape=jax.ShapeDtypeStruct((classes * cells, cells), jnp.bfloat16),
        in_specs=[WHOLE],
        out_specs=WHOLE,
        cost_estimate=pl.CostEstimate(flops=1 << 31, bytes_accessed=0, transcendentals=0),
        compiler_params=pltpu.CompilerParams(vmem_limit_bytes=8 << 20),
        name="home",
    )(code)


def select_kernel(mate_ref, near_ref, mate_near_ref, *select_refs):
    entries, cells = mate_ref.shape
    step = away()
    for ref, code, distance in zip(
        select_refs,
        (mate_ref[...], near_ref[:entries, :], near_ref[entries:, :], mate_near_ref[...]),
        (-step, step, 2 * step, -2 * step),
    ):
        build_select(code, (REACH - distance) * cells, ref, 0, ref.shape[0] // cells)


def selections(mate_code, near_codes, mate_near_code, classes):
    cells = mate_code.shape[1]
    select = jax.ShapeDtypeStruct((classes * cells, cells), jnp.bfloat16)
    return pl.pallas_call(
        select_kernel,
        out_shape=[select] * 4,
        in_specs=[WHOLE] * 3,
        out_specs=[WHOLE] * 4,
        cost_estimate=pl.CostEstimate(flops=1 << 20, bytes_accessed=0, transcendentals=0),
        compiler_params=pltpu.CompilerParams(vmem_limit_bytes=8 << 20),
        name="selections",
    )(mate_code, near_codes, mate_near_code)


def push_away_kernel(
    windows, held_ref, low_ref, high_ref, other_ref,
    mate_select_ref, far_select_ref, mate_near_ref,
    terms_ref, mate_ref, far_ref, padded, product,
):
    rows, classes, _ = held_ref.shape
    cells = far_ref.shape[1]
    split = low_ref.shape[0]

    def own_half(start, size):
        if start * classes < split:
            return low_ref[start * classes : (start + size) * classes, :]
        row = start * classes - split
        return high_ref[row : row + size * classes, :]

    def part_classes(source, start, size):
        for k in range(classes):
            term = source[pl.ds(start * classes + k, size, stride=classes), :]
            terms_ref[start : start + size, k * cells : (k + 1) * cells] = term.astype(jnp.bfloat16)

    for index, (low, high, offset) in enumerate(windows):
        def run(low=low, high=high, offset=offset):
            pad_into(padded, offset, other_ref)
            right = padded[: high - low, :].astype(jnp.bfloat16)
            for start, size in chunks(rows, CHUNK):
                left = held_ref[start : start + size, :, low:high]
                part = slice(start * classes, (start + size) * classes)
                product[part, :] = own_half(start, size) + jnp.dot(
                    left.reshape(size * classes, high - low), right,
                    preferred_element_type=jnp.float32,
                )
                part_classes(product, start, size)
        pl.when(lax.axis_index("sub") != index)(run)

    if not windows:
        for start, size in chunks(rows, CHUNK):
            product[start * classes : (start + size) * classes, :] = own_half(start, size)
            part_classes(product, start, size)

    terms = terms_ref[...]
    chosen = jnp.concatenate([mate_select_ref[...], far_select_ref[...], mate_near_ref[...]], axis=1)
    total = jnp.dot(terms, chosen, preferred_element_type=jnp.float32).astype(jnp.bfloat16)
    mate_ref[:, :cells] = total[:, :cells]
    far_ref[...] = total[:, cells : 2 * cells]
    mate_ref[:, cells:] = total[:, 2 * cells :]


def push_away(held, low, high, other, mate_select, far_select, mate_near, windows):
    rows, classes, depth = held.shape
    cells = other.shape[1]
    span = max([high - low for low, high, _ in windows], default=LANES)
    return pl.pallas_call(
        functools.partial(push_away_kernel, windows),
        out_shape=[
            jax.ShapeDtypeStruct((rows, classes * cells), jnp.bfloat16),
            jax.ShapeDtypeStruct((rows, 2 * cells), jnp.bfloat16),
            jax.ShapeDtypeStruct((rows, cells), jnp.bfloat16),
        ],
        in_specs=[WHOLE] * 7,
        out_specs=[WHOLE] * 3,
        scratch_shapes=[
            pltpu.VMEM((span, cells), jnp.float32),
            pltpu.VMEM((rows * classes, cells), jnp.float32),
        ],
        cost_estimate=pl.CostEstimate(
            flops=2 * rows * classes * cells * (span + 3 * cells),
            bytes_accessed=2 * rows * classes * depth,
            transcendentals=0,
        ),
        compiler_params=pltpu.CompilerParams(vmem_limit_bytes=32 << 20),
        name="push_away",
    )(held, low, high, other, mate_select, far_select, mate_near)


def push_home_kernel(terms_ref, home_ref, near_select_ref, came_ref, own_ref, near_ref):
    cells = near_ref.shape[1]
    chosen = jnp.concatenate([home_ref[...], near_select_ref[...]], axis=1)
    total = jnp.dot(terms_ref[...], chosen, preferred_element_type=jnp.float32)
    total = total + came_ref[...].astype(jnp.float32)
    own_ref[...] = total[:, :cells]
    near_ref[...] = total[:, cells:].astype(jnp.bfloat16)


def push_home(terms, home, near_select, came):
    rows = terms.shape[0]
    cells = home.shape[1]
    return pl.pallas_call(
        push_home_kernel,
        out_shape=[
            jax.ShapeDtypeStruct((rows, cells), jnp.float32),
            jax.ShapeDtypeStruct((rows, cells), jnp.bfloat16),
        ],
        in_specs=[WHOLE] * 4,
        out_specs=[WHOLE] * 2,
        cost_estimate=pl.CostEstimate(
            flops=2 * terms.size * 2 * cells, bytes_accessed=4 * terms.size, transcendentals=0
        ),
        compiler_params=pltpu.CompilerParams(vmem_limit_bytes=16 << 20),
        name="push_home",
    )(terms, home, near_select, came)


def shards(up_check, up_inverse, translate, down_inverse, list_slot, list_class, list_count):
    classes, rows, depth = translate.shape
    cells, entries = list_slot.shape
    halves = lax.axis_size("sub") == 2

    active = lax.broadcasted_iota(jnp.int32, (entries, cells), 0) < list_count[None, :]
    code = jnp.where(active, (list_class.T << CLASS_SHIFT) + list_slot.T, -1)
    mate_code, home = lax.optimization_barrier((to_mate(code), home_selection(code, classes)))
    near_codes = to_near(jnp.concatenate([code, mate_code], axis=0))

    operators = jnp.transpose(translate, (1, 0, 2))
    if halves:
        windows = half_windows(rows, depth, 2)
        equivalent = joined_product(up_inverse, up_check, across_sub(up_check))
        other = across_sub(equivalent)
    else:
        windows = [(0, depth, 0)]
        equivalent = lax.all_gather(
            jnp.dot(
                up_inverse, lax.all_gather(up_check, "sub", axis=0, tiled=True),
                preferred_element_type=jnp.float32,
            ).astype(jnp.bfloat16),
            "sub", axis=0, tiled=True,
        )
        other = equivalent

    parts = chunks(rows, CHUNK)
    half = pl.cdiv(len(parts), 2)
    low = prepare(operators, equivalent, windows, parts[:half])
    near_codes, low = lax.optimization_barrier((near_codes, low))
    mate_near_code = to_mate(near_codes[:entries])
    high = prepare(operators, equivalent, windows, parts[half:])
    mate_near_code, high = lax.optimization_barrier((mate_near_code, high))
    mate_select, near_select, far_select, mate_near = selections(
        mate_code, near_codes, mate_near_code, classes
    )
    terms, mate_sum, far_sum = push_away(
        operators, low, high, other, mate_select, far_select, mate_near,
        windows if halves else [],
    )
    mate_came = to_mate(mate_sum)
    far_came = to_far(far_sum)
    own_sum, near_sum = push_home(terms, home, near_select, mate_came)
    near_came = to_near(near_sum)
    down_check = (
        own_sum + (far_came.astype(jnp.float32) + near_came.astype(jnp.float32))
    ).astype(jnp.bfloat16)
    if halves:
        other_down = across_sub(down_check)
        return rest(down_inverse, first(down_inverse, down_check, windows), other_down, windows)
    return jnp.dot(
        down_inverse, lax.all_gather(down_check, "sub", axis=0, tiled=True),
        preferred_element_type=jnp.float32,
    ).astype(jnp.bfloat16)


def solution(mesh):
    in_specs = (
        P("sub", "tile"),
        P("sub", None),
        P(None, "sub", None),
        P("sub", None),
        P("tile", None),
        P("tile", None),
        P("tile"),
    )
    out_specs = P("sub", "tile")
    return jax.shard_map(shards, mesh=mesh, in_specs=in_specs, out_specs=out_specs, check_vma=False)
```

```python
import functools

import jax
import jax.numpy as jnp
from jax import lax
from jax.experimental import pallas as pl
from jax.experimental.pallas import tpu as pltpu
from jax.sharding import PartitionSpec as P

REACH = 2
CLASS_SHIFT = 10
CHUNK = 112
LANES = 128
WHOLE = pl.BlockSpec(memory_space=pltpu.VMEM)


def across_sub(shard):
    return lax.ppermute(shard, "sub", [(0, 1), (1, 0)])


def to_mate(value):
    count = lax.axis_size("tile")
    pairs = [(t, t ^ 1) for t in range(count) if t ^ 1 < count]
    return lax.ppermute(value, "tile", pairs)


def to_near(value):
    count = lax.axis_size("tile")
    pairs = [(t, t + 2 * (t % 2) - 1) for t in range(count)]
    return lax.ppermute(value, "tile", [(a, b) for a, b in pairs if 0 <= b < count])


def to_near_crosswise(value):
    count = lax.axis_size("tile")
    pairs = []
    for t in range(count):
        target = t + 2 * (t % 2) - 1
        if 0 <= target < count:
            pairs += [(2 * t + index, 2 * target + 1 - index) for index in range(2)]
    return lax.ppermute(value, ("tile", "sub"), pairs)


def to_far(value):
    count = lax.axis_size("tile")
    pairs = [(t, t + 4 * (t % 2) - 2) for t in range(count)]
    return lax.ppermute(value, "tile", [(a, b) for a, b in pairs if 0 <= b < count])


def away():
    return 2 * lax.rem(lax.axis_index("tile"), 2) - 1


def half_windows(shard_rows, depth, count):
    windows = []
    for index in range(count):
        low, high = index * shard_rows, (index + 1) * shard_rows
        start = low // LANES * LANES
        stop = min(pl.cdiv(high, LANES) * LANES, depth)
        windows.append((start, stop, low - start))
    return windows


def chunks(rows, size):
    return [(start, min(size, rows - start)) for start in range(0, rows, size)]


def pad_into(padded, offset, *refs):
    padded[...] = jnp.zeros(padded.shape, padded.dtype)
    for i, ref in enumerate(refs):
        rows, cells = ref.shape
        padded[offset : offset + rows, i * cells : (i + 1) * cells] = ref[...].astype(padded.dtype)


def joined_kernel(matrix_ref, own_ref, other_ref, out_ref, joined):
    rows = own_ref.shape[0]
    halves = [slice(0, rows), slice(rows, 2 * rows)]
    for index in range(2):
        def place(index=index):
            joined[halves[index], :] = own_ref[...].astype(jnp.float32)
            joined[halves[1 - index], :] = other_ref[...].astype(jnp.float32)
        pl.when(lax.axis_index("sub") == index)(place)
    out_ref[...] = jnp.dot(
        matrix_ref[...], joined[...].astype(jnp.bfloat16), preferred_element_type=jnp.float32
    ).astype(jnp.bfloat16)


def joined_product(matrix, own, other):
    rows, depth = matrix.shape
    cells = own.shape[1]
    return pl.pallas_call(
        joined_kernel,
        out_shape=jax.ShapeDtypeStruct((rows, cells), jnp.bfloat16),
        in_specs=[WHOLE] * 3,
        out_specs=WHOLE,
        scratch_shapes=[pltpu.VMEM((depth, cells), jnp.float32)],
        cost_estimate=pl.CostEstimate(
            flops=2 * rows * depth * cells, bytes_accessed=2 * rows * depth, transcendentals=0
        ),
        compiler_params=pltpu.CompilerParams(vmem_limit_bytes=8 << 20),
        name="joined",
    )(matrix, own, other)


def first_kernel(windows, matrix_ref, own_ref, out_ref, padded):
    for index, (low, high, offset) in enumerate(windows):
        def run(low=low, high=high, offset=offset):
            pad_into(padded, offset, own_ref)
            out_ref[...] = jnp.dot(
                matrix_ref[:, low:high], padded[: high - low, :].astype(jnp.bfloat16),
                preferred_element_type=jnp.float32,
            )
        pl.when(lax.axis_index("sub") == index)(run)


def first(matrix, own, windows):
    rows, depth = matrix.shape
    cells = own.shape[1]
    span = max(high - low for low, high, _ in windows)
    return pl.pallas_call(
        functools.partial(first_kernel, windows),
        out_shape=jax.ShapeDtypeStruct((rows, cells), jnp.float32),
        in_specs=[WHOLE] * 2,
        out_specs=WHOLE,
        scratch_shapes=[pltpu.VMEM((span, cells), jnp.float32)],
        cost_estimate=pl.CostEstimate(
            flops=2 * rows * depth * cells, bytes_accessed=4 * rows * depth, transcendentals=0
        ),
        compiler_params=pltpu.CompilerParams(vmem_limit_bytes=16 << 20),
        name="first",
    )(matrix, own)


def rest_kernel(windows, matrix_ref, part_ref, other_ref, out_ref, padded):
    for index, (low, high, offset) in enumerate(windows):
        def run(low=low, high=high, offset=offset):
            pad_into(padded, offset, other_ref)
            out_ref[...] = (
                part_ref[...]
                + jnp.dot(
                    matrix_ref[:, low:high], padded[: high - low, :].astype(jnp.bfloat16),
                    preferred_element_type=jnp.float32,
                )
            ).astype(jnp.bfloat16)
        pl.when(lax.axis_index("sub") != index)(run)


def rest(matrix, part, other, windows):
    rows, depth = matrix.shape
    cells = other.shape[1]
    span = max(high - low for low, high, _ in windows)
    return pl.pallas_call(
        functools.partial(rest_kernel, windows),
        out_shape=jax.ShapeDtypeStruct((rows, cells), jnp.bfloat16),
        in_specs=[WHOLE] * 3,
        out_specs=WHOLE,
        scratch_shapes=[pltpu.VMEM((span, cells), jnp.float32)],
        cost_estimate=pl.CostEstimate(
            flops=2 * rows * span * cells, bytes_accessed=2 * rows * span, transcendentals=0
        ),
        compiler_params=pltpu.CompilerParams(vmem_limit_bytes=16 << 20),
        name="rest",
    )(matrix, part, other)


def build_select(code, base, out_ref, column, classes):
    entries, cells = code.shape
    slots = (code & ((1 << CLASS_SHIFT) - 1)) - base
    kinds = code >> CLASS_SHIFT
    band = 32
    for low in range(0, cells, band):
        source = lax.broadcasted_iota(jnp.int32, (band, cells), 0) + low
        totals = [jnp.zeros((band, cells), jnp.bfloat16)] * classes
        for entry in range(entries):
            hit = jnp.where(slots[entry : entry + 1, :] == source, 1.0, 0.0).astype(jnp.bfloat16)
            for k in range(classes):
                used = jnp.where(kinds[entry : entry + 1, :] == k, 1.0, 0.0).astype(jnp.bfloat16)
                totals[k] = totals[k] + hit * used
        for k in range(classes):
            row = k * cells + low
            out_ref[row : row + band, column : column + cells] = totals[k]


def prepare_kernel(
    windows, part, operators_ref, own_ref, product_ref, padded
):
    classes = operators_ref.shape[1]

    for index, (low, high, offset) in enumerate(windows):
        def run(low=low, high=high, offset=offset):
            pad_into(padded, offset, own_ref)
            right = padded[: high - low, :].astype(jnp.bfloat16)
            for start, size in part:
                left = operators_ref[start : start + size, :, low:high]
                row = (start - part[0][0]) * classes
                product_ref[row : row + size * classes, :] = jnp.dot(
                    left.reshape(size * classes, high - low), right,
                    preferred_element_type=jnp.float32,
                )
        if len(windows) == 1:
            run()
        else:
            pl.when(lax.axis_index("sub") == index)(run)


def prepare(operators, own, windows, part):
    classes = operators.shape[1]
    cells = own.shape[1]
    span = max(high - low for low, high, _ in windows)
    rows = sum(size for _, size in part)
    return pl.pallas_call(
        functools.partial(prepare_kernel, windows, part),
        out_shape=jax.ShapeDtypeStruct((rows * classes, cells), jnp.float32),
        in_specs=[WHOLE] * 2,
        out_specs=WHOLE,
        scratch_shapes=[pltpu.VMEM((span, cells), jnp.float32)],
        cost_estimate=pl.CostEstimate(flops=1 << 32, bytes_accessed=0, transcendentals=0),
        compiler_params=pltpu.CompilerParams(vmem_limit_bytes=24 << 20),
        name="prepare",
    )(operators, own)


def home_kernel(code_ref, out_ref):
    cells = code_ref.shape[1]
    build_select(code_ref[...], REACH * cells, out_ref, 0, out_ref.shape[0] // cells)


def home_selection(code, classes):
    cells = code.shape[1]
    return pl.pallas_call(
        home_kernel,
        out_shape=jax.ShapeDtypeStruct((classes * cells, cells), jnp.bfloat16),
        in_specs=[WHOLE],
        out_specs=WHOLE,
        cost_estimate=pl.CostEstimate(flops=1 << 31, bytes_accessed=0, transcendentals=0),
        compiler_params=pltpu.CompilerParams(vmem_limit_bytes=8 << 20),
        name="home",
    )(code)


def select_kernel(mate_ref, near_ref, mate_near_ref, *select_refs):
    entries, cells = mate_ref.shape
    step = away()
    for ref, code, distance in zip(
        select_refs,
        (mate_ref[...], near_ref[:entries, :], near_ref[entries:, :], mate_near_ref[...]),
        (-step, step, 2 * step, -2 * step),
    ):
        build_select(code, (REACH - distance) * cells, ref, 0, ref.shape[0] // cells)


def selections(mate_code, near_codes, mate_near_code, classes):
    cells = mate_code.shape[1]
    select = jax.ShapeDtypeStruct((classes * cells, cells), jnp.bfloat16)
    return pl.pallas_call(
        select_kernel,
        out_shape=[select] * 4,
        in_specs=[WHOLE] * 3,
        out_specs=[WHOLE] * 4,
        cost_estimate=pl.CostEstimate(flops=1 << 20, bytes_accessed=0, transcendentals=0),
        compiler_params=pltpu.CompilerParams(vmem_limit_bytes=8 << 20),
        name="selections",
    )(mate_code, near_codes, mate_near_code)


def push_away_kernel(
    windows, held_ref, low_ref, high_ref, other_ref,
    mate_select_ref, far_select_ref, mate_near_ref,
    terms_ref, mate_ref, far_ref, padded, product,
):
    rows, classes, _ = held_ref.shape
    cells = far_ref.shape[1]
    split = low_ref.shape[0]

    def own_half(start, size):
        if start * classes < split:
            return low_ref[start * classes : (start + size) * classes, :]
        row = start * classes - split
        return high_ref[row : row + size * classes, :]

    def part_classes(source, start, size):
        for k in range(classes):
            term = source[pl.ds(start * classes + k, size, stride=classes), :]
            terms_ref[start : start + size, k * cells : (k + 1) * cells] = term.astype(jnp.bfloat16)

    for index, (low, high, offset) in enumerate(windows):
        def run(low=low, high=high, offset=offset):
            pad_into(padded, offset, other_ref)
            right = padded[: high - low, :].astype(jnp.bfloat16)
            for start, size in chunks(rows, CHUNK):
                left = held_ref[start : start + size, :, low:high]
                part = slice(start * classes, (start + size) * classes)
                product[part, :] = own_half(start, size) + jnp.dot(
                    left.reshape(size * classes, high - low), right,
                    preferred_element_type=jnp.float32,
                )
                part_classes(product, start, size)
        pl.when(lax.axis_index("sub") != index)(run)

    if not windows:
        for start, size in chunks(rows, CHUNK):
            product[start * classes : (start + size) * classes, :] = own_half(start, size)
            part_classes(product, start, size)

    terms = terms_ref[...]
    chosen = jnp.concatenate([mate_select_ref[...], far_select_ref[...], mate_near_ref[...]], axis=1)
    total = jnp.dot(terms, chosen, preferred_element_type=jnp.float32).astype(jnp.bfloat16)
    mate_ref[:, :cells] = total[:, :cells]
    far_ref[...] = total[:, cells : 2 * cells]
    mate_ref[:, cells:] = total[:, 2 * cells :]


def push_away(held, low, high, other, mate_select, far_select, mate_near, windows):
    rows, classes, depth = held.shape
    cells = other.shape[1]
    span = max([high - low for low, high, _ in windows], default=LANES)
    return pl.pallas_call(
        functools.partial(push_away_kernel, windows),
        out_shape=[
            jax.ShapeDtypeStruct((rows, classes * cells), jnp.bfloat16),
            jax.ShapeDtypeStruct((rows, 2 * cells), jnp.bfloat16),
            jax.ShapeDtypeStruct((rows, cells), jnp.bfloat16),
        ],
        in_specs=[WHOLE] * 7,
        out_specs=[WHOLE] * 3,
        scratch_shapes=[
            pltpu.VMEM((span, cells), jnp.float32),
            pltpu.VMEM((rows * classes, cells), jnp.float32),
        ],
        cost_estimate=pl.CostEstimate(
            flops=2 * rows * classes * cells * (span + 3 * cells),
            bytes_accessed=2 * rows * classes * depth,
            transcendentals=0,
        ),
        compiler_params=pltpu.CompilerParams(vmem_limit_bytes=32 << 20),
        name="push_away",
    )(held, low, high, other, mate_select, far_select, mate_near)


def push_home_kernel(terms_ref, home_ref, near_select_ref, came_ref, own_ref, near_ref):
    cells = near_ref.shape[1]
    chosen = jnp.concatenate([home_ref[...], near_select_ref[...]], axis=1)
    total = jnp.dot(terms_ref[...], chosen, preferred_element_type=jnp.float32)
    total = total + came_ref[...].astype(jnp.float32)
    own_ref[...] = total[:, :cells]
    near_ref[...] = total[:, cells:].astype(jnp.bfloat16)


def push_home(terms, home, near_select, came):
    rows = terms.shape[0]
    cells = home.shape[1]
    return pl.pallas_call(
        push_home_kernel,
        out_shape=[
            jax.ShapeDtypeStruct((rows, cells), jnp.float32),
            jax.ShapeDtypeStruct((rows, cells), jnp.bfloat16),
        ],
        in_specs=[WHOLE] * 4,
        out_specs=[WHOLE] * 2,
        cost_estimate=pl.CostEstimate(
            flops=2 * terms.size * 2 * cells, bytes_accessed=4 * terms.size, transcendentals=0
        ),
        compiler_params=pltpu.CompilerParams(vmem_limit_bytes=16 << 20),
        name="push_home",
    )(terms, home, near_select, came)


def shards(up_check, up_inverse, translate, down_inverse, list_slot, list_class, list_count):
    classes, rows, depth = translate.shape
    cells, entries = list_slot.shape
    halves = lax.axis_size("sub") == 2

    active = lax.broadcasted_iota(jnp.int32, (entries, cells), 0) < list_count[None, :]
    code = jnp.where(active, (list_class.T << CLASS_SHIFT) + list_slot.T, -1)
    mate_code, home = lax.optimization_barrier((to_mate(code), home_selection(code, classes)))
    near_codes = to_near(jnp.concatenate([code, mate_code], axis=0))

    operators = jnp.transpose(translate, (1, 0, 2))
    if halves:
        windows = half_windows(rows, depth, 2)
        equivalent = joined_product(up_inverse, up_check, across_sub(up_check))
        other = across_sub(equivalent)
    else:
        windows = [(0, depth, 0)]
        equivalent = lax.all_gather(
            jnp.dot(
                up_inverse, lax.all_gather(up_check, "sub", axis=0, tiled=True),
                preferred_element_type=jnp.float32,
            ).astype(jnp.bfloat16),
            "sub", axis=0, tiled=True,
        )
        other = equivalent

    parts = chunks(rows, CHUNK)
    half = pl.cdiv(len(parts), 2)
    low = prepare(operators, equivalent, windows, parts[:half])
    near_codes, low = lax.optimization_barrier((near_codes, low))
    mate_near_code = to_mate(near_codes[:entries])
    high = prepare(operators, equivalent, windows, parts[half:])
    mate_near_code, high = lax.optimization_barrier((mate_near_code, high))
    mate_select, near_select, far_select, mate_near = selections(
        mate_code, near_codes, mate_near_code, classes
    )
    terms, mate_sum, far_sum = push_away(
        operators, low, high, other, mate_select, far_select, mate_near,
        windows if halves else [],
    )
    mate_came = to_mate(mate_sum)
    far_came = to_far(far_sum)
    own_sum, near_sum = push_home(terms, home, near_select, mate_came)
    near_came = to_near(near_sum)
    if halves:
        near_crossed = to_near_crosswise(near_sum)
        far_came, _ = lax.optimization_barrier((far_came, near_sum))
    base = own_sum + far_came.astype(jnp.float32)
    if halves:
        half_base = base.astype(jnp.bfloat16)
        near_came, _ = lax.optimization_barrier((near_came, half_base))
        other_base = across_sub(half_base)
    down_check = (base + near_came.astype(jnp.float32)).astype(jnp.bfloat16)
    if halves:
        other_down = (
            other_base.astype(jnp.float32) + near_crossed.astype(jnp.float32)
        ).astype(jnp.bfloat16)
        return rest(down_inverse, first(down_inverse, down_check, windows), other_down, windows)
    return jnp.dot(
        down_inverse, lax.all_gather(down_check, "sub", axis=0, tiled=True),
        preferred_element_type=jnp.float32,
    ).astype(jnp.bfloat16)


def solution(mesh):
    in_specs = (
        P("sub", "tile"),
        P("sub", None),
        P(None, "sub", None),
        P("sub", None),
        P("tile", None),
        P("tile", None),
        P("tile"),
    )
    out_specs = P("sub", "tile")
    return jax.shard_map(shards, mesh=mesh, in_specs=in_specs, out_specs=out_specs, check_vma=False)
```

```python
import functools

import jax
import jax.numpy as jnp
from jax import lax
from jax.experimental import pallas as pl
from jax.experimental.pallas import tpu as pltpu
from jax.sharding import PartitionSpec as P

REACH = 2
CLASS_SHIFT = 10
CHUNK = 112
LANES = 128
WHOLE = pl.BlockSpec(memory_space=pltpu.VMEM)


def across_sub(shard):
    return lax.ppermute(shard, "sub", [(0, 1), (1, 0)])


def to_mate(value):
    count = lax.axis_size("tile")
    pairs = [(t, t ^ 1) for t in range(count) if t ^ 1 < count]
    return lax.ppermute(value, "tile", pairs)


def to_near(value):
    count = lax.axis_size("tile")
    pairs = [(t, t + 2 * (t % 2) - 1) for t in range(count)]
    return lax.ppermute(value, "tile", [(a, b) for a, b in pairs if 0 <= b < count])


def to_near_crosswise(value):
    count = lax.axis_size("tile")
    pairs = []
    for t in range(count):
        target = t + 2 * (t % 2) - 1
        if 0 <= target < count:
            pairs += [(2 * t + index, 2 * target + 1 - index) for index in range(2)]
    return lax.ppermute(value, ("tile", "sub"), pairs)


def to_far(value):
    count = lax.axis_size("tile")
    pairs = [(t, t + 4 * (t % 2) - 2) for t in range(count)]
    return lax.ppermute(value, "tile", [(a, b) for a, b in pairs if 0 <= b < count])


def away():
    return 2 * lax.rem(lax.axis_index("tile"), 2) - 1


def half_windows(shard_rows, depth, count):
    windows = []
    for index in range(count):
        low, high = index * shard_rows, (index + 1) * shard_rows
        start = low // LANES * LANES
        stop = min(pl.cdiv(high, LANES) * LANES, depth)
        windows.append((start, stop, low - start))
    return windows


def chunks(rows, size):
    return [(start, min(size, rows - start)) for start in range(0, rows, size)]


def pad_into(padded, offset, *refs):
    padded[...] = jnp.zeros(padded.shape, padded.dtype)
    for i, ref in enumerate(refs):
        rows, cells = ref.shape
        padded[offset : offset + rows, i * cells : (i + 1) * cells] = ref[...].astype(padded.dtype)


def joined_kernel(matrix_ref, own_ref, other_ref, out_ref, joined):
    rows = own_ref.shape[0]
    halves = [slice(0, rows), slice(rows, 2 * rows)]
    for index in range(2):
        def place(index=index):
            joined[halves[index], :] = own_ref[...].astype(jnp.float32)
            joined[halves[1 - index], :] = other_ref[...].astype(jnp.float32)
        pl.when(lax.axis_index("sub") == index)(place)
    out_ref[...] = jnp.dot(
        matrix_ref[...], joined[...].astype(jnp.bfloat16), preferred_element_type=jnp.float32
    ).astype(jnp.bfloat16)


def joined_product(matrix, own, other):
    rows, depth = matrix.shape
    cells = own.shape[1]
    return pl.pallas_call(
        joined_kernel,
        out_shape=jax.ShapeDtypeStruct((rows, cells), jnp.bfloat16),
        in_specs=[WHOLE] * 3,
        out_specs=WHOLE,
        scratch_shapes=[pltpu.VMEM((depth, cells), jnp.float32)],
        cost_estimate=pl.CostEstimate(
            flops=2 * rows * depth * cells, bytes_accessed=2 * rows * depth, transcendentals=0
        ),
        compiler_params=pltpu.CompilerParams(vmem_limit_bytes=8 << 20),
        name="joined",
    )(matrix, own, other)


def build_select(code, base, out_ref, column, classes):
    entries, cells = code.shape
    slots = (code & ((1 << CLASS_SHIFT) - 1)) - base
    kinds = code >> CLASS_SHIFT
    band = 32
    for low in range(0, cells, band):
        source = lax.broadcasted_iota(jnp.int32, (band, cells), 0) + low
        totals = [jnp.zeros((band, cells), jnp.bfloat16)] * classes
        for entry in range(entries):
            hit = jnp.where(slots[entry : entry + 1, :] == source, 1.0, 0.0).astype(jnp.bfloat16)
            for k in range(classes):
                used = jnp.where(kinds[entry : entry + 1, :] == k, 1.0, 0.0).astype(jnp.bfloat16)
                totals[k] = totals[k] + hit * used
        for k in range(classes):
            row = k * cells + low
            out_ref[row : row + band, column : column + cells] = totals[k]


def prepare_kernel(
    windows, part, operators_ref, own_ref, product_ref, padded
):
    classes = operators_ref.shape[1]

    for index, (low, high, offset) in enumerate(windows):
        def run(low=low, high=high, offset=offset):
            pad_into(padded, offset, own_ref)
            right = padded[: high - low, :].astype(jnp.bfloat16)
            for start, size in part:
                left = operators_ref[start : start + size, :, low:high]
                row = (start - part[0][0]) * classes
                product_ref[row : row + size * classes, :] = jnp.dot(
                    left.reshape(size * classes, high - low), right,
                    preferred_element_type=jnp.float32,
                )
        if len(windows) == 1:
            run()
        else:
            pl.when(lax.axis_index("sub") == index)(run)


def prepare(operators, own, windows, part):
    classes = operators.shape[1]
    cells = own.shape[1]
    span = max(high - low for low, high, _ in windows)
    rows = sum(size for _, size in part)
    return pl.pallas_call(
        functools.partial(prepare_kernel, windows, part),
        out_shape=jax.ShapeDtypeStruct((rows * classes, cells), jnp.float32),
        in_specs=[WHOLE] * 2,
        out_specs=WHOLE,
        scratch_shapes=[pltpu.VMEM((span, cells), jnp.float32)],
        cost_estimate=pl.CostEstimate(flops=1 << 32, bytes_accessed=0, transcendentals=0),
        compiler_params=pltpu.CompilerParams(vmem_limit_bytes=24 << 20),
        name="prepare",
    )(operators, own)


def home_kernel(code_ref, out_ref):
    cells = code_ref.shape[1]
    build_select(code_ref[...], REACH * cells, out_ref, 0, out_ref.shape[0] // cells)


def home_selection(code, classes):
    cells = code.shape[1]
    return pl.pallas_call(
        home_kernel,
        out_shape=jax.ShapeDtypeStruct((classes * cells, cells), jnp.bfloat16),
        in_specs=[WHOLE],
        out_specs=WHOLE,
        cost_estimate=pl.CostEstimate(flops=1 << 31, bytes_accessed=0, transcendentals=0),
        compiler_params=pltpu.CompilerParams(vmem_limit_bytes=8 << 20),
        name="home",
    )(code)


def select_kernel(mate_ref, near_ref, mate_near_ref, *select_refs):
    entries, cells = mate_ref.shape
    step = away()
    for ref, code, distance in zip(
        select_refs,
        (mate_ref[...], near_ref[:entries, :], near_ref[entries:, :], mate_near_ref[...]),
        (-step, step, 2 * step, -2 * step),
    ):
        build_select(code, (REACH - distance) * cells, ref, 0, ref.shape[0] // cells)


def selections(mate_code, near_codes, mate_near_code, classes):
    cells = mate_code.shape[1]
    select = jax.ShapeDtypeStruct((classes * cells, cells), jnp.bfloat16)
    return pl.pallas_call(
        select_kernel,
        out_shape=[select] * 4,
        in_specs=[WHOLE] * 3,
        out_specs=[WHOLE] * 4,
        cost_estimate=pl.CostEstimate(flops=1 << 20, bytes_accessed=0, transcendentals=0),
        compiler_params=pltpu.CompilerParams(vmem_limit_bytes=8 << 20),
        name="selections",
    )(mate_code, near_codes, mate_near_code)


def push_away_kernel(
    windows, held_ref, low_ref, high_ref, other_ref,
    mate_select_ref, far_select_ref, mate_near_ref,
    terms_ref, mate_ref, far_ref, padded, product,
):
    rows, classes, _ = held_ref.shape
    cells = far_ref.shape[1]
    split = low_ref.shape[0]

    def own_half(start, size):
        if start * classes < split:
            return low_ref[start * classes : (start + size) * classes, :]
        row = start * classes - split
        return high_ref[row : row + size * classes, :]

    def part_classes(source, start, size):
        for k in range(classes):
            term = source[pl.ds(start * classes + k, size, stride=classes), :]
            terms_ref[start : start + size, k * cells : (k + 1) * cells] = term.astype(jnp.bfloat16)

    for index, (low, high, offset) in enumerate(windows):
        def run(low=low, high=high, offset=offset):
            pad_into(padded, offset, other_ref)
            right = padded[: high - low, :].astype(jnp.bfloat16)
            for start, size in chunks(rows, CHUNK):
                left = held_ref[start : start + size, :, low:high]
                part = slice(start * classes, (start + size) * classes)
                product[part, :] = own_half(start, size) + jnp.dot(
                    left.reshape(size * classes, high - low), right,
                    preferred_element_type=jnp.float32,
                )
                part_classes(product, start, size)
        pl.when(lax.axis_index("sub") != index)(run)

    if not windows:
        for start, size in chunks(rows, CHUNK):
            product[start * classes : (start + size) * classes, :] = own_half(start, size)
            part_classes(product, start, size)

    terms = terms_ref[...]
    chosen = jnp.concatenate([mate_select_ref[...], far_select_ref[...], mate_near_ref[...]], axis=1)
    total = jnp.dot(terms, chosen, preferred_element_type=jnp.float32).astype(jnp.bfloat16)
    mate_ref[:, :cells] = total[:, :cells]
    far_ref[...] = total[:, cells : 2 * cells]
    mate_ref[:, cells:] = total[:, 2 * cells :]


def push_away(held, low, high, other, mate_select, far_select, mate_near, windows):
    rows, classes, depth = held.shape
    cells = other.shape[1]
    span = max([high - low for low, high, _ in windows], default=LANES)
    return pl.pallas_call(
        functools.partial(push_away_kernel, windows),
        out_shape=[
            jax.ShapeDtypeStruct((rows, classes * cells), jnp.bfloat16),
            jax.ShapeDtypeStruct((rows, 2 * cells), jnp.bfloat16),
            jax.ShapeDtypeStruct((rows, cells), jnp.bfloat16),
        ],
        in_specs=[WHOLE] * 7,
        out_specs=[WHOLE] * 3,
        scratch_shapes=[
            pltpu.VMEM((span, cells), jnp.float32),
            pltpu.VMEM((rows * classes, cells), jnp.float32),
        ],
        cost_estimate=pl.CostEstimate(
            flops=2 * rows * classes * cells * (span + 3 * cells),
            bytes_accessed=2 * rows * classes * depth,
            transcendentals=0,
        ),
        compiler_params=pltpu.CompilerParams(vmem_limit_bytes=32 << 20),
        name="push_away",
    )(held, low, high, other, mate_select, far_select, mate_near)


def push_home_kernel(terms_ref, home_ref, near_select_ref, came_ref, own_ref, near_ref):
    cells = near_ref.shape[1]
    chosen = jnp.concatenate([home_ref[...], near_select_ref[...]], axis=1)
    total = jnp.dot(terms_ref[...], chosen, preferred_element_type=jnp.float32)
    total = total + came_ref[...].astype(jnp.float32)
    own_ref[...] = total[:, :cells]
    near_ref[...] = total[:, cells:].astype(jnp.bfloat16)


def push_home(terms, home, near_select, came):
    rows = terms.shape[0]
    cells = home.shape[1]
    return pl.pallas_call(
        push_home_kernel,
        out_shape=[
            jax.ShapeDtypeStruct((rows, cells), jnp.float32),
            jax.ShapeDtypeStruct((rows, cells), jnp.bfloat16),
        ],
        in_specs=[WHOLE] * 4,
        out_specs=[WHOLE] * 2,
        cost_estimate=pl.CostEstimate(
            flops=2 * terms.size * 2 * cells, bytes_accessed=4 * terms.size, transcendentals=0
        ),
        compiler_params=pltpu.CompilerParams(vmem_limit_bytes=16 << 20),
        name="push_home",
    )(terms, home, near_select, came)


def shards(up_check, up_inverse, translate, down_inverse, list_slot, list_class, list_count):
    classes, rows, depth = translate.shape
    cells, entries = list_slot.shape
    halves = lax.axis_size("sub") == 2

    active = lax.broadcasted_iota(jnp.int32, (entries, cells), 0) < list_count[None, :]
    code = jnp.where(active, (list_class.T << CLASS_SHIFT) + list_slot.T, -1)
    mate_code, home = lax.optimization_barrier((to_mate(code), home_selection(code, classes)))
    near_codes = to_near(jnp.concatenate([code, mate_code], axis=0))

    operators = jnp.transpose(translate, (1, 0, 2))
    if halves:
        windows = half_windows(rows, depth, 2)
        equivalent = joined_product(up_inverse, up_check, across_sub(up_check))
        other = across_sub(equivalent)
    else:
        windows = [(0, depth, 0)]
        equivalent = lax.all_gather(
            jnp.dot(
                up_inverse, lax.all_gather(up_check, "sub", axis=0, tiled=True),
                preferred_element_type=jnp.float32,
            ).astype(jnp.bfloat16),
            "sub", axis=0, tiled=True,
        )
        other = equivalent

    parts = chunks(rows, CHUNK)
    half = pl.cdiv(len(parts), 2)
    low = prepare(operators, equivalent, windows, parts[:half])
    near_codes, low = lax.optimization_barrier((near_codes, low))
    mate_near_code = to_mate(near_codes[:entries])
    high = prepare(operators, equivalent, windows, parts[half:])
    mate_near_code, high = lax.optimization_barrier((mate_near_code, high))
    mate_select, near_select, far_select, mate_near = selections(
        mate_code, near_codes, mate_near_code, classes
    )
    terms, mate_sum, far_sum = push_away(
        operators, low, high, other, mate_select, far_select, mate_near,
        windows if halves else [],
    )
    mate_came = to_mate(mate_sum)
    far_came = to_far(far_sum)
    own_sum, near_sum = push_home(terms, home, near_select, mate_came)
    near_came = to_near(near_sum)
    if halves:
        near_crossed = to_near_crosswise(near_sum)
        far_came, _ = lax.optimization_barrier((far_came, near_sum))
    base = own_sum + far_came.astype(jnp.float32)
    if halves:
        half_base = base.astype(jnp.bfloat16)
        near_came, _ = lax.optimization_barrier((near_came, half_base))
        other_base = across_sub(half_base)
    down_check = (base + near_came.astype(jnp.float32)).astype(jnp.bfloat16)
    if halves:
        other_down = (
            other_base.astype(jnp.float32) + near_crossed.astype(jnp.float32)
        ).astype(jnp.bfloat16)
        return joined_product(down_inverse, down_check, other_down)
    return jnp.dot(
        down_inverse, lax.all_gather(down_check, "sub", axis=0, tiled=True),
        preferred_element_type=jnp.float32,
    ).astype(jnp.bfloat16)


def solution(mesh):
    in_specs = (
        P("sub", "tile"),
        P("sub", None),
        P(None, "sub", None),
        P("sub", None),
        P("tile", None),
        P("tile", None),
        P("tile"),
    )
    out_specs = P("sub", "tile")
    return jax.shard_map(shards, mesh=mesh, in_specs=in_specs, out_specs=out_specs, check_vma=False)
```

```python
import functools

import jax
import jax.numpy as jnp
from jax import lax
from jax.experimental import pallas as pl
from jax.experimental.pallas import tpu as pltpu
from jax.sharding import PartitionSpec as P

REACH = 2
CLASS_SHIFT = 10
CHUNK = 112
LANES = 128
WHOLE = pl.BlockSpec(memory_space=pltpu.VMEM)


def across_sub(shard):
    return lax.ppermute(shard, "sub", [(0, 1), (1, 0)])


def to_mate(value):
    count = lax.axis_size("tile")
    pairs = [(t, t ^ 1) for t in range(count) if t ^ 1 < count]
    return lax.ppermute(value, "tile", pairs)


def to_near(value):
    count = lax.axis_size("tile")
    pairs = [(t, t + 2 * (t % 2) - 1) for t in range(count)]
    return lax.ppermute(value, "tile", [(a, b) for a, b in pairs if 0 <= b < count])


def to_near_crosswise(value):
    count = lax.axis_size("tile")
    pairs = []
    for t in range(count):
        target = t + 2 * (t % 2) - 1
        if 0 <= target < count:
            pairs += [(2 * t + index, 2 * target + 1 - index) for index in range(2)]
    return lax.ppermute(value, ("tile", "sub"), pairs)


def to_far(value):
    count = lax.axis_size("tile")
    pairs = [(t, t + 4 * (t % 2) - 2) for t in range(count)]
    return lax.ppermute(value, "tile", [(a, b) for a, b in pairs if 0 <= b < count])


def away():
    return 2 * lax.rem(lax.axis_index("tile"), 2) - 1


def half_windows(shard_rows, depth, count):
    windows = []
    for index in range(count):
        low, high = index * shard_rows, (index + 1) * shard_rows
        start = low // LANES * LANES
        stop = min(pl.cdiv(high, LANES) * LANES, depth)
        windows.append((start, stop, low - start))
    return windows


def chunks(rows, size):
    return [(start, min(size, rows - start)) for start in range(0, rows, size)]


def pad_into(padded, offset, *refs):
    padded[...] = jnp.zeros(padded.shape, padded.dtype)
    for i, ref in enumerate(refs):
        rows, cells = ref.shape
        padded[offset : offset + rows, i * cells : (i + 1) * cells] = ref[...].astype(padded.dtype)


def joined_kernel(matrix_ref, own_ref, other_ref, out_ref, joined):
    rows = own_ref.shape[0]
    halves = [slice(0, rows), slice(rows, 2 * rows)]
    for index in range(2):
        def place(index=index):
            joined[halves[index], :] = own_ref[...].astype(jnp.float32)
            joined[halves[1 - index], :] = other_ref[...].astype(jnp.float32)
        pl.when(lax.axis_index("sub") == index)(place)
    out_ref[...] = jnp.dot(
        matrix_ref[...], joined[...].astype(jnp.bfloat16), preferred_element_type=jnp.float32
    ).astype(jnp.bfloat16)


def joined_product(matrix, own, other):
    rows, depth = matrix.shape
    cells = own.shape[1]
    return pl.pallas_call(
        joined_kernel,
        out_shape=jax.ShapeDtypeStruct((rows, cells), jnp.bfloat16),
        in_specs=[WHOLE] * 3,
        out_specs=WHOLE,
        scratch_shapes=[pltpu.VMEM((depth, cells), jnp.float32)],
        cost_estimate=pl.CostEstimate(
            flops=2 * rows * depth * cells, bytes_accessed=2 * rows * depth, transcendentals=0
        ),
        compiler_params=pltpu.CompilerParams(vmem_limit_bytes=8 << 20),
        name="joined",
    )(matrix, own, other)


def build_select(code, base, out_ref, column, classes):
    entries, cells = code.shape
    slots = (code & ((1 << CLASS_SHIFT) - 1)) - base
    kinds = code >> CLASS_SHIFT
    band = 32
    for low in range(0, cells, band):
        source = lax.broadcasted_iota(jnp.int32, (band, cells), 0) + low
        totals = [jnp.zeros((band, cells), jnp.bfloat16)] * classes
        for entry in range(entries):
            hit = jnp.where(slots[entry : entry + 1, :] == source, 1.0, 0.0).astype(jnp.bfloat16)
            for k in range(classes):
                used = jnp.where(kinds[entry : entry + 1, :] == k, 1.0, 0.0).astype(jnp.bfloat16)
                totals[k] = totals[k] + hit * used
        for k in range(classes):
            row = k * cells + low
            out_ref[row : row + band, column : column + cells] = totals[k]


def prepare_kernel(
    windows, part, operators_ref, own_ref, product_ref, padded
):
    classes = operators_ref.shape[1]

    for index, (low, high, offset) in enumerate(windows):
        def run(low=low, high=high, offset=offset):
            pad_into(padded, offset, own_ref)
            right = padded[: high - low, :].astype(jnp.bfloat16)
            for start, size in part:
                left = operators_ref[start : start + size, :, low:high]
                row = (start - part[0][0]) * classes
                product_ref[row : row + size * classes, :] = jnp.dot(
                    left.reshape(size * classes, high - low), right,
                    preferred_element_type=jnp.float32,
                )
        if len(windows) == 1:
            run()
        else:
            pl.when(lax.axis_index("sub") == index)(run)


def prepare(operators, own, windows, part):
    classes = operators.shape[1]
    cells = own.shape[1]
    span = max(high - low for low, high, _ in windows)
    rows = sum(size for _, size in part)
    return pl.pallas_call(
        functools.partial(prepare_kernel, windows, part),
        out_shape=jax.ShapeDtypeStruct((rows * classes, cells), jnp.float32),
        in_specs=[WHOLE] * 2,
        out_specs=WHOLE,
        scratch_shapes=[pltpu.VMEM((span, cells), jnp.float32)],
        cost_estimate=pl.CostEstimate(flops=1 << 32, bytes_accessed=0, transcendentals=0),
        compiler_params=pltpu.CompilerParams(vmem_limit_bytes=24 << 20),
        name="prepare",
    )(operators, own)


def home_kernel(code_ref, out_ref):
    cells = code_ref.shape[1]
    build_select(code_ref[...], REACH * cells, out_ref, 0, out_ref.shape[0] // cells)


def home_selection(code, classes):
    cells = code.shape[1]
    return pl.pallas_call(
        home_kernel,
        out_shape=jax.ShapeDtypeStruct((classes * cells, cells), jnp.bfloat16),
        in_specs=[WHOLE],
        out_specs=WHOLE,
        cost_estimate=pl.CostEstimate(flops=1 << 31, bytes_accessed=0, transcendentals=0),
        compiler_params=pltpu.CompilerParams(vmem_limit_bytes=8 << 20),
        name="home",
    )(code)


def select_kernel(mate_ref, near_ref, mate_near_ref, *select_refs):
    entries, cells = mate_ref.shape
    step = away()
    for ref, code, distance in zip(
        select_refs,
        (mate_ref[...], near_ref[:entries, :], near_ref[entries:, :], mate_near_ref[...]),
        (-step, step, 2 * step, -2 * step),
    ):
        build_select(code, (REACH - distance) * cells, ref, 0, ref.shape[0] // cells)


def selections(mate_code, near_codes, mate_near_code, classes):
    cells = mate_code.shape[1]
    select = jax.ShapeDtypeStruct((classes * cells, cells), jnp.bfloat16)
    return pl.pallas_call(
        select_kernel,
        out_shape=[select] * 4,
        in_specs=[WHOLE] * 3,
        out_specs=[WHOLE] * 4,
        cost_estimate=pl.CostEstimate(flops=1 << 20, bytes_accessed=0, transcendentals=0),
        compiler_params=pltpu.CompilerParams(vmem_limit_bytes=8 << 20),
        name="selections",
    )(mate_code, near_codes, mate_near_code)


def push_away_kernel(
    windows, held_ref, low_ref, high_ref, other_ref,
    mate_select_ref, far_select_ref, mate_near_ref,
    terms_ref, mate_ref, far_ref, padded, product,
):
    rows, classes, _ = held_ref.shape
    cells = far_ref.shape[1]
    split = low_ref.shape[0]

    def own_half(start, size):
        if start * classes < split:
            return low_ref[start * classes : (start + size) * classes, :]
        row = start * classes - split
        return high_ref[row : row + size * classes, :]

    def part_classes(source, start, size):
        for k in range(classes):
            term = source[pl.ds(start * classes + k, size, stride=classes), :]
            terms_ref[start : start + size, k * cells : (k + 1) * cells] = term.astype(jnp.bfloat16)

    for index, (low, high, offset) in enumerate(windows):
        def run(low=low, high=high, offset=offset):
            pad_into(padded, offset, other_ref)
            right = padded[: high - low, :].astype(jnp.bfloat16)
            for start, size in chunks(rows, CHUNK):
                left = held_ref[start : start + size, :, low:high]
                part = slice(start * classes, (start + size) * classes)
                product[part, :] = own_half(start, size) + jnp.dot(
                    left.reshape(size * classes, high - low), right,
                    preferred_element_type=jnp.float32,
                )
                part_classes(product, start, size)
        pl.when(lax.axis_index("sub") != index)(run)

    if not windows:
        for start, size in chunks(rows, CHUNK):
            product[start * classes : (start + size) * classes, :] = own_half(start, size)
            part_classes(product, start, size)

    terms = terms_ref[...]
    chosen = jnp.concatenate([mate_select_ref[...], far_select_ref[...], mate_near_ref[...]], axis=1)
    total = jnp.dot(terms, chosen, preferred_element_type=jnp.float32).astype(jnp.bfloat16)
    mate_ref[:, :cells] = total[:, :cells]
    far_ref[...] = total[:, cells : 2 * cells]
    mate_ref[:, cells:] = total[:, 2 * cells :]


def push_away(held, low, high, other, mate_select, far_select, mate_near, windows):
    rows, classes, depth = held.shape
    cells = other.shape[1]
    span = max([high - low for low, high, _ in windows], default=LANES)
    return pl.pallas_call(
        functools.partial(push_away_kernel, windows),
        out_shape=[
            jax.ShapeDtypeStruct((rows, classes * cells), jnp.bfloat16),
            jax.ShapeDtypeStruct((rows, 2 * cells), jnp.bfloat16),
            jax.ShapeDtypeStruct((rows, cells), jnp.bfloat16),
        ],
        in_specs=[WHOLE] * 7,
        out_specs=[WHOLE] * 3,
        scratch_shapes=[
            pltpu.VMEM((span, cells), jnp.float32),
            pltpu.VMEM((rows * classes, cells), jnp.float32),
        ],
        cost_estimate=pl.CostEstimate(
            flops=2 * rows * classes * cells * (span + 3 * cells),
            bytes_accessed=2 * rows * classes * depth,
            transcendentals=0,
        ),
        compiler_params=pltpu.CompilerParams(vmem_limit_bytes=32 << 20),
        name="push_away",
    )(held, low, high, other, mate_select, far_select, mate_near)


def push_home_kernel(terms_ref, home_ref, near_select_ref, came_ref, own_ref, near_ref):
    cells = near_ref.shape[1]
    chosen = jnp.concatenate([home_ref[...], near_select_ref[...]], axis=1)
    total = jnp.dot(terms_ref[...], chosen, preferred_element_type=jnp.float32)
    total = total + came_ref[...].astype(jnp.float32)
    own_ref[...] = total[:, :cells]
    near_ref[...] = total[:, cells:].astype(jnp.bfloat16)


def push_home(terms, home, near_select, came):
    rows = terms.shape[0]
    cells = home.shape[1]
    return pl.pallas_call(
        push_home_kernel,
        out_shape=[
            jax.ShapeDtypeStruct((rows, cells), jnp.float32),
            jax.ShapeDtypeStruct((rows, cells), jnp.bfloat16),
        ],
        in_specs=[WHOLE] * 4,
        out_specs=[WHOLE] * 2,
        cost_estimate=pl.CostEstimate(
            flops=2 * terms.size * 2 * cells, bytes_accessed=4 * terms.size, transcendentals=0
        ),
        compiler_params=pltpu.CompilerParams(vmem_limit_bytes=16 << 20),
        name="push_home",
    )(terms, home, near_select, came)


def shards(up_check, up_inverse, translate, down_inverse, list_slot, list_class, list_count):
    classes, rows, depth = translate.shape
    cells, entries = list_slot.shape
    halves = lax.axis_size("sub") == 2

    if halves:
        other_check = across_sub(up_check)
        list_slot, up_check = lax.optimization_barrier((list_slot, up_check))

    active = lax.broadcasted_iota(jnp.int32, (entries, cells), 0) < list_count[None, :]
    code = jnp.where(active, (list_class.T << CLASS_SHIFT) + list_slot.T, -1)
    mate_code, home = lax.optimization_barrier((to_mate(code), home_selection(code, classes)))
    near_codes = to_near(jnp.concatenate([code, mate_code], axis=0))

    operators = jnp.transpose(translate, (1, 0, 2))
    if halves:
        windows = half_windows(rows, depth, 2)
        equivalent = joined_product(up_inverse, up_check, other_check)
        other = across_sub(equivalent)
    else:
        windows = [(0, depth, 0)]
        equivalent = lax.all_gather(
            jnp.dot(
                up_inverse, lax.all_gather(up_check, "sub", axis=0, tiled=True),
                preferred_element_type=jnp.float32,
            ).astype(jnp.bfloat16),
            "sub", axis=0, tiled=True,
        )
        other = equivalent

    parts = chunks(rows, CHUNK)
    half = pl.cdiv(len(parts), 2)
    low = prepare(operators, equivalent, windows, parts[:half])
    near_codes, low = lax.optimization_barrier((near_codes, low))
    mate_near_code = to_mate(near_codes[:entries])
    high = prepare(operators, equivalent, windows, parts[half:])
    mate_near_code, high = lax.optimization_barrier((mate_near_code, high))
    mate_select, near_select, far_select, mate_near = selections(
        mate_code, near_codes, mate_near_code, classes
    )
    terms, mate_sum, far_sum = push_away(
        operators, low, high, other, mate_select, far_select, mate_near,
        windows if halves else [],
    )
    mate_came = to_mate(mate_sum)
    far_came = to_far(far_sum)
    own_sum, near_sum = push_home(terms, home, near_select, mate_came)
    near_came = to_near(near_sum)
    if halves:
        near_crossed = to_near_crosswise(near_sum)
        far_came, _ = lax.optimization_barrier((far_came, near_sum))
    base = own_sum + far_came.astype(jnp.float32)
    if halves:
        half_base = base.astype(jnp.bfloat16)
        near_came, _ = lax.optimization_barrier((near_came, half_base))
        other_base = across_sub(half_base)
    down_check = (base + near_came.astype(jnp.float32)).astype(jnp.bfloat16)
    if halves:
        other_down = (
            other_base.astype(jnp.float32) + near_crossed.astype(jnp.float32)
        ).astype(jnp.bfloat16)
        return joined_product(down_inverse, down_check, other_down)
    return jnp.dot(
        down_inverse, lax.all_gather(down_check, "sub", axis=0, tiled=True),
        preferred_element_type=jnp.float32,
    ).astype(jnp.bfloat16)


def solution(mesh):
    in_specs = (
        P("sub", "tile"),
        P("sub", None),
        P(None, "sub", None),
        P("sub", None),
        P("tile", None),
        P("tile", None),
        P("tile"),
    )
    out_specs = P("sub", "tile")
    return jax.shard_map(shards, mesh=mesh, in_specs=in_specs, out_specs=out_specs, check_vma=False)
```

```python
import functools

import jax
import jax.numpy as jnp
from jax import lax
from jax.experimental import pallas as pl
from jax.experimental.pallas import tpu as pltpu
from jax.sharding import PartitionSpec as P

REACH = 2
CLASS_SHIFT = 10
CHUNK = 112
LANES = 128
WHOLE = pl.BlockSpec(memory_space=pltpu.VMEM)


def across_sub(shard):
    return lax.ppermute(shard, "sub", [(0, 1), (1, 0)])


def to_mate(value):
    count = lax.axis_size("tile")
    pairs = [(t, t ^ 1) for t in range(count) if t ^ 1 < count]
    return lax.ppermute(value, "tile", pairs)


def to_near(value):
    count = lax.axis_size("tile")
    pairs = [(t, t + 2 * (t % 2) - 1) for t in range(count)]
    return lax.ppermute(value, "tile", [(a, b) for a, b in pairs if 0 <= b < count])


def to_near_crosswise(value):
    count = lax.axis_size("tile")
    pairs = []
    for t in range(count):
        target = t + 2 * (t % 2) - 1
        if 0 <= target < count:
            pairs += [(2 * t + index, 2 * target + 1 - index) for index in range(2)]
    return lax.ppermute(value, ("tile", "sub"), pairs)


def to_far(value):
    count = lax.axis_size("tile")
    pairs = [(t, t + 4 * (t % 2) - 2) for t in range(count)]
    return lax.ppermute(value, "tile", [(a, b) for a, b in pairs if 0 <= b < count])


def away():
    return 2 * lax.rem(lax.axis_index("tile"), 2) - 1


def half_windows(shard_rows, depth, count):
    windows = []
    for index in range(count):
        low, high = index * shard_rows, (index + 1) * shard_rows
        start = low // LANES * LANES
        stop = min(pl.cdiv(high, LANES) * LANES, depth)
        windows.append((start, stop, low - start))
    return windows


def chunks(rows, size):
    return [(start, min(size, rows - start)) for start in range(0, rows, size)]


def pad_into(padded, offset, *refs):
    padded[...] = jnp.zeros(padded.shape, padded.dtype)
    for i, ref in enumerate(refs):
        rows, cells = ref.shape
        padded[offset : offset + rows, i * cells : (i + 1) * cells] = ref[...].astype(padded.dtype)


def joined_kernel(matrix_ref, own_ref, other_ref, out_ref, joined):
    rows = own_ref.shape[0]
    halves = [slice(0, rows), slice(rows, 2 * rows)]
    for index in range(2):
        def place(index=index):
            joined[halves[index], :] = own_ref[...].astype(jnp.float32)
            joined[halves[1 - index], :] = other_ref[...].astype(jnp.float32)
        pl.when(lax.axis_index("sub") == index)(place)
    out_ref[...] = jnp.dot(
        matrix_ref[...], joined[...].astype(jnp.bfloat16), preferred_element_type=jnp.float32
    ).astype(jnp.bfloat16)


def joined_product(matrix, own, other):
    rows, depth = matrix.shape
    cells = own.shape[1]
    return pl.pallas_call(
        joined_kernel,
        out_shape=jax.ShapeDtypeStruct((rows, cells), jnp.bfloat16),
        in_specs=[WHOLE] * 3,
        out_specs=WHOLE,
        scratch_shapes=[pltpu.VMEM((depth, cells), jnp.float32)],
        cost_estimate=pl.CostEstimate(
            flops=2 * rows * depth * cells, bytes_accessed=2 * rows * depth, transcendentals=0
        ),
        compiler_params=pltpu.CompilerParams(vmem_limit_bytes=8 << 20),
        name="joined",
    )(matrix, own, other)


def build_select(code, base, out_ref, column, classes):
    entries, cells = code.shape
    slots = (code & ((1 << CLASS_SHIFT) - 1)) - base
    kinds = code >> CLASS_SHIFT
    band = 32
    for low in range(0, cells, band):
        source = lax.broadcasted_iota(jnp.int32, (band, cells), 0) + low
        totals = [jnp.zeros((band, cells), jnp.bfloat16)] * classes
        for entry in range(entries):
            hit = jnp.where(slots[entry : entry + 1, :] == source, 1.0, 0.0).astype(jnp.bfloat16)
            for k in range(classes):
                used = jnp.where(kinds[entry : entry + 1, :] == k, 1.0, 0.0).astype(jnp.bfloat16)
                totals[k] = totals[k] + hit * used
        for k in range(classes):
            row = k * cells + low
            out_ref[row : row + band, column : column + cells] = totals[k]


def prepare_kernel(
    windows, part, operators_ref, own_ref, product_ref, padded
):
    classes = operators_ref.shape[1]

    for index, (low, high, offset) in enumerate(windows):
        def run(low=low, high=high, offset=offset):
            pad_into(padded, offset, own_ref)
            right = padded[: high - low, :].astype(jnp.bfloat16)
            for start, size in part:
                left = operators_ref[start : start + size, :, low:high]
                row = (start - part[0][0]) * classes
                product_ref[row : row + size * classes, :] = jnp.dot(
                    left.reshape(size * classes, high - low), right,
                    preferred_element_type=jnp.float32,
                )
        if len(windows) == 1:
            run()
        else:
            pl.when(lax.axis_index("sub") == index)(run)


def prepare(operators, own, windows, part):
    classes = operators.shape[1]
    cells = own.shape[1]
    span = max(high - low for low, high, _ in windows)
    rows = sum(size for _, size in part)
    return pl.pallas_call(
        functools.partial(prepare_kernel, windows, part),
        out_shape=jax.ShapeDtypeStruct((rows * classes, cells), jnp.float32),
        in_specs=[WHOLE] * 2,
        out_specs=WHOLE,
        scratch_shapes=[pltpu.VMEM((span, cells), jnp.float32)],
        cost_estimate=pl.CostEstimate(flops=1 << 32, bytes_accessed=0, transcendentals=0),
        compiler_params=pltpu.CompilerParams(vmem_limit_bytes=24 << 20),
        name="prepare",
    )(operators, own)


def home_kernel(code_ref, out_ref):
    cells = code_ref.shape[1]
    build_select(code_ref[...], REACH * cells, out_ref, 0, out_ref.shape[0] // cells)


def home_selection(code, classes):
    cells = code.shape[1]
    return pl.pallas_call(
        home_kernel,
        out_shape=jax.ShapeDtypeStruct((classes * cells, cells), jnp.bfloat16),
        in_specs=[WHOLE],
        out_specs=WHOLE,
        cost_estimate=pl.CostEstimate(flops=1 << 31, bytes_accessed=0, transcendentals=0),
        compiler_params=pltpu.CompilerParams(vmem_limit_bytes=8 << 20),
        name="home",
    )(code)


def select_kernel(mate_ref, near_ref, mate_near_ref, *select_refs):
    entries, cells = mate_ref.shape
    step = away()
    for ref, code, distance in zip(
        select_refs,
        (mate_ref[...], near_ref[:entries, :], near_ref[entries:, :], mate_near_ref[...]),
        (-step, step, 2 * step, -2 * step),
    ):
        build_select(code, (REACH - distance) * cells, ref, 0, ref.shape[0] // cells)


def selections(mate_code, near_codes, mate_near_code, classes):
    cells = mate_code.shape[1]
    select = jax.ShapeDtypeStruct((classes * cells, cells), jnp.bfloat16)
    return pl.pallas_call(
        select_kernel,
        out_shape=[select] * 4,
        in_specs=[WHOLE] * 3,
        out_specs=[WHOLE] * 4,
        cost_estimate=pl.CostEstimate(flops=1 << 20, bytes_accessed=0, transcendentals=0),
        compiler_params=pltpu.CompilerParams(vmem_limit_bytes=8 << 20),
        name="selections",
    )(mate_code, near_codes, mate_near_code)


def push_away_kernel(
    windows, held_ref, low_ref, high_ref, other_ref,
    mate_select_ref, far_select_ref, mate_near_ref,
    terms_ref, mate_ref, far_ref, padded, product,
):
    rows, classes, _ = held_ref.shape
    cells = far_ref.shape[1]
    split = low_ref.shape[0]

    def own_half(start, size):
        if start * classes < split:
            return low_ref[start * classes : (start + size) * classes, :]
        row = start * classes - split
        return high_ref[row : row + size * classes, :]

    def part_classes(source, start, size):
        for k in range(classes):
            term = source[pl.ds(start * classes + k, size, stride=classes), :]
            terms_ref[start : start + size, k * cells : (k + 1) * cells] = term.astype(jnp.bfloat16)

    for index, (low, high, offset) in enumerate(windows):
        def run(low=low, high=high, offset=offset):
            pad_into(padded, offset, other_ref)
            right = padded[: high - low, :].astype(jnp.bfloat16)
            for start, size in chunks(rows, CHUNK):
                left = held_ref[start : start + size, :, low:high]
                part = slice(start * classes, (start + size) * classes)
                product[part, :] = own_half(start, size) + jnp.dot(
                    left.reshape(size * classes, high - low), right,
                    preferred_element_type=jnp.float32,
                )
                part_classes(product, start, size)
        pl.when(lax.axis_index("sub") != index)(run)

    if not windows:
        for start, size in chunks(rows, CHUNK):
            product[start * classes : (start + size) * classes, :] = own_half(start, size)
            part_classes(product, start, size)

    terms = terms_ref[...]
    chosen = jnp.concatenate([mate_select_ref[...], far_select_ref[...], mate_near_ref[...]], axis=1)
    total = jnp.dot(terms, chosen, preferred_element_type=jnp.float32).astype(jnp.bfloat16)
    mate_ref[:, :cells] = total[:, :cells]
    far_ref[...] = total[:, cells : 2 * cells]
    mate_ref[:, cells:] = total[:, 2 * cells :]


def push_away(held, low, high, other, mate_select, far_select, mate_near, windows):
    rows, classes, depth = held.shape
    cells = other.shape[1]
    span = max([high - low for low, high, _ in windows], default=LANES)
    return pl.pallas_call(
        functools.partial(push_away_kernel, windows),
        out_shape=[
            jax.ShapeDtypeStruct((rows, classes * cells), jnp.bfloat16),
            jax.ShapeDtypeStruct((rows, 2 * cells), jnp.bfloat16),
            jax.ShapeDtypeStruct((rows, cells), jnp.bfloat16),
        ],
        in_specs=[WHOLE] * 7,
        out_specs=[WHOLE] * 3,
        scratch_shapes=[
            pltpu.VMEM((span, cells), jnp.float32),
            pltpu.VMEM((rows * classes, cells), jnp.float32),
        ],
        cost_estimate=pl.CostEstimate(
            flops=2 * rows * classes * cells * (span + 3 * cells),
            bytes_accessed=2 * rows * classes * depth,
            transcendentals=0,
        ),
        compiler_params=pltpu.CompilerParams(vmem_limit_bytes=32 << 20),
        name="push_away",
    )(held, low, high, other, mate_select, far_select, mate_near)


def push_home_kernel(column, terms_ref, select_ref, came_ref, out_ref):
    cells = out_ref.shape[1]
    total = jnp.dot(terms_ref[...], select_ref[...], preferred_element_type=jnp.float32)
    came = came_ref[:, column * cells : (column + 1) * cells]
    out_ref[...] = (total + came.astype(jnp.float32)).astype(out_ref.dtype)


def push_home(terms, select, came, column, dtype):
    rows = terms.shape[0]
    cells = select.shape[1]
    return pl.pallas_call(
        functools.partial(push_home_kernel, column),
        out_shape=jax.ShapeDtypeStruct((rows, cells), dtype),
        in_specs=[WHOLE] * 3,
        out_specs=WHOLE,
        cost_estimate=pl.CostEstimate(
            flops=2 * terms.size * cells, bytes_accessed=4 * terms.size, transcendentals=0
        ),
        compiler_params=pltpu.CompilerParams(vmem_limit_bytes=16 << 20),
        name="push_home",
    )(terms, select, came)


def shards(up_check, up_inverse, translate, down_inverse, list_slot, list_class, list_count):
    classes, rows, depth = translate.shape
    cells, entries = list_slot.shape
    halves = lax.axis_size("sub") == 2

    if halves:
        other_check = across_sub(up_check)
        list_slot, up_check = lax.optimization_barrier((list_slot, up_check))

    active = lax.broadcasted_iota(jnp.int32, (entries, cells), 0) < list_count[None, :]
    code = jnp.where(active, (list_class.T << CLASS_SHIFT) + list_slot.T, -1)
    mate_code, home = lax.optimization_barrier((to_mate(code), home_selection(code, classes)))
    near_codes = to_near(jnp.concatenate([code, mate_code], axis=0))

    operators = jnp.transpose(translate, (1, 0, 2))
    if halves:
        windows = half_windows(rows, depth, 2)
        equivalent = joined_product(up_inverse, up_check, other_check)
        other = across_sub(equivalent)
    else:
        windows = [(0, depth, 0)]
        equivalent = lax.all_gather(
            jnp.dot(
                up_inverse, lax.all_gather(up_check, "sub", axis=0, tiled=True),
                preferred_element_type=jnp.float32,
            ).astype(jnp.bfloat16),
            "sub", axis=0, tiled=True,
        )
        other = equivalent

    parts = chunks(rows, CHUNK)
    half = pl.cdiv(len(parts), 2)
    low = prepare(operators, equivalent, windows, parts[:half])
    near_codes, low = lax.optimization_barrier((near_codes, low))
    mate_near_code = to_mate(near_codes[:entries])
    high = prepare(operators, equivalent, windows, parts[half:])
    mate_near_code, high = lax.optimization_barrier((mate_near_code, high))
    mate_select, near_select, far_select, mate_near = selections(
        mate_code, near_codes, mate_near_code, classes
    )
    terms, mate_sum, far_sum = push_away(
        operators, low, high, other, mate_select, far_select, mate_near,
        windows if halves else [],
    )
    mate_came = to_mate(mate_sum)
    far_came = to_far(far_sum)
    near_sum = push_home(terms, near_select, mate_came, 1, jnp.bfloat16)
    terms, near_sum = lax.optimization_barrier((terms, near_sum))
    own_sum = push_home(terms, home, mate_came, 0, jnp.float32)
    near_came = to_near(near_sum)
    if halves:
        near_crossed = to_near_crosswise(near_sum)
        far_came, _ = lax.optimization_barrier((far_came, near_sum))
    base = own_sum + far_came.astype(jnp.float32)
    if halves:
        half_base = base.astype(jnp.bfloat16)
        near_came, _ = lax.optimization_barrier((near_came, half_base))
        other_base = across_sub(half_base)
    down_check = (base + near_came.astype(jnp.float32)).astype(jnp.bfloat16)
    if halves:
        other_down = (
            other_base.astype(jnp.float32) + near_crossed.astype(jnp.float32)
        ).astype(jnp.bfloat16)
        return joined_product(down_inverse, down_check, other_down)
    return jnp.dot(
        down_inverse, lax.all_gather(down_check, "sub", axis=0, tiled=True),
        preferred_element_type=jnp.float32,
    ).astype(jnp.bfloat16)


def solution(mesh):
    in_specs = (
        P("sub", "tile"),
        P("sub", None),
        P(None, "sub", None),
        P("sub", None),
        P("tile", None),
        P("tile", None),
        P("tile"),
    )
    out_specs = P("sub", "tile")
    return jax.shard_map(shards, mesh=mesh, in_specs=in_specs, out_specs=out_specs, check_vma=False)
```

```python
import functools

import jax
import jax.numpy as jnp
from jax import lax
from jax.experimental import pallas as pl
from jax.experimental.pallas import tpu as pltpu
from jax.sharding import PartitionSpec as P

REACH = 2
CLASS_SHIFT = 10
CHUNK = 112
LANES = 128
WHOLE = pl.BlockSpec(memory_space=pltpu.VMEM)


def across_sub(shard):
    return lax.ppermute(shard, "sub", [(0, 1), (1, 0)])


def to_mate(value):
    count = lax.axis_size("tile")
    pairs = [(t, t ^ 1) for t in range(count) if t ^ 1 < count]
    return lax.ppermute(value, "tile", pairs)


def to_near(value):
    count = lax.axis_size("tile")
    pairs = [(t, t + 2 * (t % 2) - 1) for t in range(count)]
    return lax.ppermute(value, "tile", [(a, b) for a, b in pairs if 0 <= b < count])


def to_near_crosswise(value):
    count = lax.axis_size("tile")
    pairs = []
    for t in range(count):
        target = t + 2 * (t % 2) - 1
        if 0 <= target < count:
            pairs += [(2 * t + index, 2 * target + 1 - index) for index in range(2)]
    return lax.ppermute(value, ("tile", "sub"), pairs)


def to_far(value):
    count = lax.axis_size("tile")
    pairs = [(t, t + 4 * (t % 2) - 2) for t in range(count)]
    return lax.ppermute(value, "tile", [(a, b) for a, b in pairs if 0 <= b < count])


def away():
    return 2 * lax.rem(lax.axis_index("tile"), 2) - 1


def half_windows(shard_rows, depth, count):
    windows = []
    for index in range(count):
        low, high = index * shard_rows, (index + 1) * shard_rows
        start = low // LANES * LANES
        stop = min(pl.cdiv(high, LANES) * LANES, depth)
        windows.append((start, stop, low - start))
    return windows


def chunks(rows, size):
    return [(start, min(size, rows - start)) for start in range(0, rows, size)]


def pad_into(padded, offset, *refs):
    padded[...] = jnp.zeros(padded.shape, padded.dtype)
    for i, ref in enumerate(refs):
        rows, cells = ref.shape
        padded[offset : offset + rows, i * cells : (i + 1) * cells] = ref[...].astype(padded.dtype)


def joined_kernel(matrix_ref, own_ref, other_ref, out_ref, joined):
    rows = own_ref.shape[0]
    halves = [slice(0, rows), slice(rows, 2 * rows)]
    for index in range(2):
        def place(index=index):
            joined[halves[index], :] = own_ref[...].astype(jnp.float32)
            joined[halves[1 - index], :] = other_ref[...].astype(jnp.float32)
        pl.when(lax.axis_index("sub") == index)(place)
    out_ref[...] = jnp.dot(
        matrix_ref[...], joined[...].astype(jnp.bfloat16), preferred_element_type=jnp.float32
    ).astype(jnp.bfloat16)


def joined_product(matrix, own, other):
    rows, depth = matrix.shape
    cells = own.shape[1]
    return pl.pallas_call(
        joined_kernel,
        out_shape=jax.ShapeDtypeStruct((rows, cells), jnp.bfloat16),
        in_specs=[WHOLE] * 3,
        out_specs=WHOLE,
        scratch_shapes=[pltpu.VMEM((depth, cells), jnp.float32)],
        cost_estimate=pl.CostEstimate(
            flops=2 * rows * depth * cells, bytes_accessed=2 * rows * depth, transcendentals=0
        ),
        compiler_params=pltpu.CompilerParams(vmem_limit_bytes=8 << 20),
        name="joined",
    )(matrix, own, other)


def first_kernel(windows, matrix_ref, own_ref, out_ref, padded):
    for index, (low, high, offset) in enumerate(windows):
        def run(low=low, high=high, offset=offset):
            pad_into(padded, offset, own_ref)
            out_ref[...] = jnp.dot(
                matrix_ref[:, low:high], padded[: high - low, :].astype(jnp.bfloat16),
                preferred_element_type=jnp.float32,
            )
        pl.when(lax.axis_index("sub") == index)(run)


def first(matrix, own, windows):
    rows, depth = matrix.shape
    cells = own.shape[1]
    span = max(high - low for low, high, _ in windows)
    return pl.pallas_call(
        functools.partial(first_kernel, windows),
        out_shape=jax.ShapeDtypeStruct((rows, cells), jnp.float32),
        in_specs=[WHOLE] * 2,
        out_specs=WHOLE,
        scratch_shapes=[pltpu.VMEM((span, cells), jnp.float32)],
        cost_estimate=pl.CostEstimate(
            flops=2 * rows * depth * cells, bytes_accessed=4 * rows * depth, transcendentals=0
        ),
        compiler_params=pltpu.CompilerParams(vmem_limit_bytes=16 << 20),
        name="first",
    )(matrix, own)


def rest_kernel(windows, matrix_ref, part_ref, other_ref, out_ref, padded):
    for index, (low, high, offset) in enumerate(windows):
        def run(low=low, high=high, offset=offset):
            pad_into(padded, offset, other_ref)
            out_ref[...] = (
                part_ref[...]
                + jnp.dot(
                    matrix_ref[:, low:high], padded[: high - low, :].astype(jnp.bfloat16),
                    preferred_element_type=jnp.float32,
                )
            ).astype(jnp.bfloat16)
        pl.when(lax.axis_index("sub") != index)(run)


def rest(matrix, part, other, windows):
    rows, depth = matrix.shape
    cells = other.shape[1]
    span = max(high - low for low, high, _ in windows)
    return pl.pallas_call(
        functools.partial(rest_kernel, windows),
        out_shape=jax.ShapeDtypeStruct((rows, cells), jnp.bfloat16),
        in_specs=[WHOLE] * 3,
        out_specs=WHOLE,
        scratch_shapes=[pltpu.VMEM((span, cells), jnp.float32)],
        cost_estimate=pl.CostEstimate(
            flops=2 * rows * span * cells, bytes_accessed=2 * rows * span, transcendentals=0
        ),
        compiler_params=pltpu.CompilerParams(vmem_limit_bytes=16 << 20),
        name="rest",
    )(matrix, part, other)


def build_select(code, base, out_ref, column, classes):
    entries, cells = code.shape
    slots = (code & ((1 << CLASS_SHIFT) - 1)) - base
    kinds = code >> CLASS_SHIFT
    band = 32
    for low in range(0, cells, band):
        source = lax.broadcasted_iota(jnp.int32, (band, cells), 0) + low
        totals = [jnp.zeros((band, cells), jnp.bfloat16)] * classes
        for entry in range(entries):
            hit = jnp.where(slots[entry : entry + 1, :] == source, 1.0, 0.0).astype(jnp.bfloat16)
            for k in range(classes):
                used = jnp.where(kinds[entry : entry + 1, :] == k, 1.0, 0.0).astype(jnp.bfloat16)
                totals[k] = totals[k] + hit * used
        for k in range(classes):
            row = k * cells + low
            out_ref[row : row + band, column : column + cells] = totals[k]


def prepare_kernel(
    windows, part, operators_ref, own_ref, product_ref, padded
):
    classes = operators_ref.shape[1]

    for index, (low, high, offset) in enumerate(windows):
        def run(low=low, high=high, offset=offset):
            pad_into(padded, offset, own_ref)
            right = padded[: high - low, :].astype(jnp.bfloat16)
            for start, size in part:
                left = operators_ref[start : start + size, :, low:high]
                row = (start - part[0][0]) * classes
                product_ref[row : row + size * classes, :] = jnp.dot(
                    left.reshape(size * classes, high - low), right,
                    preferred_element_type=jnp.float32,
                )
        if len(windows) == 1:
            run()
        else:
            pl.when(lax.axis_index("sub") == index)(run)


def prepare(operators, own, windows, part):
    classes = operators.shape[1]
    cells = own.shape[1]
    span = max(high - low for low, high, _ in windows)
    rows = sum(size for _, size in part)
    return pl.pallas_call(
        functools.partial(prepare_kernel, windows, part),
        out_shape=jax.ShapeDtypeStruct((rows * classes, cells), jnp.float32),
        in_specs=[WHOLE] * 2,
        out_specs=WHOLE,
        scratch_shapes=[pltpu.VMEM((span, cells), jnp.float32)],
        cost_estimate=pl.CostEstimate(flops=1 << 32, bytes_accessed=0, transcendentals=0),
        compiler_params=pltpu.CompilerParams(vmem_limit_bytes=24 << 20),
        name="prepare",
    )(operators, own)


def home_kernel(code_ref, out_ref):
    cells = code_ref.shape[1]
    build_select(code_ref[...], REACH * cells, out_ref, 0, out_ref.shape[0] // cells)


def home_selection(code, classes):
    cells = code.shape[1]
    return pl.pallas_call(
        home_kernel,
        out_shape=jax.ShapeDtypeStruct((classes * cells, cells), jnp.bfloat16),
        in_specs=[WHOLE],
        out_specs=WHOLE,
        cost_estimate=pl.CostEstimate(flops=1 << 31, bytes_accessed=0, transcendentals=0),
        compiler_params=pltpu.CompilerParams(vmem_limit_bytes=8 << 20),
        name="home",
    )(code)


def select_kernel(mate_ref, near_ref, mate_near_ref, *select_refs):
    entries, cells = mate_ref.shape
    step = away()
    for ref, code, distance in zip(
        select_refs,
        (mate_ref[...], near_ref[:entries, :], near_ref[entries:, :], mate_near_ref[...]),
        (-step, step, 2 * step, -2 * step),
    ):
        build_select(code, (REACH - distance) * cells, ref, 0, ref.shape[0] // cells)


def selections(mate_code, near_codes, mate_near_code, classes):
    cells = mate_code.shape[1]
    select = jax.ShapeDtypeStruct((classes * cells, cells), jnp.bfloat16)
    return pl.pallas_call(
        select_kernel,
        out_shape=[select] * 4,
        in_specs=[WHOLE] * 3,
        out_specs=[WHOLE] * 4,
        cost_estimate=pl.CostEstimate(flops=1 << 20, bytes_accessed=0, transcendentals=0),
        compiler_params=pltpu.CompilerParams(vmem_limit_bytes=8 << 20),
        name="selections",
    )(mate_code, near_codes, mate_near_code)


def push_away_kernel(
    windows, held_ref, low_ref, high_ref, other_ref,
    mate_select_ref, far_select_ref, mate_near_ref,
    terms_ref, mate_ref, far_ref, padded, product,
):
    rows, classes, _ = held_ref.shape
    cells = far_ref.shape[1]
    split = low_ref.shape[0]

    def own_half(start, size):
        if start * classes < split:
            return low_ref[start * classes : (start + size) * classes, :]
        row = start * classes - split
        return high_ref[row : row + size * classes, :]

    def part_classes(source, start, size):
        for k in range(classes):
            term = source[pl.ds(start * classes + k, size, stride=classes), :]
            terms_ref[start : start + size, k * cells : (k + 1) * cells] = term.astype(jnp.bfloat16)

    for index, (low, high, offset) in enumerate(windows):
        def run(low=low, high=high, offset=offset):
            pad_into(padded, offset, other_ref)
            right = padded[: high - low, :].astype(jnp.bfloat16)
            for start, size in chunks(rows, CHUNK):
                left = held_ref[start : start + size, :, low:high]
                part = slice(start * classes, (start + size) * classes)
                product[part, :] = own_half(start, size) + jnp.dot(
                    left.reshape(size * classes, high - low), right,
                    preferred_element_type=jnp.float32,
                )
                part_classes(product, start, size)
        pl.when(lax.axis_index("sub") != index)(run)

    if not windows:
        for start, size in chunks(rows, CHUNK):
            product[start * classes : (start + size) * classes, :] = own_half(start, size)
            part_classes(product, start, size)

    terms = terms_ref[...]
    chosen = jnp.concatenate([mate_select_ref[...], far_select_ref[...], mate_near_ref[...]], axis=1)
    total = jnp.dot(terms, chosen, preferred_element_type=jnp.float32).astype(jnp.bfloat16)
    mate_ref[:, :cells] = total[:, :cells]
    far_ref[...] = total[:, cells : 2 * cells]
    mate_ref[:, cells:] = total[:, 2 * cells :]


def push_away(held, low, high, other, mate_select, far_select, mate_near, windows):
    rows, classes, depth = held.shape
    cells = other.shape[1]
    span = max([high - low for low, high, _ in windows], default=LANES)
    return pl.pallas_call(
        functools.partial(push_away_kernel, windows),
        out_shape=[
            jax.ShapeDtypeStruct((rows, classes * cells), jnp.bfloat16),
            jax.ShapeDtypeStruct((rows, 2 * cells), jnp.bfloat16),
            jax.ShapeDtypeStruct((rows, cells), jnp.bfloat16),
        ],
        in_specs=[WHOLE] * 7,
        out_specs=[WHOLE] * 3,
        scratch_shapes=[
            pltpu.VMEM((span, cells), jnp.float32),
            pltpu.VMEM((rows * classes, cells), jnp.float32),
        ],
        cost_estimate=pl.CostEstimate(
            flops=2 * rows * classes * cells * (span + 3 * cells),
            bytes_accessed=2 * rows * classes * depth,
            transcendentals=0,
        ),
        compiler_params=pltpu.CompilerParams(vmem_limit_bytes=32 << 20),
        name="push_away",
    )(held, low, high, other, mate_select, far_select, mate_near)


def push_home_kernel(terms_ref, home_ref, near_select_ref, came_ref, own_ref, near_ref):
    cells = near_ref.shape[1]
    chosen = jnp.concatenate([home_ref[...], near_select_ref[...]], axis=1)
    total = jnp.dot(terms_ref[...], chosen, preferred_element_type=jnp.float32)
    total = total + came_ref[...].astype(jnp.float32)
    own_ref[...] = total[:, :cells]
    near_ref[...] = total[:, cells:].astype(jnp.bfloat16)


def push_home(terms, home, near_select, came):
    rows = terms.shape[0]
    cells = home.shape[1]
    return pl.pallas_call(
        push_home_kernel,
        out_shape=[
            jax.ShapeDtypeStruct((rows, cells), jnp.float32),
            jax.ShapeDtypeStruct((rows, cells), jnp.bfloat16),
        ],
        in_specs=[WHOLE] * 4,
        out_specs=[WHOLE] * 2,
        cost_estimate=pl.CostEstimate(
            flops=2 * terms.size * 2 * cells, bytes_accessed=4 * terms.size, transcendentals=0
        ),
        compiler_params=pltpu.CompilerParams(vmem_limit_bytes=16 << 20),
        name="push_home",
    )(terms, home, near_select, came)


def shards(up_check, up_inverse, translate, down_inverse, list_slot, list_class, list_count):
    classes, rows, depth = translate.shape
    cells, entries = list_slot.shape
    halves = lax.axis_size("sub") == 2

    if halves:
        other_check = across_sub(up_check)
        list_slot, up_check = lax.optimization_barrier((list_slot, up_check))

    active = lax.broadcasted_iota(jnp.int32, (entries, cells), 0) < list_count[None, :]
    code = jnp.where(active, (list_class.T << CLASS_SHIFT) + list_slot.T, -1)
    mate_code, home = lax.optimization_barrier((to_mate(code), home_selection(code, classes)))
    near_codes = to_near(jnp.concatenate([code, mate_code], axis=0))

    operators = jnp.transpose(translate, (1, 0, 2))
    if halves:
        windows = half_windows(rows, depth, 2)
        equivalent = joined_product(up_inverse, up_check, other_check)
        other = across_sub(equivalent)
    else:
        windows = [(0, depth, 0)]
        equivalent = lax.all_gather(
            jnp.dot(
                up_inverse, lax.all_gather(up_check, "sub", axis=0, tiled=True),
                preferred_element_type=jnp.float32,
            ).astype(jnp.bfloat16),
            "sub", axis=0, tiled=True,
        )
        other = equivalent

    parts = chunks(rows, CHUNK)
    half = pl.cdiv(len(parts), 2)
    low = prepare(operators, equivalent, windows, parts[:half])
    near_codes, low = lax.optimization_barrier((near_codes, low))
    mate_near_code = to_mate(near_codes[:entries])
    high = prepare(operators, equivalent, windows, parts[half:])
    mate_near_code, high = lax.optimization_barrier((mate_near_code, high))
    mate_select, near_select, far_select, mate_near = selections(
        mate_code, near_codes, mate_near_code, classes
    )
    terms, mate_sum, far_sum = push_away(
        operators, low, high, other, mate_select, far_select, mate_near,
        windows if halves else [],
    )
    mate_came = to_mate(mate_sum)
    far_came = to_far(far_sum)
    own_sum, near_sum = push_home(terms, home, near_select, mate_came)
    near_came = to_near(near_sum)
    if halves:
        near_crossed = to_near_crosswise(near_sum)
        far_came, _ = lax.optimization_barrier((far_came, near_sum))
    base = own_sum + far_came.astype(jnp.float32)
    if halves:
        half_base = base.astype(jnp.bfloat16)
        near_came, _ = lax.optimization_barrier((near_came, half_base))
        other_base = across_sub(half_base)
    down_check = (base + near_came.astype(jnp.float32)).astype(jnp.bfloat16)
    if halves:
        other_down = (
            other_base.astype(jnp.float32) + near_crossed.astype(jnp.float32)
        ).astype(jnp.bfloat16)
        return rest(down_inverse, first(down_inverse, down_check, windows), other_down, windows)
    return jnp.dot(
        down_inverse, lax.all_gather(down_check, "sub", axis=0, tiled=True),
        preferred_element_type=jnp.float32,
    ).astype(jnp.bfloat16)


def solution(mesh):
    in_specs = (
        P("sub", "tile"),
        P("sub", None),
        P(None, "sub", None),
        P("sub", None),
        P("tile", None),
        P("tile", None),
        P("tile"),
    )
    out_specs = P("sub", "tile")
    return jax.shard_map(shards, mesh=mesh, in_specs=in_specs, out_specs=out_specs, check_vma=False)
```
